128 devices in a mesh: dp: 32 (over z, y, x_lo), tensor: 4 (over x_hi, core).
Axes of the slice: x: 4 (x_hi: 2, x_lo: 2; x = x_hi * 2 + x_lo), y: 4, z: 4, core: 2. Of those that a mesh axis runs over, the one named last changes fastest.
Arguments:
- tokens: bfloat16 [32, 768, 2048], P('dp', 'tensor'), may hold values from -6 to 6
- cotangent: bfloat16 [32, 768, 2048], P('dp', 'tensor'), may hold values from -6 to 6
- adapter_ids: int32 [32], P('dp'), may hold values from 0 to 7
- norm_gains: bfloat16 [2, 2048], replicated, may hold values from 0.4 to 2.8
- lambda_vectors: float32 [4, 8, 128], P(None, 'tensor'), may hold values from -1.2 to 1.2
- weight_inputs: bfloat16 [3, 2048, 2048], P(None, 'dp', 'tensor'), may hold values from -0.125 to 0.125
- weight_output: bfloat16 [2048, 2048], P('tensor', 'dp'), may hold values from -0.125 to 0.125
- hidden_weight_matrix: bfloat16 [2, 2048, 5632], P(None, 'dp', 'tensor'), may hold values from -0.125 to 0.125
- weight_down: bfloat16 [5632, 2048], P('tensor', 'dp'), may hold values from -0.15625 to 0.15625
- adapter_wide: float32 [7, 128, 2048], P(None, None, ('dp', 'tensor')), may hold values from -0.3125 to 0.3125
- adapter_attention: float32 [4, 128, 2048], P(None, 'dp', 'tensor'), may hold values from -0.3125 to 0.3125
- adapter_feedforward: float32 [3, 128, 5632], P(None, 'dp', 'tensor'), may hold values from -0.3125 to 0.3125
- moment_wide: float32 [7, 128, 2048], P(None, None, ('dp', 'tensor')), may hold values from -0.00030517578 to 0.00030517578
- variance_wide: float32 [7, 128, 2048], P(None, None, ('dp', 'tensor')), may hold values from 1.981661e-10 to 7.926644e-10
- moment_attention: float32 [4, 128, 2048], P(None, 'dp', 'tensor'), may hold values from -0.00030517578 to 0.00030517578
- variance_attention: float32 [4, 128, 2048], P(None, 'dp', 'tensor'), may hold values from 1.981661e-10 to 7.926644e-10
- moment_feedforward: float32 [3, 128, 5632], P(None, 'dp', 'tensor'), may hold values from -0.00030517578 to 0.00030517578
- variance_feedforward: float32 [3, 128, 5632], P(None, 'dp', 'tensor'), may hold values from 1.981661e-10 to 7.926644e-10
Outputs:
- out_tokens: bfloat16 [32, 768, 2048], P('dp', 'tensor')
- tokens_grad: bfloat16 [32, 768, 2048], P('dp', 'tensor')
- grad_norm: float32 [], replicated
- grad_wide: float32 [7, 128, 2048], P(None, None, ('dp', 'tensor'))
- grad_attention: float32 [4, 128, 2048], P(None, 'dp', 'tensor')
- grad_feedforward: float32 [3, 128, 5632], P(None, 'dp', 'tensor')
- next_wide: float32 [7, 128, 2048], P(None, None, ('dp', 'tensor'))
- next_attention: float32 [4, 128, 2048], P(None, 'dp', 'tensor')
- next_feedforward: float32 [3, 128, 5632], P(None, 'dp', 'tensor')
- next_moment_wide: float32 [7, 128, 2048], P(None, None, ('dp', 'tensor'))
- next_moment_attention: float32 [4, 128, 2048], P(None, 'dp', 'tensor')
- next_moment_feedforward: float32 [3, 128, 5632], P(None, 'dp', 'tensor')
- next_variance_wide: float32 [7, 128, 2048], P(None, None, ('dp', 'tensor'))
- next_variance_attention: float32 [4, 128, 2048], P(None, 'dp', 'tensor')
- next_variance_feedforward: float32 [3, 128, 5632], P(None, 'dp', 'tensor')
The draws below stay inside these ranges and needn't reach their ends.
All inputs are finite; a program needn't handle non-finite values.
Results may differ from the reference program's by a relative error of at most 0.025.
Values may be sent and summed in bfloat16 or wider, within the bound.
No kernel may reach another device: no remote copies, remote signals or barrier semaphores. Data moves between devices by JAX's collectives and lax.ppermute only.
A program may use at most 192 MiB of HBM per device.

```python
import math
import jax
import jax.numpy as jnp
from jax import lax

D = 2048
HEADS = 8
HEAD_DIM = 128
FF = 5632
ADAPTERS = 8
RANK = 16
BLOCK = 256
STEP = 10
PROJ = 2048
SEQ_LEN = 768
SEQS = 32
ADAPT_ROWS = 128
ADAPT_PARAMS = 5046272


def draw_norm_gains(key, part):
    key = jax.random.fold_in(key, 11)
    ramp = jnp.arange(D, dtype=jnp.float32) / (D - 1)
    rough = jax.random.uniform(key, (2, D), jnp.float32, 0.85, 1.15)
    values = 0.6 * jnp.exp(ramp * math.log(3.0)) * rough
    return values.astype(jnp.bfloat16)


def plant(entries, own_key, least, high):
    spot = [jax.random.randint(jax.random.fold_in(own_key, axis), (), 0, length) for axis, length in enumerate(entries.shape)]
    longest = entries.shape.index(max(entries.shape))
    neighbour = spot[:longest] + [(spot[longest] + 1) % entries.shape[longest]] + spot[longest + 1:]
    return entries.at[tuple(spot)].set(least).at[tuple(neighbour)].set(high)


def levels(own_key, dims, cuts, low, largest):
    level = 1.0
    for dim, shards_of in cuts:
        heights = jax.random.uniform(jax.random.fold_in(jax.random.fold_in(own_key, 6), dim), (shards_of,), jnp.float32, low / len(cuts), largest / len(cuts))
        level = level * jnp.repeat(jnp.exp(heights), dims[dim] // shards_of).reshape((-1,) + (1,) * (len(dims) - 1 - dim))
    return level


def scatter_about(stream_key, dims, scale, reach, split=(), kind=jnp.bfloat16):
    entries = scale * jax.random.normal(stream_key, dims, jnp.float32)
    if split:
        entries = entries * levels(stream_key, dims, split, -0.22, 0.18)
    return jnp.clip(entries, -reach, reach).astype(kind)


def setup_inputs(seed: int = 0) -> dict:
    key_of = jax.random.split(jax.random.key(seed), 19)
    tokens = scatter_about(key_of[0], (SEQS, SEQ_LEN, D), 1.0, 6.0, ((0, 32), (1, 4)))
    cotangent = scatter_about(key_of[1], (SEQS, SEQ_LEN, D), 1.0, 6.0, ((0, 32), (1, 4)))
    adapter_ids = plant(jax.random.randint(key_of[2], (SEQS,), 0, ADAPTERS), jax.random.fold_in(key_of[2], 1), 0, ADAPTERS - 1).astype(jnp.int32)
    norm_gains = draw_norm_gains(jax.random.fold_in(key_of[18], 71), 0)
    lambda_vectors = scatter_about(key_of[4], (4, HEADS, HEAD_DIM), 0.2, 1.2, ((1, 4),), jnp.float32)
    weight_inputs = scatter_about(key_of[5], (3, D, PROJ), D ** -0.5, 0.125, ((1, 32), (2, 4)))
    weight_output = scatter_about(key_of[6], (PROJ, D), PROJ ** -0.5, 0.125, ((0, 4), (1, 32)))
    hidden_weight_matrix = scatter_about(key_of[7], (2, D, FF), D ** -0.5, 0.125, ((1, 32), (2, 4)))
    weight_down = scatter_about(key_of[8], (FF, D), (FF // 4) ** -0.5, 0.15625, ((0, 4), (1, 32)))
    adapter_wide = scatter_about(key_of[9], (7, ADAPT_ROWS, D), (25 * RANK) ** -0.5, 0.3125, ((2, 128),), jnp.float32)
    adapter_attention = scatter_about(key_of[10], (4, ADAPT_ROWS, PROJ), (25 * RANK) ** -0.5, 0.3125, ((1, 32), (2, 4)), jnp.float32)
    adapter_feedforward = scatter_about(key_of[11], (3, ADAPT_ROWS, FF), (25 * RANK) ** -0.5, 0.3125, ((1, 32), (2, 4)), jnp.float32)
    moment_wide = scatter_about(key_of[12], (7, ADAPT_ROWS, D), (0.111 / ADAPT_PARAMS ** 0.5), 0.00030517578, ((2, 128),), jnp.float32)
    variance_wide = jnp.clip(jnp.exp(math.log(7.926643785793885e-10) - 1.3862944 * jax.random.uniform(key_of[13], (7, ADAPT_ROWS, D), jnp.float32) ** levels(key_of[13], (7, ADAPT_ROWS, D), ((2, 128),), -0.2, 0.2)), 1.9816609464484713e-10, 7.926643785793885e-10)
    moment_attention = scatter_about(key_of[14], (4, ADAPT_ROWS, PROJ), (0.111 / ADAPT_PARAMS ** 0.5), 0.00030517578, ((1, 32), (2, 4)), jnp.float32)
    variance_attention = jnp.clip(jnp.exp(math.log(7.926643785793885e-10) - 1.3862944 * jax.random.uniform(key_of[15], (4, ADAPT_ROWS, PROJ), jnp.float32) ** levels(key_of[15], (4, ADAPT_ROWS, PROJ), ((1, 32), (2, 4)), -0.2, 0.2)), 1.9816609464484713e-10, 7.926643785793885e-10)
    moment_feedforward = scatter_about(key_of[16], (3, ADAPT_ROWS, FF), (0.111 / ADAPT_PARAMS ** 0.5), 0.00030517578, ((1, 32), (2, 4)), jnp.float32)
    variance_feedforward = jnp.clip(jnp.exp(math.log(7.926643785793885e-10) - 1.3862944 * jax.random.uniform(key_of[17], (3, ADAPT_ROWS, FF), jnp.float32) ** levels(key_of[17], (3, ADAPT_ROWS, FF), ((1, 32), (2, 4)), -0.2, 0.2)), 1.9816609464484713e-10, 7.926643785793885e-10)
    return dict(tokens=tokens, cotangent=cotangent, adapter_ids=adapter_ids, norm_gains=norm_gains, lambda_vectors=lambda_vectors, weight_inputs=weight_inputs, weight_output=weight_output, hidden_weight_matrix=hidden_weight_matrix, weight_down=weight_down, adapter_wide=adapter_wide, adapter_attention=adapter_attention, adapter_feedforward=adapter_feedforward, moment_wide=moment_wide, variance_wide=variance_wide, moment_attention=moment_attention, variance_attention=variance_attention, moment_feedforward=moment_feedforward, variance_feedforward=variance_feedforward)


@jax.custom_vjp
def low(v):
    return lax.optimization_barrier(v.astype(jnp.bfloat16)).astype(jnp.float32)

@jax.custom_vjp
def low_back(v):
    return v

def low_keep(v):
    return (low(v), None)

def low_pass(kept, grad):
    return (grad,)

def back_keep(v):
    return (v, None)

def back_low(kept, grad):
    return (low(grad),)
low.defvjp(low_keep, low_pass)
low_back.defvjp(back_keep, back_low)
NORM_EPS = 1e-05
ADAPTER_SCALING = 0.5
LAMBDA_INIT = 0.2
OUT_GAIN = 0.8
CLIP_NORM = 1.0
LEARN_RATE = 0.05
BETA_FIRST = 0.9
BETA_SECOND = 0.999
ADAM_EPS = 1e-08
WEIGHT_DECAY = 0.01
NEG_LARGE = -1e+30
PRECISE = lax.Precision.HIGHEST

def product(left, right):
    return jnp.dot(left, right, precision=PRECISE, preferred_element_type=jnp.float32)

def contract_matrices(form, left, right):
    return jnp.einsum(form, left, right, precision=PRECISE, preferred_element_type=jnp.float32)

def rms_scale(values, gain_value):
    return values * lax.rsqrt(lax.optimization_barrier(jnp.mean(values * values, axis=-1, keepdims=True)) + NORM_EPS) * gain_value

def select_rows(stacked, onehot):
    shaped = stacked.reshape(stacked.shape[0], ADAPTERS, RANK, stacked.shape[2])
    return contract_matrices('e,xerc->xrc', onehot, shaped)

def attention(projected, lambda_head):
    queries = projected[0].reshape(SEQ_LEN, HEADS, 2, HEAD_DIM).transpose(1, 2, 0, 3)
    keys_all = projected[1].reshape(SEQ_LEN, HEADS, 2, HEAD_DIM).transpose(1, 2, 0, 3)
    values = projected[2].reshape(SEQ_LEN, HEADS, 2 * HEAD_DIM).transpose(1, 0, 2)
    position = jnp.arange(SEQ_LEN, dtype=jnp.int32) // BLOCK
    mask_bias = jnp.where(position[None, :] <= position[:, None], 0.0, NEG_LARGE).astype(jnp.float32)

    def one_head(head_items):
        query_pair, key_pair, value_head, lambda_one = head_items
        raw_scores = contract_matrices('cld,cmd->clm', query_pair, key_pair)
        scores = low_back(raw_scores) * HEAD_DIM ** (-0.5) + mask_bias
        probs = jax.nn.softmax(scores, axis=-1)
        combined = low(probs[0] - lambda_one * probs[1])
        return product(combined, value_head)
    outputs = lax.map(jax.checkpoint(one_head), (queries, keys_all, values, lambda_head))
    return outputs.transpose(1, 0, 2).reshape(SEQ_LEN, PROJ)

def layer(tokens_f, wide, attn_stack, ffn_stack, onehot, frozen):
    weight_inputs, weight_output, hidden_weight_matrix, weight_down, gain_values, lambda_head = frozen
    picked_wide = low(select_rows(wide, onehot))
    picked_attention = low(select_rows(attn_stack, onehot))
    selected_feedforward = low(select_rows(ffn_stack, onehot))
    normed_one = low(rms_scale(tokens_f, gain_values[0]))
    lowrank_inputs = low_back(low(contract_matrices('td,xrd->xtr', normed_one, picked_wide[0:3])))
    projected = contract_matrices('td,xdc->xtc', normed_one, weight_inputs) + ADAPTER_SCALING * contract_matrices('xtr,xrc->xtc', lowrank_inputs, picked_attention[0:3])
    projected = low_back(low(projected))
    raw_out = low_back(attention(projected, lambda_head))
    heads_out = raw_out.reshape(SEQ_LEN, HEADS, 2 * HEAD_DIM)
    attention_in = low(rms_scale(heads_out, OUT_GAIN).reshape(SEQ_LEN, PROJ))
    lowrank_out = low_back(low(contract_matrices('tc,rc->tr', attention_in, picked_attention[3])))
    branch_one = low_back(product(attention_in, weight_output) + ADAPTER_SCALING * product(lowrank_out, picked_wide[5]))
    residual_one = tokens_f + branch_one
    second_normalized = low(rms_scale(residual_one, gain_values[1]))
    low_rank_hidden = low_back(low(contract_matrices('td,xrd->xtr', second_normalized, picked_wide[3:5])))
    gate_up_product = contract_matrices('za,wav->wzv', second_normalized, hidden_weight_matrix) + ADAPTER_SCALING * contract_matrices('bcv,bvw->bcw', low_rank_hidden, selected_feedforward[0:2])
    gate_up_product = low_back(gate_up_product)
    hidden = low(jax.nn.silu(gate_up_product[0]) * gate_up_product[1])
    lowrank_down = low_back(low(contract_matrices('tf,rf->tr', hidden, selected_feedforward[2])))
    branch_two = low_back(product(hidden, weight_down) + ADAPTER_SCALING * product(lowrank_down, picked_wide[6]))
    return residual_one + branch_two

def adam_step(parameter, gradient, moment, variance, factor):
    clipped = gradient * factor
    moment_new = BETA_FIRST * moment + (1.0 - BETA_FIRST) * clipped
    variance_new = BETA_SECOND * variance + (1.0 - BETA_SECOND) * clipped * clipped
    moment_hat = moment_new / (1.0 - BETA_FIRST ** STEP)
    variance_hat = variance_new / (1.0 - BETA_SECOND ** STEP)
    updated = parameter - LEARN_RATE * (moment_hat / (jnp.sqrt(variance_hat) + ADAM_EPS) + WEIGHT_DECAY * parameter)
    return (clipped, updated, moment_new, variance_new)

def reference(tokens, cotangent, adapter_ids, norm_gains, lambda_vectors, weight_inputs, weight_output, hidden_weight_matrix, weight_down, adapter_wide, adapter_attention, adapter_feedforward, moment_wide, variance_wide, moment_attention, variance_attention, moment_feedforward, variance_feedforward):
    lambda_head = jnp.exp(lax.optimization_barrier(jnp.sum(lambda_vectors[0] * lambda_vectors[1], axis=-1))) - jnp.exp(lax.optimization_barrier(jnp.sum(lambda_vectors[2] * lambda_vectors[3], axis=-1))) + LAMBDA_INIT
    frozen = (weight_inputs.astype(jnp.float32), weight_output.astype(jnp.float32), hidden_weight_matrix.astype(jnp.float32), weight_down.astype(jnp.float32), norm_gains.astype(jnp.float32), lambda_head)

    def one_sequence(carry, seq_items):
        seq_tokens, seq_cotangent, identity = seq_items
        onehot = (jnp.arange(ADAPTERS, dtype=jnp.int32) == identity).astype(jnp.float32)

        def forward(tokens_f, wide, attn_stack, ffn_stack):
            return layer(tokens_f, wide, attn_stack, ffn_stack, onehot, frozen)
        result, pullback = jax.vjp(forward, seq_tokens.astype(jnp.float32), adapter_wide, adapter_attention, adapter_feedforward)
        grad_tokens, grad_one, grad_two, grad_three = pullback(seq_cotangent.astype(jnp.float32))
        summed = (carry[0] + grad_one, carry[1] + grad_two, carry[2] + grad_three)
        return (summed, (result.astype(jnp.bfloat16), grad_tokens.astype(jnp.bfloat16)))
    start = (jnp.zeros_like(adapter_wide), jnp.zeros_like(adapter_attention), jnp.zeros_like(adapter_feedforward))
    raw_grads, outputs = lax.scan(one_sequence, start, (tokens, cotangent, adapter_ids))
    out_tokens, tokens_grad = outputs
    total_squares = jnp.sum(raw_grads[0] * raw_grads[0]) + jnp.sum(raw_grads[1] * raw_grads[1]) + jnp.sum(raw_grads[2] * raw_grads[2])
    grad_norm = jnp.sqrt(total_squares)
    factor = CLIP_NORM / (grad_norm + 1e-06)
    wide_new = adam_step(adapter_wide, raw_grads[0], moment_wide, variance_wide, factor)
    attention_new = adam_step(adapter_attention, raw_grads[1], moment_attention, variance_attention, factor)
    feedforward_new = adam_step(adapter_feedforward, raw_grads[2], moment_feedforward, variance_feedforward, factor)
    return (out_tokens, tokens_grad, grad_norm, wide_new[0], attention_new[0], feedforward_new[0], wide_new[1], attention_new[1], feedforward_new[1], wide_new[2], attention_new[2], feedforward_new[2], wide_new[3], attention_new[3], feedforward_new[3])
```

```python
import jax
import jax.numpy as jnp
from jax import lax
from jax.sharding import PartitionSpec as P

HEAD_DIM = 128
ADAPTERS = 8
RANK = 16
BLOCK = 256
STEP = 10


NORM_EPS = 1e-05
ADAPTER_SCALING = 0.5
LAMBDA_INIT = 0.2
OUT_GAIN = 0.8
CLIP_NORM = 1.0
LEARN_RATE = 0.05
BETA_FIRST = 0.9
BETA_SECOND = 0.999
ADAM_EPS = 1e-08
WEIGHT_DECAY = 0.01
NEG_LARGE = -1e30
AXES = ("dp", "tensor")
B16 = jnp.bfloat16
F32 = jnp.float32


def product(left, right):
    return jnp.dot(left, right, preferred_element_type=F32)


def contract(form, left, right):
    return jnp.einsum(form, left, right, preferred_element_type=F32)


def index_of(z, y, x, core):
    x, y, z, core = x % 4, y % 4, z % 4, core % 2
    return ((z * 4 + y) * 2 + x % 2) * 4 + (x // 2) * 2 + core


def routes(move):
    pairs = []
    for z in range(4):
        for y in range(4):
            for x in range(4):
                for core in range(2):
                    pairs.append((index_of(z, y, x, core), index_of(*move(z, y, x, core))))
    return pairs


UP_Z = routes(lambda z, y, x, c: (z + 1, y, x, c))
DOWN_Z = routes(lambda z, y, x, c: (z - 1, y, x, c))
FAR_Z = routes(lambda z, y, x, c: (z + 2, y, x, c))
UP_Y = routes(lambda z, y, x, c: (z, y + 1, x, c))
DOWN_Y = routes(lambda z, y, x, c: (z, y - 1, x, c))
FAR_Y = routes(lambda z, y, x, c: (z, y + 2, x, c))
PAIR_X = routes(lambda z, y, x, c: (z, y, x ^ 1, c))
FAR_X = routes(lambda z, y, x, c: (z, y, x + 2, c))
CORES = routes(lambda z, y, x, c: (z, y, x, 1 - c))


def send(values, pairs):
    return lax.ppermute(values, AXES, pairs)


def put(buffer, values, *starts):
    return lax.dynamic_update_slice(buffer, values, starts)


class Place:
    def __init__(self):
        dp, tensor = lax.axis_index("dp"), lax.axis_index("tensor")
        self.z, self.y, self.x = dp // 8, (dp // 2) % 4, dp % 2
        self.far, self.core = tensor // 2, tensor % 2
        self.dp, self.tensor = dp, tensor


def gather_rows(shard, place, widths):
    z, y, x = place.z, place.y, place.x
    other = send(shard, PAIR_X)
    pair = jnp.where(x == 0, jnp.stack([shard, other]), jnp.stack([other, shard]))
    half = shard.shape[0] // 2
    full = shard.shape[1]

    def ring(block, step_up, step_down, step_far, here):
        wide = jnp.zeros((4,) + block.shape, block.dtype)
        wide = put(wide, block[None], here, 0, 0, 0)
        wide = put(wide, send(block, step_up)[None], (here + 3) % 4, 0, 0, 0)
        wide = put(wide, send(block, step_down)[None], (here + 1) % 4, 0, 0, 0)
        return put(wide, send(block, step_far)[None], (here + 2) % 4, 0, 0, 0)

    def ring_relay(plane, step_up, step_down):
        below = send(plane, step_up)
        above = send(plane, step_down)
        return (plane, below, above, send(below[:2], step_up), send(above[2:], step_down))

    part_a, part_b = pair[:, :half], pair[:, half:]
    pieces_a = ring_relay(ring(part_a, UP_Y, DOWN_Y, FAR_Y, y), UP_Z, DOWN_Z)
    pieces_b = ring_relay(ring(part_b, UP_Z, DOWN_Z, FAR_Z, z), UP_Y, DOWN_Y)
    out, start = [], 0
    for width in widths:
        whole = jnp.zeros((4, 4, 2, 2, half, width), shard.dtype)
        cut = lambda v: v[..., start : start + width]
        here, below, above, far_a, far_b = [cut(v) for v in pieces_a]
        for piece, at_z, at_y in (
            (here, z, 0),
            (below, (z + 3) % 4, 0),
            (above, (z + 1) % 4, 0),
            (far_a, (z + 2) % 4, 0),
            (far_b, (z + 2) % 4, 2),
        ):
            whole = put(whole, piece[None, :, :, None], at_z, at_y, 0, 0, 0, 0)
        here, below, above, far_a, far_b = [cut(v) for v in pieces_b]
        for piece, at_y, at_z in (
            (here, y, 0),
            (below, (y + 3) % 4, 0),
            (above, (y + 1) % 4, 0),
            (far_a, (y + 2) % 4, 0),
            (far_b, (y + 2) % 4, 2),
        ):
            whole = put(whole, piece[:, None, :, None], at_z, at_y, 0, 1, 0, 0)
        out.append(whole.reshape(64 * half, width))
        start += width
    return out


def gather_tokens(shard, place):
    core = send(shard, CORES)
    far = send(shard, FAR_X)
    far_core = send(far, CORES)
    t = place.tensor
    whole = jnp.zeros((4,) + shard.shape, shard.dtype)
    zeros = (0,) * shard.ndim
    whole = put(whole, shard[None], t, *zeros)
    whole = put(whole, core[None], t ^ 1, *zeros)
    whole = put(whole, far[None], t ^ 2, *zeros)
    whole = put(whole, far_core[None], t ^ 3, *zeros)
    return whole.reshape((4 * shard.shape[0],) + shard.shape[1:])


def scatter_tokens(partial, place):
    rows = partial.shape[0] // 4
    blocks = partial.reshape(2, 2, rows, partial.shape[1])
    away = lax.dynamic_index_in_dim(blocks, 1 - place.core, 1, keepdims=False)
    near = lax.dynamic_index_in_dim(blocks, place.core, 1, keepdims=False)
    summed = near.astype(F32) + send(away.astype(B16), CORES).astype(F32)
    leaving = lax.dynamic_index_in_dim(summed, 1 - place.far, 0, keepdims=False)
    staying = lax.dynamic_index_in_dim(summed, place.far, 0, keepdims=False)
    return staying + send(leaving.astype(B16), FAR_X).astype(F32)


def norm_forward(values, gain_value):
    factor = lax.rsqrt(jnp.mean(values * values, axis=-1, keepdims=True) + NORM_EPS)
    return (values * factor * gain_value, factor)


def norm_backward(values, factor, gain_value, gradient):
    scaled = gradient * gain_value
    return factor * (
        scaled - values * factor * factor * jnp.mean(scaled * values, axis=-1, keepdims=True)
    )


def head_scores(query_pair, key_pair, mask_bias):
    return contract("cld,cmd->clm", query_pair, key_pair) * HEAD_DIM ** (-0.5) + mask_bias


def head_forward(query_pair, key_pair, values, lambda_one, mask_bias):
    scores = head_scores(query_pair, key_pair, mask_bias)
    row_max = jnp.max(scores, axis=-1, keepdims=True)
    shifted = jnp.exp(scores - row_max)
    row_sum = jnp.sum(shifted, axis=-1, keepdims=True)
    probabilities = shifted / row_sum
    log_total = row_max + jnp.log(row_sum)
    combined = (probabilities[0] - lambda_one * probabilities[1]).astype(B16)
    return (product(combined, values), log_total[..., 0])


def head_backward(query_pair, key_pair, values, lambda_one, log_total, grad_out, mask_bias):
    scores = head_scores(query_pair, key_pair, mask_bias)
    probabilities = jnp.exp(scores - log_total[..., None])
    combined = (probabilities[0] - lambda_one * probabilities[1]).astype(B16)
    grad_values = contract("lm,ld->md", combined, grad_out)
    grad_combined = contract("ld,md->lm", grad_out, values)
    weighting = jnp.stack([jnp.ones_like(lambda_one), -lambda_one])
    grad_probs = weighting[:, None, None] * grad_combined[None]
    row_inner = jnp.sum(grad_probs * probabilities, axis=-1, keepdims=True)
    grad_scores = (probabilities * (grad_probs - row_inner) * HEAD_DIM ** (-0.5)).astype(B16)
    grad_query = contract("clm,cmd->cld", grad_scores, key_pair)
    grad_key = contract("clm,cld->cmd", grad_scores, query_pair)
    return (grad_query, grad_key, grad_values)


def adam_step(parameter, gradient, moment, variance, factor):
    clipped = gradient * factor
    moment_new = BETA_FIRST * moment + (1.0 - BETA_FIRST) * clipped
    variance_new = BETA_SECOND * variance + (1.0 - BETA_SECOND) * clipped * clipped
    moment_hat = moment_new / (1.0 - BETA_FIRST**STEP)
    variance_hat = variance_new / (1.0 - BETA_SECOND**STEP)
    updated = parameter - LEARN_RATE * (
        moment_hat / (jnp.sqrt(variance_hat) + ADAM_EPS) + WEIGHT_DECAY * parameter
    )
    return (clipped, updated, moment_new, variance_new)


def flat_rows(stacked):
    moved = stacked.astype(B16).transpose(1, 0, 2)
    return moved.reshape(stacked.shape[1], -1)


def fold_rows(rows, lanes):
    padded = jnp.pad(rows, ((0, 0), (0, 16 * lanes - rows.shape[1])))
    return padded.reshape(64, lanes)


def pick_rows(gathered, adapter, width):
    lanes = gathered.shape[1]
    mine = lax.dynamic_slice_in_dim(gathered, adapter * 256, 256, 0)
    return mine.reshape(16, 16 * lanes)[:, :width]


def local(
    tokens,
    cotangent,
    adapter_ids,
    norm_gains,
    lambda_vectors,
    weight_inputs,
    weight_output,
    hidden_weight_matrix,
    weight_down,
    adapter_wide,
    adapter_attention,
    adapter_feedforward,
    moment_wide,
    variance_wide,
    moment_attention,
    variance_attention,
    moment_feedforward,
    variance_feedforward,
):
    place = Place()
    adapter = adapter_ids[0]
    local_tokens = tokens[0].astype(F32)
    upstream_b = cotangent[0]
    gain_values = norm_gains.astype(F32)
    lambda_all = (
        jnp.exp(jnp.sum(lambda_vectors[0] * lambda_vectors[1], axis=-1))
        - jnp.exp(jnp.sum(lambda_vectors[2] * lambda_vectors[3], axis=-1))
        + LAMBDA_INIT
    )
    heads_local = lambda_vectors.shape[1]
    proj = weight_inputs.shape[2]
    ff = hidden_weight_matrix.shape[2]
    length = tokens.shape[1] * 4
    position = jnp.arange(length, dtype=jnp.int32) // BLOCK
    mask_bias = jnp.where(position[None, :] <= position[:, None], 0.0, NEG_LARGE).astype(F32)

    wide_flat = jnp.pad(
        adapter_wide.astype(B16).transpose(0, 2, 1).reshape(112, 128), ((0, 16), (0, 0))
    )
    shard_one = jnp.concatenate(
        [
            weight_inputs[0],
            weight_inputs[1],
            weight_inputs[2],
            weight_output.T,
            fold_rows(flat_rows(adapter_attention), 128),
            wide_flat[:64],
            wide_flat[64:],
        ],
        axis=1,
    )
    shard_two = jnp.concatenate(
        [
            hidden_weight_matrix[0],
            hidden_weight_matrix[1],
            fold_rows(flat_rows(adapter_feedforward[0:2]), 256),
        ],
        axis=1,
    )
    shard_three = jnp.concatenate(
        [weight_down.T, fold_rows(flat_rows(adapter_feedforward[2:3]), 128)], axis=1
    )
    w_in, w_out, fold_attention, fold_wide = gather_rows(
        shard_one, place, (3 * proj, proj, 128, 256)
    )
    w_hidden, fold_hidden = gather_rows(shard_two, place, (2 * ff, 256))
    w_down, fold_down = gather_rows(shard_three, place, (ff, 128))
    pick_attention = pick_rows(fold_attention, adapter, 4 * proj)
    pick_hidden = pick_rows(fold_hidden, adapter, 2 * ff)
    pick_down = pick_rows(fold_down, adapter, ff)

    onehot_rows = (
        jnp.arange(128)[None, :, None]
        == (adapter * RANK + jnp.arange(128) - RANK * jnp.arange(8)[:, None])[:, None, :]
    ) & (jnp.arange(128)[None, None, :] // RANK == jnp.arange(8)[:, None, None])
    wide_mine = (
        fold_wide.reshape(32, 4, 16, 2, 128).transpose(0, 2, 3, 1, 4).reshape(512, 1024)
    )
    picked_t = product(wide_mine, onehot_rows.astype(B16).reshape(1024, 128)).astype(B16)
    picked_all = gather_tokens(picked_t, place).reshape(4, 32, 16, 128)
    picked_wide = picked_all.transpose(1, 0, 2, 3).reshape(2048, 128)

    def diagonal(rows, width):
        count = rows.shape[1] // width
        column = jnp.arange(rows.shape[1]) // width
        row = jnp.arange(count * RANK) // RANK
        tiled = jnp.concatenate([rows] * count, axis=0)
        return jnp.where(row[:, None] == column[None, :], tiled, 0).astype(B16)

    half = jnp.asarray(ADAPTER_SCALING, B16)

    normed_one, scale_one = norm_forward(local_tokens, gain_values[0])
    normed_one_b = normed_one.astype(B16)
    seq_normed_one = gather_tokens(normed_one_b, place)
    seq_upstream = gather_tokens(upstream_b, place)
    lowrank_inputs = product(seq_normed_one, picked_wide).astype(B16)[:, 0:48]
    diag_in = diagonal(pick_attention[:, : 3 * proj], proj)
    projected_b = (
        product(seq_normed_one, w_in) + product(lowrank_inputs * half, diag_in)
    ).astype(B16)
    split = lambda v: v.reshape(length, heads_local, 2, HEAD_DIM).transpose(1, 2, 0, 3)
    query_heads = split(projected_b[:, :proj])
    key_heads = split(projected_b[:, proj : 2 * proj])
    value_heads = (
        projected_b[:, 2 * proj :].reshape(length, heads_local, 2 * HEAD_DIM).transpose(1, 0, 2)
    )

    def forward_head(head_items):
        query_pair, key_pair, values, lambda_one = head_items
        return head_forward(query_pair, key_pair, values, lambda_one, mask_bias)

    raw_heads, log_totals = lax.map(forward_head, (query_heads, key_heads, value_heads, lambda_all))
    head_factor = lax.rsqrt(jnp.mean(raw_heads * raw_heads, axis=-1, keepdims=True) + NORM_EPS)
    attention_b = (
        (raw_heads * head_factor * OUT_GAIN).transpose(1, 0, 2).reshape(length, -1).astype(B16)
    )
    pick_out = pick_attention[:, 3 * proj :]
    pad_rank = lambda v: jnp.pad(v, ((0, 0), (0, 128 - v.shape[1])))
    out_sum = scatter_tokens(
        jnp.concatenate(
            [
                contract("lc,dc->ld", attention_b, w_out).astype(B16),
                pad_rank(contract("lc,rc->lr", attention_b, pick_out).astype(B16)),
            ],
            axis=1,
        ),
        place,
    )
    lowrank_out_b = out_sum[:, 2048 : 2048 + RANK].astype(B16)
    residual_one = (
        local_tokens
        + out_sum[:, :2048]
        + contract("tr,dr->td", lowrank_out_b * half, picked_wide[:, 80:96])
    )

    second_normalized, scale_two = norm_forward(residual_one, gain_values[1])
    normed_two_b = second_normalized.astype(B16)
    seq_normed_two = gather_tokens(normed_two_b, place)
    lowrank_hidden = product(seq_normed_two, picked_wide).astype(B16)[:, 48:80]
    diag_hidden = diagonal(pick_hidden, ff)
    gate_up = product(seq_normed_two, w_hidden) + product(lowrank_hidden * half, diag_hidden)
    gate, upper = gate_up[:, :ff], gate_up[:, ff:]
    hidden_b = (jax.nn.silu(gate) * upper).astype(B16)
    down_sum = scatter_tokens(
        jnp.concatenate(
            [
                contract("lf,df->ld", hidden_b, w_down).astype(B16),
                pad_rank(contract("lf,rf->lr", hidden_b, pick_down).astype(B16)),
            ],
            axis=1,
        ),
        place,
    )
    lowrank_down_b = down_sum[:, 2048 : 2048 + RANK].astype(B16)
    result = (
        residual_one
        + down_sum[:, :2048]
        + contract("tr,dr->td", lowrank_down_b * half, picked_wide[:, 96:112])
    )

    grad_right_down = ADAPTER_SCALING * contract("td,tr->dr", upstream_b, lowrank_down_b)
    grad_lowrank_down = (ADAPTER_SCALING * product(seq_upstream, picked_wide)).astype(B16)[:, 96:112]
    grad_hidden = product(seq_upstream, w_down) + product(grad_lowrank_down, pick_down)
    grad_left_down = contract("lr,lf->rf", grad_lowrank_down, hidden_b)
    sigmoid_gate = jax.nn.sigmoid(gate)
    grad_gate = grad_hidden * upper * sigmoid_gate * (1.0 + gate * (1.0 - sigmoid_gate))
    grad_upper = grad_hidden * gate * sigmoid_gate
    grad_gate_up = jnp.concatenate([grad_gate.astype(B16), grad_upper.astype(B16)], axis=1)
    right_hidden = [
        ADAPTER_SCALING
        * contract(
            "lr,lf->rf",
            lowrank_hidden[:, RANK * i : RANK * (i + 1)],
            grad_gate_up[:, ff * i : ff * (i + 1)],
        )
        for i in range(2)
    ]
    hidden_sum = scatter_tokens(
        jnp.concatenate(
            [
                contract("lf,df->ld", grad_gate_up, w_hidden).astype(B16),
                pad_rank(
                    (ADAPTER_SCALING * contract("lf,rf->lr", grad_gate_up, diag_hidden)).astype(B16)
                ),
            ],
            axis=1,
        ),
        place,
    )
    grad_lowrank_hidden = hidden_sum[:, 2048 : 2048 + 2 * RANK].astype(B16)
    grad_left_hidden = contract("td,tr->dr", normed_two_b, grad_lowrank_hidden)
    grad_normed_two = hidden_sum[:, :2048] + contract(
        "tr,dr->td", grad_lowrank_hidden, picked_wide[:, 48:80]
    )
    grad_residual = upstream_b.astype(F32) + norm_backward(
        residual_one, scale_two, gain_values[1], grad_normed_two
    )

    grad_branch_b = grad_residual.astype(B16)
    grad_right_out = ADAPTER_SCALING * contract("td,tr->dr", grad_branch_b, lowrank_out_b)
    seq_grad_branch = gather_tokens(grad_branch_b, place)
    grad_lowrank_out = (ADAPTER_SCALING * product(seq_grad_branch, picked_wide)).astype(B16)[
        :, 80:96
    ]
    grad_attention_in = product(seq_grad_branch, w_out) + product(grad_lowrank_out, pick_out)
    grad_left_out = contract("lr,lc->rc", grad_lowrank_out, attention_b)
    grad_heads = grad_attention_in.reshape(length, heads_local, 2 * HEAD_DIM).transpose(1, 0, 2)
    grad_raw_b = norm_backward(raw_heads, head_factor, OUT_GAIN, grad_heads).astype(B16)

    def backward_head(head_items):
        query_pair, key_pair, values, lambda_one, log_total, grad_out = head_items
        return head_backward(
            query_pair, key_pair, values, lambda_one, log_total, grad_out, mask_bias
        )

    grad_query, grad_key, grad_value = lax.map(
        backward_head, (query_heads, key_heads, value_heads, lambda_all, log_totals, grad_raw_b)
    )
    grad_projected_b = jnp.concatenate(
        [
            grad_query.transpose(2, 0, 1, 3).reshape(length, -1),
            grad_key.transpose(2, 0, 1, 3).reshape(length, -1),
            grad_value.transpose(1, 0, 2).reshape(length, -1),
        ],
        axis=1,
    ).astype(B16)
    right_inputs = [
        ADAPTER_SCALING
        * contract(
            "lr,lc->rc",
            lowrank_inputs[:, RANK * i : RANK * (i + 1)],
            grad_projected_b[:, proj * i : proj * (i + 1)],
        )
        for i in range(3)
    ]
    input_sum = scatter_tokens(
        jnp.concatenate(
            [
                contract("lc,dc->ld", grad_projected_b, w_in).astype(B16),
                pad_rank(
                    (ADAPTER_SCALING * contract("lc,rc->lr", grad_projected_b, diag_in)).astype(B16)
                ),
            ],
            axis=1,
        ),
        place,
    )
    grad_lowrank_inputs = input_sum[:, 2048 : 2048 + 3 * RANK].astype(B16)
    grad_left_inputs = contract("td,tr->dr", normed_one_b, grad_lowrank_inputs)
    grad_normed_one = input_sum[:, :2048] + contract(
        "tr,dr->td", grad_lowrank_inputs, picked_wide[:, 0:48]
    )
    grad_input = grad_residual + norm_backward(
        local_tokens, scale_one, gain_values[0], grad_normed_one
    )

    wide_grads = jnp.concatenate(
        [
            grad_left_inputs,
            grad_left_hidden,
            grad_right_out,
            grad_right_down,
            jnp.zeros((2048, RANK), F32),
        ],
        axis=1,
    ).astype(B16)
    split_grads = jnp.concatenate(
        right_inputs + [grad_left_out] + right_hidden + [grad_left_down], axis=1
    ).astype(B16)
    columns = split_grads.shape[1]
    piece = -(-columns // 1024) * 128
    split_blocks = (
        jnp.pad(split_grads, ((0, 0), (0, 8 * piece - columns)))
        .reshape(4, 4, 2, 4, piece)
        .transpose(1, 2, 0, 3, 4)
        .reshape(128, piece // 128, 128)
    )
    blocks = jnp.concatenate(
        [
            wide_grads.reshape(128, 16, 128),
            split_blocks,
            jnp.broadcast_to(adapter.astype(B16), (128, 8 - piece // 128, 128)),
        ],
        axis=1,
    )
    arrived = lax.all_to_all(blocks, AXES, split_axis=0, concat_axis=0, tiled=True)
    ids_all = arrived.reshape(32, 4, 24, 128)[:, 0, 23, 0].astype(jnp.int32)
    member = ids_all[None, :] == jnp.arange(ADAPTERS)[:, None]
    onehot = member.astype(B16)
    wide_sum = contract(
        "es,sn->en",
        onehot,
        arrived[:, :16].reshape(32, 4 * 16 * 128),
    ).reshape(8, 4, 16, 128).sum(1)
    split_sum = contract(
        "es,sn->en", onehot, arrived[:, 16:].reshape(32, 4 * 8 * 128)
    ).reshape(8, 4, 8, 128)[:, :, : piece // 128]
    squares = jnp.sum(wide_sum * wide_sum) + jnp.sum(split_sum * split_sum)
    grads_wide = (
        wide_sum[:, :, :112].reshape(8, 16, 7, 16).transpose(2, 0, 3, 1).reshape(7, 128, 16)
    )
    mine = place.dp % 4
    split_out = jnp.concatenate(
        [split_sum.reshape(32, 7, 128), jnp.zeros((32, 1, 128), F32)], axis=1
    ).reshape(8, 1, 4, 8, 128)
    quarter = jnp.arange(4)[None, :, None, None, None]
    spread = jnp.where(quarter == mine, split_out, 0.0).reshape(128, 8, 128)
    spread = jnp.where(jnp.arange(8)[None, :, None] == 7, squares, spread)
    placed = lax.all_to_all(spread, AXES, split_axis=0, concat_axis=0, tiled=True)
    total_squares = jnp.sum(placed[:, 7, 0])
    from_mine = lax.dynamic_index_in_dim(
        placed.reshape(8, 4, 4, 8, 128), mine, 1, keepdims=False
    )
    split_rows = from_mine[:, :, :7].reshape(4, 8 * piece)[:, :columns]
    grads_attention = split_rows[:, : 4 * proj].reshape(4, 4, proj).transpose(1, 0, 2)
    grads_feedforward = split_rows[:, 4 * proj :].reshape(4, 3, ff).transpose(1, 0, 2)

    grad_norm = jnp.sqrt(total_squares)
    factor = CLIP_NORM / (grad_norm + 1e-06)
    wide_new = adam_step(adapter_wide, grads_wide, moment_wide, variance_wide, factor)
    attention_new = adam_step(
        adapter_attention, grads_attention, moment_attention, variance_attention, factor
    )
    feedforward_new = adam_step(
        adapter_feedforward, grads_feedforward, moment_feedforward, variance_feedforward, factor
    )
    return (
        result.astype(B16)[None],
        grad_input.astype(B16)[None],
        grad_norm,
        wide_new[0],
        attention_new[0],
        feedforward_new[0],
        wide_new[1],
        attention_new[1],
        feedforward_new[1],
        wide_new[2],
        attention_new[2],
        feedforward_new[2],
        wide_new[3],
        attention_new[3],
        feedforward_new[3],
    )


def solution(mesh):
    return jax.shard_map(
        local,
        mesh=mesh,
        in_specs=(
            P("dp", "tensor", None),
            P("dp", "tensor", None),
            P("dp"),
            P(),
            P(None, "tensor", None),
            P(None, "dp", "tensor"),
            P("tensor", "dp"),
            P(None, "dp", "tensor"),
            P("tensor", "dp"),
            P(None, None, ("dp", "tensor")),
            P(None, "dp", "tensor"),
            P(None, "dp", "tensor"),
            P(None, None, ("dp", "tensor")),
            P(None, None, ("dp", "tensor")),
            P(None, "dp", "tensor"),
            P(None, "dp", "tensor"),
            P(None, "dp", "tensor"),
            P(None, "dp", "tensor"),
        ),
        out_specs=(
            P("dp", "tensor", None),
            P("dp", "tensor", None),
            P(),
            P(None, None, ("dp", "tensor")),
            P(None, "dp", "tensor"),
            P(None, "dp", "tensor"),
            P(None, None, ("dp", "tensor")),
            P(None, "dp", "tensor"),
            P(None, "dp", "tensor"),
            P(None, None, ("dp", "tensor")),
            P(None, "dp", "tensor"),
            P(None, "dp", "tensor"),
            P(None, None, ("dp", "tensor")),
            P(None, "dp", "tensor"),
            P(None, "dp", "tensor"),
        ),
        check_vma=False,
    )
```

```python
import jax
import jax.numpy as jnp
from jax import lax
from jax.experimental import pallas as pl
from jax.experimental.pallas import tpu as pltpu
from jax.sharding import PartitionSpec as P

HEAD_DIM = 128
ADAPTERS = 8
RANK = 16
BLOCK = 256
STEP = 10


NORM_EPS = 1e-05
ADAPTER_SCALING = 0.5
LAMBDA_INIT = 0.2
OUT_GAIN = 0.8
CLIP_NORM = 1.0
LEARN_RATE = 0.05
BETA_FIRST = 0.9
BETA_SECOND = 0.999
ADAM_EPS = 1e-08
WEIGHT_DECAY = 0.01
NEG_LARGE = -1e30
AXES = ("dp", "tensor")
B16 = jnp.bfloat16
F32 = jnp.float32


def product(left, right):
    return jnp.dot(left, right, preferred_element_type=F32)


def contract(form, left, right):
    return jnp.einsum(form, left, right, preferred_element_type=F32)


def index_of(z, y, x, core):
    x, y, z, core = x % 4, y % 4, z % 4, core % 2
    return ((z * 4 + y) * 2 + x % 2) * 4 + (x // 2) * 2 + core


def routes(move):
    pairs = []
    for z in range(4):
        for y in range(4):
            for x in range(4):
                for core in range(2):
                    pairs.append((index_of(z, y, x, core), index_of(*move(z, y, x, core))))
    return pairs


UP_Z = routes(lambda z, y, x, c: (z + 1, y, x, c))
DOWN_Z = routes(lambda z, y, x, c: (z - 1, y, x, c))
FAR_Z = routes(lambda z, y, x, c: (z + 2, y, x, c))
UP_Y = routes(lambda z, y, x, c: (z, y + 1, x, c))
DOWN_Y = routes(lambda z, y, x, c: (z, y - 1, x, c))
FAR_Y = routes(lambda z, y, x, c: (z, y + 2, x, c))
PAIR_X = routes(lambda z, y, x, c: (z, y, x ^ 1, c))
FAR_X = routes(lambda z, y, x, c: (z, y, x + 2, c))
CORES = routes(lambda z, y, x, c: (z, y, x, 1 - c))


def send(values, pairs):
    return lax.ppermute(values, AXES, pairs)


class Place:
    def __init__(self):
        tensor = lax.axis_index("tensor")
        self.far, self.core, self.tensor = tensor // 2, tensor % 2, tensor
        self.dp = lax.axis_index("dp")


def together(*values):
    return lax.optimization_barrier(values)


OFFSETS = (0, 3, 1, 2)


def assemble(pieces_a, pieces_b, widths):
    half = pieces_a[0].shape[1]
    rows = 64 * half

    def kernel(*refs):
        sources, outs, sem = (refs[:5], refs[5:10]), refs[10:-1], refs[-1]
        dp = lax.axis_index("dp")
        at = (dp // 8, (dp // 2) & 3)
        x = dp & 1
        copies = []
        for order in range(2):
            for outer in range(4):
                for block in range(8):
                    places = [0, 0]
                    places[order] = (at[order] + OFFSETS[outer]) & 3
                    places[1 - order] = (at[1 - order] + OFFSETS[block // 2]) & 3
                    index = (places[0] * 4 + places[1]) * 2 + (x ^ (block % 2))
                    row = pl.multiple_of(index * (2 * half) + order * half, half)
                    if outer < 3:
                        source = sources[order][outer].at[block]
                    else:
                        source = sources[order][3 + block // 4].at[block % 4]
                    start = 0
                    for out, width in zip(outs, widths):
                        copy = pltpu.make_async_copy(
                            source.at[:, pl.ds(start, width)], out.at[pl.ds(row, half), :], sem
                        )
                        copy.start()
                        copies.append(copy)
                        start += width
        for copy in copies:
            copy.wait()

    return pl.pallas_call(
        kernel,
        out_shape=[jax.ShapeDtypeStruct((rows, width), B16) for width in widths],
        in_specs=[pl.BlockSpec(memory_space=pl.ANY)] * 10,
        out_specs=[pl.BlockSpec(memory_space=pl.ANY)] * len(widths),
        scratch_shapes=[pltpu.SemaphoreType.DMA],
        cost_estimate=pl.CostEstimate(
            flops=0, bytes_accessed=4 * rows * sum(widths), transcendentals=0
        ),
    )(*pieces_a, *pieces_b)


def first_blocks(shard, other):
    half = shard.shape[0] // 2
    return (jnp.stack([shard[:half], other[:half]]), jnp.stack([shard[half:], other[half:]]))


def ring_sends(part_a, part_b):
    return [(part_a, UP_Y), (part_a, DOWN_Y), (part_b, UP_Z), (part_b, DOWN_Z)]


def plane_sends(part_a, part_b):
    return [(part_a, UP_Z), (part_a, DOWN_Z), (part_b, UP_Y), (part_b, DOWN_Y)]


def relay_sends(sends, arrived):
    out = []
    for i, (_, pairs) in enumerate(sends):
        middle = arrived[i].shape[0] // 2
        out.append((arrived[i][:middle] if i % 2 == 0 else arrived[i][middle:], pairs))
    return out


def planes(part_a, part_b, near, far):
    return (
        jnp.concatenate([part_a, near[0], near[1], far[0], far[1]], axis=0),
        jnp.concatenate([part_b, near[2], near[3], far[2], far[3]], axis=0),
    )


def exchange(sends, *others):
    results = [send(values, pairs) for values, pairs in sends]
    out = together(*results, *others)
    return list(out[: len(sends)]), list(out[len(sends) :])


def in_place(values, place, axis=0):
    own, core, far, far_core = values
    swap_core, swap_far = place.core == 1, place.far == 1
    near = jnp.stack([jnp.where(swap_core, core, own), jnp.where(swap_core, own, core)])
    away = jnp.stack([jnp.where(swap_core, far_core, far), jnp.where(swap_core, far, far_core)])
    return jnp.concatenate(
        [jnp.where(swap_far, away, near), jnp.where(swap_far, near, away)], axis=0
    )


def scatter_tokens(near, away):
    sent = send(away().astype(B16), CORES)
    summed = near() + sent.astype(F32)
    rows = summed.shape[0] // 2
    return summed[:rows] + send(summed[rows:].astype(B16), FAR_X).astype(F32)


def norm_forward(values, gain_value):
    factor = lax.rsqrt(jnp.mean(values * values, axis=-1, keepdims=True) + NORM_EPS)
    return (values * factor * gain_value, factor)


def norm_backward(values, factor, gain_value, gradient):
    scaled = gradient * gain_value
    return factor * (
        scaled - values * factor * factor * jnp.mean(scaled * values, axis=-1, keepdims=True)
    )


TRANSPOSED_RIGHT = (((1,), (1,)), ((), ()))
TRANSPOSED_LEFT = (((0,), (0,)), ((), ()))


def dot_of(left, right, dims):
    return lax.dot_general(left, right, dims, preferred_element_type=F32)


def quarter_places(own, rows):
    return [pl.multiple_of((own ^ t) * rows, rows) for t in range(4)]


def attention_forward(own, lambda_all, near, far, heads):
    half, width = near.shape
    length, proj = 2 * half, width // 3
    rows = half // 2

    def kernel(own_ref, lambda_ref, near_ref, far_ref, att_ref, raw_ref, lse_ref, qkv_ref):
        for t in range(4):
            at = own_ref[0] ^ t
            start = pl.multiple_of((at & 1) * rows, rows)

            @pl.when(at < 2)
            def _():
                qkv_ref[t * rows : (t + 1) * rows, :] = near_ref[pl.ds(start, rows), :]

            @pl.when(at >= 2)
            def _():
                qkv_ref[t * rows : (t + 1) * rows, :] = far_ref[pl.ds(start, rows), :]

        for head in range(heads):
            column = head * 2 * HEAD_DIM
            value_columns = slice(2 * proj + column, 2 * proj + column + 2 * HEAD_DIM)
            for block in range(length // BLOCK):
                queries = slice(block * BLOCK, (block + 1) * BLOCK)
                keys = slice(0, (block + 1) * BLOCK)
                parts = []
                for c in range(2):
                    first = column + c * HEAD_DIM
                    scores = (
                        dot_of(
                            qkv_ref[keys, proj + first : proj + first + HEAD_DIM],
                            qkv_ref[queries, first : first + HEAD_DIM],
                            TRANSPOSED_RIGHT,
                        )
                        * HEAD_DIM**-0.5
                    )
                    top = jnp.max(scores, axis=0, keepdims=True)
                    shifted = jnp.exp(scores - top)
                    total = jnp.sum(shifted, axis=0, keepdims=True)
                    lse_ref[head * 2 + c : head * 2 + c + 1, queries] = top + jnp.log(total)
                    parts.append(shifted * (1.0 / total))
                combined = (parts[0] - lambda_ref[head] * parts[1]).astype(B16)
                raw = dot_of(combined, qkv_ref[keys, value_columns], TRANSPOSED_LEFT)
                raw_ref[queries, column : column + 2 * HEAD_DIM] = raw
        for t in range(4):
            start = pl.multiple_of((own_ref[0] ^ t) * rows, rows)
            for head in range(heads):
                columns = slice(head * 2 * HEAD_DIM, (head + 1) * 2 * HEAD_DIM)
                raw = raw_ref[t * rows : (t + 1) * rows, columns]
                factor = lax.rsqrt(jnp.mean(raw * raw, axis=-1, keepdims=True) + NORM_EPS)
                att_ref[pl.ds(start, rows), columns] = (raw * factor * OUT_GAIN).astype(B16)

    vmem = pl.BlockSpec(memory_space=pltpu.VMEM)
    smem = pl.BlockSpec(memory_space=pltpu.SMEM)
    return pl.pallas_call(
        kernel,
        out_shape=[
            jax.ShapeDtypeStruct((length, proj), B16),
            jax.ShapeDtypeStruct((length, proj), F32),
            jax.ShapeDtypeStruct((2 * heads, length), F32),
            jax.ShapeDtypeStruct((length, width), B16),
        ],
        in_specs=[smem, smem, vmem, vmem],
        out_specs=[vmem] * 4,
        compiler_params=pltpu.CompilerParams(vmem_limit_bytes=40 * 2**20),
        cost_estimate=pl.CostEstimate(
            flops=4 * length * length * proj, bytes_accessed=12 * length * width, transcendentals=2 * length * length * heads
        ),
    )(own, lambda_all, near, far)


def attention_backward(own, lambda_all, qkv, raw, lse, grad_near, grad_far, heads):
    length, width = qkv.shape
    proj, rows = width // 3, length // 4

    def kernel(
        own_ref, lambda_ref, qkv_ref, raw_ref, lse_ref, near_ref, far_ref, out_ref, graw_ref, acc_ref
    ):
        for t in range(4):
            at = own_ref[0] ^ t
            start = pl.multiple_of((at & 1) * rows, rows)

            def branch(source):
                for head in range(heads):
                    columns = slice(head * 2 * HEAD_DIM, (head + 1) * 2 * HEAD_DIM)
                    values = raw_ref[t * rows : (t + 1) * rows, columns]
                    factor = lax.rsqrt(
                        jnp.mean(values * values, axis=-1, keepdims=True) + NORM_EPS
                    )
                    grad = norm_backward(
                        values, factor, OUT_GAIN, source[pl.ds(start, rows), columns]
                    )
                    graw_ref[t * rows : (t + 1) * rows, columns] = grad.astype(B16)

            @pl.when(at < 2)
            def _():
                branch(near_ref)

            @pl.when(at >= 2)
            def _():
                branch(far_ref)

        for head in range(heads):
            column = head * 2 * HEAD_DIM
            value_columns = slice(2 * proj + column, 2 * proj + column + 2 * HEAD_DIM)
            key_columns = slice(proj + column, proj + column + 2 * HEAD_DIM)
            for block in reversed(range(length // BLOCK)):
                queries = slice(block * BLOCK, (block + 1) * BLOCK)
                keys = slice(0, (block + 1) * BLOCK)
                graw = graw_ref[queries, column : column + 2 * HEAD_DIM]
                probs = []
                for c in range(2):
                    first = column + c * HEAD_DIM
                    scores = (
                        dot_of(
                            qkv_ref[keys, proj + first : proj + first + HEAD_DIM],
                            qkv_ref[queries, first : first + HEAD_DIM],
                            TRANSPOSED_RIGHT,
                        )
                        * HEAD_DIM**-0.5
                    )
                    probs.append(
                        jnp.exp(scores - lse_ref[head * 2 + c : head * 2 + c + 1, queries])
                    )
                lambda_one = lambda_ref[head]
                combined = (probs[0] - lambda_one * probs[1]).astype(B16)
                grad_values = product(combined, graw)
                grad_combined = dot_of(qkv_ref[keys, value_columns], graw, TRANSPOSED_RIGHT)
                grad_keys = []
                for c in range(2):
                    first = column + c * HEAD_DIM
                    weighted = probs[c] * grad_combined
                    inner = jnp.sum(weighted, axis=0, keepdims=True)
                    scale = HEAD_DIM**-0.5 if c == 0 else -lambda_one * HEAD_DIM**-0.5
                    grad_scores = ((weighted - probs[c] * inner) * scale).astype(B16)
                    grad_keys.append(product(grad_scores, qkv_ref[queries, first : first + HEAD_DIM]))
                    acc_ref[queries, first : first + HEAD_DIM] = dot_of(
                        grad_scores,
                        qkv_ref[keys, proj + first : proj + first + HEAD_DIM],
                        TRANSPOSED_LEFT,
                    )
                grad_key = jnp.concatenate(grad_keys, axis=1)
                if block == length // BLOCK - 1:
                    acc_ref[keys, key_columns] = grad_key
                    acc_ref[keys, value_columns] = grad_values
                else:
                    acc_ref[keys, key_columns] += grad_key
                    acc_ref[keys, value_columns] += grad_values
        for t in range(4):
            start = pl.multiple_of((own_ref[0] ^ t) * rows, rows)
            out_ref[pl.ds(start, rows), :] = acc_ref[t * rows : (t + 1) * rows, :].astype(B16)

    vmem = pl.BlockSpec(memory_space=pltpu.VMEM)
    smem = pl.BlockSpec(memory_space=pltpu.SMEM)
    return pl.pallas_call(
        kernel,
        out_shape=jax.ShapeDtypeStruct((length, width), B16),
        in_specs=[smem, smem] + [vmem] * 5,
        out_specs=vmem,
        scratch_shapes=[pltpu.VMEM((length, proj), B16), pltpu.VMEM((length, width), F32)],
        compiler_params=pltpu.CompilerParams(vmem_limit_bytes=48 * 2**20),
        cost_estimate=pl.CostEstimate(
            flops=10 * length * length * proj, bytes_accessed=14 * length * width, transcendentals=2 * length * length * heads
        ),
    )(own, lambda_all, qkv, raw, lse, grad_near, grad_far)


def adam_step(parameter, gradient, moment, variance, factor):
    clipped = gradient * factor
    moment_new = BETA_FIRST * moment + (1.0 - BETA_FIRST) * clipped
    variance_new = BETA_SECOND * variance + (1.0 - BETA_SECOND) * clipped * clipped
    moment_hat = moment_new / (1.0 - BETA_FIRST**STEP)
    variance_hat = variance_new / (1.0 - BETA_SECOND**STEP)
    updated = parameter - LEARN_RATE * (
        moment_hat / (jnp.sqrt(variance_hat) + ADAM_EPS) + WEIGHT_DECAY * parameter
    )
    return (clipped, updated, moment_new, variance_new)


def flat_rows(stacked):
    moved = stacked.astype(B16).transpose(1, 0, 2)
    return moved.reshape(stacked.shape[1], -1)


def fold_rows(rows, lanes):
    padded = jnp.pad(rows, ((0, 0), (0, 16 * lanes - rows.shape[1])))
    return padded.reshape(64, lanes)


def pick_rows(gathered, adapter, width):
    lanes = gathered.shape[1]
    mine = lax.dynamic_slice_in_dim(gathered, adapter * 256, 256, 0)
    return mine.reshape(16, 16 * lanes)[:, :width]


def local(
    tokens,
    cotangent,
    adapter_ids,
    norm_gains,
    lambda_vectors,
    weight_inputs,
    weight_output,
    hidden_weight_matrix,
    weight_down,
    adapter_wide,
    adapter_attention,
    adapter_feedforward,
    moment_wide,
    variance_wide,
    moment_attention,
    variance_attention,
    moment_feedforward,
    variance_feedforward,
):
    place = Place()
    adapter = adapter_ids[0]
    own_quarter = place.tensor.astype(jnp.int32).reshape(1)
    local_tokens = tokens[0].astype(F32)
    upstream_b = cotangent[0]
    gain_values = norm_gains.astype(F32)
    lambda_all = (
        jnp.exp(jnp.sum(lambda_vectors[0] * lambda_vectors[1], axis=-1))
        - jnp.exp(jnp.sum(lambda_vectors[2] * lambda_vectors[3], axis=-1))
        + LAMBDA_INIT
    )
    heads_local = lambda_vectors.shape[1]
    proj = weight_inputs.shape[2]
    ff = hidden_weight_matrix.shape[2]
    rows = tokens.shape[1]

    wide_flat = jnp.pad(
        adapter_wide.astype(B16).transpose(0, 2, 1).reshape(112, 128), ((0, 16), (0, 0))
    )
    shard_one = jnp.concatenate(
        [
            weight_inputs[0],
            weight_inputs[1],
            weight_inputs[2],
            weight_output.T,
            fold_rows(flat_rows(adapter_attention), 128),
            wide_flat[:64],
            wide_flat[64:],
        ],
        axis=1,
    )
    shard_two = jnp.concatenate(
        [
            hidden_weight_matrix[0],
            hidden_weight_matrix[1],
            weight_down.T,
            fold_rows(flat_rows(adapter_feedforward), 384),
        ],
        axis=1,
    )
    normed_one, scale_one = norm_forward(local_tokens, gain_values[0])
    normed_one_b = normed_one.astype(B16)

    (other_one, core_normed), (shard_one, shard_two, upstream_b) = exchange(
        [(shard_one, PAIR_X), (normed_one_b, CORES)], shard_one, shard_two, upstream_b
    )
    blocks_one = first_blocks(shard_one, other_one)
    sends = ring_sends(*blocks_one)
    (*near, other_two), (upstream_b, normed_out) = exchange(
        sends + [(shard_two, PAIR_X)], upstream_b, normed_one_b
    )
    (*far, core_upstream), (normed_out, upstream_b) = exchange(
        relay_sends(sends, near) + [(upstream_b, CORES)], normed_out, upstream_b
    )
    planes_one = planes(*blocks_one, near, far)
    sends = plane_sends(*planes_one)
    (*near_one, far_normed), (upstream_b,) = exchange(sends + [(normed_out, FAR_X)], upstream_b)
    (*far_one, far_upstream), (shard_two, other_two) = exchange(
        relay_sends(sends, near_one) + [(upstream_b, FAR_X)], shard_two, other_two
    )
    w_in, w_out, fold_one = assemble(
        (planes_one[0], near_one[0], near_one[1], far_one[0], far_one[1]),
        (planes_one[1], near_one[2], near_one[3], far_one[2], far_one[3]),
        (3 * proj, proj, 384),
    )
    blocks_two = first_blocks(shard_two, other_two)
    sends = ring_sends(*blocks_two)
    near, _ = exchange(sends)
    far, _ = exchange(relay_sends(sends, near))
    planes_two = planes(*blocks_two, near, far)
    sends = plane_sends(*planes_two)
    near_two, _ = exchange(sends)
    far_two, _ = exchange(relay_sends(sends, near_two))
    w_hidden, w_down, fold_two = assemble(
        (planes_two[0], near_two[0], near_two[1], far_two[0], far_two[1]),
        (planes_two[1], near_two[2], near_two[3], far_two[2], far_two[3]),
        (2 * ff, ff, 384),
    )
    pick_attention = pick_rows(fold_one[:, :128], adapter, 4 * proj)
    pick_feedforward = pick_rows(fold_two, adapter, 3 * ff)
    pick_hidden, pick_down = pick_feedforward[:, : 2 * ff], pick_feedforward[:, 2 * ff :]

    onehot_rows = (
        jnp.arange(128)[None, :, None]
        == (adapter * RANK + jnp.arange(128) - RANK * jnp.arange(8)[:, None])[:, None, :]
    ) & (jnp.arange(128)[None, None, :] // RANK == jnp.arange(8)[:, None, None])
    wide_mine = (
        fold_one[:, 128:].reshape(32, 4, 16, 2, 128).transpose(0, 2, 3, 1, 4).reshape(512, 1024)
    )
    picked_t = product(wide_mine, onehot_rows.astype(B16).reshape(1024, 128)).astype(B16)
    picked_far = send(picked_t, FAR_X)
    picked_all = in_place(
        [picked_t, send(picked_t, CORES), picked_far, send(picked_far, CORES)], place
    ).reshape(4, 32, 16, 128)
    picked_wide = picked_all.transpose(1, 0, 2, 3).reshape(2048, 128)

    def diagonal(values, width):
        count = values.shape[1] // width
        column = jnp.arange(values.shape[1]) // width
        row = jnp.arange(count * RANK) // RANK
        tiled = jnp.concatenate([values] * count, axis=0)
        return jnp.where(row[:, None] == column[None, :], tiled, 0).astype(B16)

    half = jnp.asarray(ADAPTER_SCALING, B16)
    pad_rank = lambda v: jnp.pad(v, ((0, 0), (0, 128 - v.shape[1])))

    seq_normed_one = [
        jnp.concatenate([normed_one_b, core_normed], axis=0),
        jnp.concatenate([far_normed, send(far_normed, CORES)], axis=0),
    ]
    seq_upstream = [
        jnp.concatenate([upstream_b, core_upstream], axis=0),
        jnp.concatenate([far_upstream, send(far_upstream, CORES)], axis=0),
    ]

    def by_core(pair):
        return [jnp.concatenate([v[:rows] for v in pair]), jnp.concatenate([v[rows:] for v in pair])]

    lowrank_inputs = [product(v, picked_wide).astype(B16)[:, 0:48] for v in seq_normed_one]
    diag_in = diagonal(pick_attention[:, : 3 * proj], proj)
    projected = [
        (product(v, w_in) + product(low * half, diag_in)).astype(B16)
        for v, low in zip(seq_normed_one, lowrank_inputs)
    ]
    attention_b, raw, lse, qkv = attention_forward(
        own_quarter, lambda_all, projected[0], projected[1], heads_local
    )
    pick_out = pick_attention[:, 3 * proj :]

    def partial_sum(values, weights, low, scaling, form="lc,dc->ld"):
        return jnp.concatenate(
            [
                contract(form, values, weights),
                pad_rank(scaling * contract("lc,rc->lr", values, low)),
            ],
            axis=1,
        )

    halves = by_core([attention_b[: 2 * rows], attention_b[2 * rows :]])
    out_sum = scatter_tokens(
        *[lambda v=v: partial_sum(v, w_out, pick_out, 1.0) for v in halves]
    )
    lowrank_out_b = out_sum[:, 2048 : 2048 + RANK].astype(B16)
    residual_one = (
        local_tokens
        + out_sum[:, :2048]
        + contract("tr,dr->td", lowrank_out_b * half, picked_wide[:, 80:96])
    )

    def gather_tokens(values):
        core, far_values = send(values, CORES), send(values, FAR_X)
        return [
            jnp.concatenate([values, core], axis=0),
            jnp.concatenate([far_values, send(far_values, CORES)], axis=0),
        ]

    second_normalized, scale_two = norm_forward(residual_one, gain_values[1])
    normed_two_b = second_normalized.astype(B16)
    seq_normed_two = gather_tokens(normed_two_b)
    lowrank_hidden = [product(v, picked_wide).astype(B16)[:, 48:80] for v in seq_normed_two]
    diag_hidden = diagonal(pick_hidden, ff)
    gate_up = [
        product(v, w_hidden) + product(low * half, diag_hidden)
        for v, low in zip(seq_normed_two, lowrank_hidden)
    ]
    hidden_b = [(jax.nn.silu(v[:, :ff]) * v[:, ff:]).astype(B16) for v in gate_up]
    down_sum = scatter_tokens(
        *[lambda v=v: partial_sum(v, w_down, pick_down, 1.0) for v in by_core(hidden_b)]
    )
    lowrank_down_b = down_sum[:, 2048 : 2048 + RANK].astype(B16)
    result = (
        residual_one
        + down_sum[:, :2048]
        + contract("tr,dr->td", lowrank_down_b * half, picked_wide[:, 96:112])
    )

    grad_right_down = ADAPTER_SCALING * contract("td,tr->dr", upstream_b, lowrank_down_b)
    grad_lowrank_down = [
        (ADAPTER_SCALING * product(v, picked_wide)).astype(B16)[:, 96:112] for v in seq_upstream
    ]
    grad_gate_up = []
    for v, low, gates in zip(seq_upstream, grad_lowrank_down, gate_up):
        grad_hidden = product(v, w_down) + product(low, pick_down)
        gate, upper = gates[:, :ff], gates[:, ff:]
        sigmoid_gate = jax.nn.sigmoid(gate)
        grad_gate = grad_hidden * upper * sigmoid_gate * (1.0 + gate * (1.0 - sigmoid_gate))
        grad_upper = grad_hidden * gate * sigmoid_gate
        grad_gate_up.append(
            jnp.concatenate([grad_gate.astype(B16), grad_upper.astype(B16)], axis=1)
        )

    def token_sum(left, right):
        return sum(contract("lr,lc->rc", a, b) for a, b in zip(left, right))

    grad_left_down = token_sum(grad_lowrank_down, hidden_b)
    right_hidden = [
        ADAPTER_SCALING
        * token_sum(
            [v[:, RANK * i : RANK * (i + 1)] for v in lowrank_hidden],
            [v[:, ff * i : ff * (i + 1)] for v in grad_gate_up],
        )
        for i in range(2)
    ]
    hidden_sum = scatter_tokens(
        *[
            lambda v=v: partial_sum(v, w_hidden, diag_hidden, ADAPTER_SCALING)
            for v in by_core(grad_gate_up)
        ]
    )
    grad_lowrank_hidden = hidden_sum[:, 2048 : 2048 + 2 * RANK].astype(B16)
    grad_left_hidden = contract("td,tr->dr", normed_two_b, grad_lowrank_hidden)
    grad_normed_two = hidden_sum[:, :2048] + contract(
        "tr,dr->td", grad_lowrank_hidden, picked_wide[:, 48:80]
    )
    grad_residual = upstream_b.astype(F32) + norm_backward(
        residual_one, scale_two, gain_values[1], grad_normed_two
    )

    grad_branch_b = grad_residual.astype(B16)
    grad_right_out = ADAPTER_SCALING * contract("td,tr->dr", grad_branch_b, lowrank_out_b)
    seq_grad_branch = gather_tokens(grad_branch_b)
    grad_lowrank_out = [
        (ADAPTER_SCALING * product(v, picked_wide)).astype(B16)[:, 80:96] for v in seq_grad_branch
    ]
    grad_attention_in = [
        product(v, w_out) + product(low, pick_out)
        for v, low in zip(seq_grad_branch, grad_lowrank_out)
    ]
    grad_left_out = token_sum(
        grad_lowrank_out, [attention_b[: 2 * rows], attention_b[2 * rows :]]
    )
    grad_projected = attention_backward(
        own_quarter, lambda_all, qkv, raw, lse, *grad_attention_in, heads_local
    )
    grad_projected_pair = [grad_projected[: 2 * rows], grad_projected[2 * rows :]]
    right_inputs = [
        ADAPTER_SCALING
        * token_sum(
            [v[:, RANK * i : RANK * (i + 1)] for v in lowrank_inputs],
            [v[:, proj * i : proj * (i + 1)] for v in grad_projected_pair],
        )
        for i in range(3)
    ]
    input_sum = scatter_tokens(
        *[
            lambda v=v: partial_sum(v, w_in, diag_in, ADAPTER_SCALING)
            for v in by_core(grad_projected_pair)
        ]
    )
    grad_lowrank_inputs = input_sum[:, 2048 : 2048 + 3 * RANK].astype(B16)
    grad_left_inputs = contract("td,tr->dr", normed_one_b, grad_lowrank_inputs)
    grad_normed_one = input_sum[:, :2048] + contract(
        "tr,dr->td", grad_lowrank_inputs, picked_wide[:, 0:48]
    )
    grad_input = grad_residual + norm_backward(
        local_tokens, scale_one, gain_values[0], grad_normed_one
    )

    wide_grads = jnp.concatenate(
        [
            grad_left_inputs,
            grad_left_hidden,
            grad_right_out,
            grad_right_down,
            jnp.zeros((2048, RANK), F32),
        ],
        axis=1,
    ).astype(B16)
    split_grads = jnp.concatenate(
        right_inputs + [grad_left_out] + right_hidden + [grad_left_down], axis=1
    ).astype(B16)
    columns = split_grads.shape[1]
    piece = -(-columns // 1024) * 128
    split_blocks = (
        jnp.pad(split_grads, ((0, 0), (0, 8 * piece - columns)))
        .reshape(4, 4, 2, 4, piece)
        .transpose(1, 2, 0, 3, 4)
        .reshape(128, piece // 128, 128)
    )
    blocks = jnp.concatenate(
        [
            wide_grads.reshape(128, 16, 128),
            split_blocks,
            jnp.broadcast_to(adapter.astype(B16), (128, 8 - piece // 128, 128)),
        ],
        axis=1,
    )
    arrived = lax.all_to_all(blocks, AXES, split_axis=0, concat_axis=0, tiled=True)
    ids_all = arrived.reshape(32, 4, 24, 128)[:, 0, 23, 0].astype(jnp.int32)
    member = ids_all[None, :] == jnp.arange(ADAPTERS)[:, None]
    onehot = member.astype(B16)
    wide_sum = contract(
        "es,sn->en",
        onehot,
        arrived[:, :16].reshape(32, 4 * 16 * 128),
    ).reshape(8, 4, 16, 128).sum(1)
    split_sum = contract(
        "es,sn->en", onehot, arrived[:, 16:].reshape(32, 4 * 8 * 128)
    ).reshape(8, 4, 8, 128)[:, :, : piece // 128]
    squares = jnp.sum(wide_sum * wide_sum) + jnp.sum(split_sum * split_sum)
    grads_wide = (
        wide_sum[:, :, :112].reshape(8, 16, 7, 16).transpose(2, 0, 3, 1).reshape(7, 128, 16)
    )
    mine = place.dp % 4
    split_out = jnp.concatenate(
        [split_sum.reshape(32, 7, 128), jnp.zeros((32, 1, 128), F32)], axis=1
    ).reshape(8, 1, 4, 8, 128)
    quarter = jnp.arange(4)[None, :, None, None, None]
    spread = jnp.where(quarter == mine, split_out, 0.0).reshape(128, 8, 128)
    spread = jnp.where(jnp.arange(8)[None, :, None] == 7, squares, spread)
    placed = lax.all_to_all(spread, AXES, split_axis=0, concat_axis=0, tiled=True)
    total_squares = jnp.sum(placed[:, 7, 0])
    from_mine = lax.dynamic_index_in_dim(
        placed.reshape(8, 4, 4, 8, 128), mine, 1, keepdims=False
    )
    split_rows = from_mine[:, :, :7].reshape(4, 8 * piece)[:, :columns]
    grads_attention = split_rows[:, : 4 * proj].reshape(4, 4, proj).transpose(1, 0, 2)
    grads_feedforward = split_rows[:, 4 * proj :].reshape(4, 3, ff).transpose(1, 0, 2)

    grad_norm = jnp.sqrt(total_squares)
    factor = CLIP_NORM / (grad_norm + 1e-06)
    wide_new = adam_step(adapter_wide, grads_wide, moment_wide, variance_wide, factor)
    attention_new = adam_step(
        adapter_attention, grads_attention, moment_attention, variance_attention, factor
    )
    feedforward_new = adam_step(
        adapter_feedforward, grads_feedforward, moment_feedforward, variance_feedforward, factor
    )
    return (
        result.astype(B16)[None],
        grad_input.astype(B16)[None],
        grad_norm,
        wide_new[0],
        attention_new[0],
        feedforward_new[0],
        wide_new[1],
        attention_new[1],
        feedforward_new[1],
        wide_new[2],
        attention_new[2],
        feedforward_new[2],
        wide_new[3],
        attention_new[3],
        feedforward_new[3],
    )


def solution(mesh):
    return jax.shard_map(
        local,
        mesh=mesh,
        in_specs=(
            P("dp", "tensor", None),
            P("dp", "tensor", None),
            P("dp"),
            P(),
            P(None, "tensor", None),
            P(None, "dp", "tensor"),
            P("tensor", "dp"),
            P(None, "dp", "tensor"),
            P("tensor", "dp"),
            P(None, None, ("dp", "tensor")),
            P(None, "dp", "tensor"),
            P(None, "dp", "tensor"),
            P(None, None, ("dp", "tensor")),
            P(None, None, ("dp", "tensor")),
            P(None, "dp", "tensor"),
            P(None, "dp", "tensor"),
            P(None, "dp", "tensor"),
            P(None, "dp", "tensor"),
        ),
        out_specs=(
            P("dp", "tensor", None),
            P("dp", "tensor", None),
            P(),
            P(None, None, ("dp", "tensor")),
            P(None, "dp", "tensor"),
            P(None, "dp", "tensor"),
            P(None, None, ("dp", "tensor")),
            P(None, "dp", "tensor"),
            P(None, "dp", "tensor"),
            P(None, None, ("dp", "tensor")),
            P(None, "dp", "tensor"),
            P(None, "dp", "tensor"),
            P(None, None, ("dp", "tensor")),
            P(None, "dp", "tensor"),
            P(None, "dp", "tensor"),
        ),
        check_vma=False,
    )
```

```python
import jax
import jax.numpy as jnp
from jax import lax
from jax.experimental import pallas as pl
from jax.experimental.pallas import tpu as pltpu
from jax.sharding import PartitionSpec as P

HEAD_DIM = 128
ADAPTERS = 8
RANK = 16
BLOCK = 256
STEP = 10


NORM_EPS = 1e-05
ADAPTER_SCALING = 0.5
LAMBDA_INIT = 0.2
OUT_GAIN = 0.8
CLIP_NORM = 1.0
LEARN_RATE = 0.05
BETA_FIRST = 0.9
BETA_SECOND = 0.999
ADAM_EPS = 1e-08
WEIGHT_DECAY = 0.01
NEG_LARGE = -1e30
AXES = ("dp", "tensor")
B16 = jnp.bfloat16
F32 = jnp.float32


def product(left, right):
    return jnp.dot(left, right, preferred_element_type=F32)


def contract(form, left, right):
    return jnp.einsum(form, left, right, preferred_element_type=F32)


def index_of(z, y, x, core):
    x, y, z, core = x % 4, y % 4, z % 4, core % 2
    return ((z * 4 + y) * 2 + x % 2) * 4 + (x // 2) * 2 + core


def routes(move):
    pairs = []
    for z in range(4):
        for y in range(4):
            for x in range(4):
                for core in range(2):
                    pairs.append((index_of(z, y, x, core), index_of(*move(z, y, x, core))))
    return pairs


UP_Z = routes(lambda z, y, x, c: (z + 1, y, x, c))
DOWN_Z = routes(lambda z, y, x, c: (z - 1, y, x, c))
FAR_Z = routes(lambda z, y, x, c: (z + 2, y, x, c))
UP_Y = routes(lambda z, y, x, c: (z, y + 1, x, c))
DOWN_Y = routes(lambda z, y, x, c: (z, y - 1, x, c))
FAR_Y = routes(lambda z, y, x, c: (z, y + 2, x, c))
PAIR_X = routes(lambda z, y, x, c: (z, y, x ^ 1, c))
FAR_X = routes(lambda z, y, x, c: (z, y, x + 2, c))
CORES = routes(lambda z, y, x, c: (z, y, x, 1 - c))


def send(values, pairs):
    return lax.ppermute(values, AXES, pairs)


class Place:
    def __init__(self):
        tensor = lax.axis_index("tensor")
        self.far, self.core, self.tensor = tensor // 2, tensor % 2, tensor
        self.dp = lax.axis_index("dp")


def together(*values):
    return lax.optimization_barrier(values)


OFFSETS = (0, 3, 1, 2)
LANES = 128
CHUNK = 512


def copy_pieces(pieces, held, sems, groups, first=0):
    sources = (pieces[:5], pieces[5:10])
    dp = lax.axis_index("dp")
    at = (dp // 8, (dp // 2) & 3)
    started = []
    for i, (start, width) in enumerate(groups):
        columns, kept = pl.ds(start, width), pl.ds(start - first, width)
        copies = []
        for order in range(2):
            for outer in range(4):
                for block in range(4):
                    places = [0, 0]
                    places[order] = (at[order] + OFFSETS[outer]) & 3
                    places[1 - order] = (at[1 - order] + OFFSETS[block]) & 3
                    if outer < 3:
                        source = sources[order][outer].at[pl.ds(2 * block, 2), :, columns]
                    else:
                        part = sources[order][3 + block // 2]
                        source = part.at[pl.ds(2 * (block % 2), 2), :, columns]
                    copy = pltpu.make_async_copy(
                        source, held.at[places[0] * 4 + places[1], :, order, :, kept], sems.at[i]
                    )
                    copy.start()
                    copies.append(copy)
        started.append(copies)
    return started


def copy_quarters(quarters, held, sem):
    rows = quarters[0].shape[0]
    copies = [
        pltpu.make_async_copy(quarter, held.at[pl.ds(i * rows, rows), :], sem)
        for i, quarter in enumerate(quarters)
    ]
    for copy in copies:
        copy.start()
    return copies


def wait_all(copies):
    for copy in copies:
        copy.wait()


def first_blocks(shard, other, place):
    half = shard.shape[0] // 2
    swap = place.dp % 2 == 1
    low, high = jnp.where(swap, other, shard), jnp.where(swap, shard, other)
    return (jnp.stack([low[:half], high[:half]]), jnp.stack([low[half:], high[half:]]))


def ring_sends(part_a, part_b):
    return [(part_a, UP_Y), (part_a, DOWN_Y), (part_b, UP_Z), (part_b, DOWN_Z)]


def plane_sends(part_a, part_b):
    return [(part_a, UP_Z), (part_a, DOWN_Z), (part_b, UP_Y), (part_b, DOWN_Y)]


def relay_sends(sends, arrived):
    out = []
    for i, (_, pairs) in enumerate(sends):
        middle = arrived[i].shape[0] // 2
        out.append((arrived[i][:middle] if i % 2 == 0 else arrived[i][middle:], pairs))
    return out


def planes(part_a, part_b, near, far, start, width):
    cut = lambda v: v[..., start : start + width]
    return (
        jnp.concatenate([cut(v) for v in (part_a, near[0], near[1], far[0], far[1])], axis=0),
        jnp.concatenate([cut(v) for v in (part_b, near[2], near[3], far[2], far[3])], axis=0),
    )


def pieces_of(plane_pair, near, far):
    return (
        plane_pair[0],
        near[0],
        near[1],
        far[0],
        far[1],
        plane_pair[1],
        near[2],
        near[3],
        far[2],
        far[3],
    )


def exchange(sends, *others):
    results = [send(values, pairs) for values, pairs in sends]
    out = together(*results, *others)
    return list(out[: len(sends)]), list(out[len(sends) :])


def in_place(values, place):
    own, core, far, far_core = values
    swap_core, swap_far = place.core == 1, place.far == 1
    near = jnp.stack([jnp.where(swap_core, core, own), jnp.where(swap_core, own, core)])
    away = jnp.stack([jnp.where(swap_core, far_core, far), jnp.where(swap_core, far, far_core)])
    return jnp.concatenate(
        [jnp.where(swap_far, away, near), jnp.where(swap_far, near, away)], axis=0
    )


def core_sum(near, away):
    summed = near + send(away, CORES).astype(F32)
    rows = summed.shape[0] // 2
    return summed[:rows], summed[rows:].astype(B16)


def norm_forward(values, gain_value):
    factor = lax.rsqrt(jnp.mean(values * values, axis=-1, keepdims=True) + NORM_EPS)
    return (values * factor * gain_value, factor)


def norm_backward(values, factor, gain_value, gradient):
    scaled = gradient * gain_value
    return factor * (
        scaled - values * factor * factor * jnp.mean(scaled * values, axis=-1, keepdims=True)
    )


RIGHT_TURNED = (((1,), (1,)), ((), ()))
LEFT_TURNED = (((0,), (0,)), ((), ()))


def dot_of(left, right, dims):
    return lax.dot_general(left, right, dims, preferred_element_type=F32)


def away_rows(ref, rows, columns):
    return jnp.concatenate([ref[rows : 2 * rows, columns], ref[3 * rows : 4 * rows, columns]])


def near_rows(ref, rows, columns):
    return jnp.concatenate([ref[0:rows, columns], ref[2 * rows : 3 * rows, columns]])


ALL = slice(None)
VMEM = pl.BlockSpec(memory_space=pltpu.VMEM)
SMEM = pl.BlockSpec(memory_space=pltpu.SMEM)
ANY = pl.BlockSpec(memory_space=pl.ANY)


def shape(dtype, *dims):
    return jax.ShapeDtypeStruct(dims, dtype)


def params(mib):
    return pltpu.CompilerParams(vmem_limit_bytes=mib * 2**20)


def cost(flops, size):
    return pl.CostEstimate(flops=int(flops), bytes_accessed=int(size), transcendentals=0)


def scores_of(qkv_ref, proj, first, queries, keys):
    return (
        dot_of(
            qkv_ref[keys, proj + first : proj + first + HEAD_DIM],
            qkv_ref[queries, first : first + HEAD_DIM],
            RIGHT_TURNED,
        )
        * HEAD_DIM**-0.5
    )


def attention_part(own, lambda_all, pieces, quarters, picked_wide, spread_in, spread_out, heads):
    rows, model = quarters[0].shape
    length, half, total = 4 * rows, pieces[0].shape[1], pieces[0].shape[2]
    proj = spread_out.shape[1]
    columns_of = lambda i: slice(i * proj, (i + 1) * proj)

    def kernel(own_ref, lambda_ref, *refs):
        piece_refs, quarter_refs = refs[:10], refs[10:14]
        wide_ref, in_ref, out_ref = refs[14:17]
        w_out, att_ref, raw_ref, lse_ref, qkv_ref, low_ref, low_out_ref, away_ref, near_ref = refs[
            17:26
        ]
        held, x_ref, sems, x_sem, out_sem = refs[26:]
        arriving = copy_quarters(quarter_refs, x_ref, x_sem)
        groups = copy_pieces(piece_refs, held, sems, [(i * proj, proj) for i in range(4)])
        wait_all(arriving)
        low_ref[...] = product(x_ref[...], wide_ref[...]).astype(B16)
        low_half = low_ref[...] * jnp.asarray(ADAPTER_SCALING, B16)
        for i in range(3):
            wait_all(groups[i])
            weights = held[:, :, :, :, columns_of(i)].reshape(model, proj)
            for f in range(2):
                part = slice(2 * f * rows, 2 * (f + 1) * rows)
                values = product(x_ref[part, :], weights) + product(
                    low_half[part], in_ref[:, columns_of(i)]
                )
                for k in range(2):
                    start = pl.multiple_of((own_ref[0] ^ (2 * f + k)) * rows, rows)
                    qkv_ref[pl.ds(start, rows), columns_of(i)] = values[
                        k * rows : (k + 1) * rows
                    ].astype(B16)
        for head in range(heads):
            column = head * 2 * HEAD_DIM
            value_columns = slice(2 * proj + column, 2 * proj + column + 2 * HEAD_DIM)
            for block in range(length // BLOCK):
                queries = slice(block * BLOCK, (block + 1) * BLOCK)
                keys = slice(0, (block + 1) * BLOCK)
                parts = []
                for c in range(2):
                    scores = scores_of(qkv_ref, proj, column + c * HEAD_DIM, queries, keys)
                    top = jnp.max(scores, axis=0, keepdims=True)
                    shifted = jnp.exp(scores - top)
                    total_sum = jnp.sum(shifted, axis=0, keepdims=True)
                    lse_ref[head * 2 + c : head * 2 + c + 1, queries] = top + jnp.log(total_sum)
                    parts.append(shifted * (1.0 / total_sum))
                combined = (parts[0] - lambda_ref[head] * parts[1]).astype(B16)
                raw = dot_of(combined, qkv_ref[keys, value_columns], LEFT_TURNED)
                raw_ref[queries, column : column + 2 * HEAD_DIM] = raw
        for t in range(4):
            start = pl.multiple_of((own_ref[0] ^ t) * rows, rows)
            for head in range(heads):
                columns = slice(head * 2 * HEAD_DIM, (head + 1) * 2 * HEAD_DIM)
                raw = raw_ref[t * rows : (t + 1) * rows, columns]
                factor = lax.rsqrt(jnp.mean(raw * raw, axis=-1, keepdims=True) + NORM_EPS)
                att_ref[pl.ds(start, rows), columns] = (raw * factor * OUT_GAIN).astype(B16)
        wait_all(groups[3])
        leaving = pltpu.make_async_copy(held, w_out, out_sem)
        leaving.start()
        low_out_ref[...] = dot_of(att_ref[...], out_ref[...], RIGHT_TURNED).astype(B16)
        for pick, target in ((away_rows, away_ref), (near_rows, near_ref)):
            values = pick(att_ref, rows, ALL)
            low = pick(low_out_ref, rows, ALL) * jnp.asarray(ADAPTER_SCALING, B16)
            for start in range(0, model, CHUNK):
                blocks = slice(start // (4 * half), (start + CHUNK) // (4 * half))
                weights = held[blocks, :, :, :, columns_of(3)].reshape(CHUNK, proj)
                target[:, start : start + CHUNK] = (
                    dot_of(values, weights, RIGHT_TURNED)
                    + dot_of(low, wide_ref[start : start + CHUNK, :], RIGHT_TURNED)
                ).astype(target.dtype)
        leaving.wait()

    return pl.pallas_call(
        kernel,
        out_shape=[
            shape(B16, 16, 2, 2, half, total),
            shape(B16, length, proj),
            shape(F32, length, proj),
            shape(F32, 2 * heads, length),
            shape(B16, length, 3 * proj),
            shape(B16, length, LANES),
            shape(B16, length, LANES),
            shape(B16, 2 * rows, model),
            shape(F32, 2 * rows, model),
        ],
        in_specs=[SMEM, SMEM] + [ANY] * 14 + [VMEM] * 3,
        out_specs=[ANY] + [VMEM] * 8,
        scratch_shapes=[
            pltpu.VMEM((16, 2, 2, half, total), B16),
            pltpu.VMEM((length, model), B16),
            pltpu.SemaphoreType.DMA((4,)),
            pltpu.SemaphoreType.DMA,
            pltpu.SemaphoreType.DMA,
        ],
        compiler_params=params(48),
        cost_estimate=cost(2.6 * length * model * total, 2.4e7),
    )(own, lambda_all, *pieces, *quarters, picked_wide, spread_in, spread_out)


def hidden_part(pieces, quarters, upstream, picked_wide, spread_hidden, spread_down):
    rows, model = quarters[0].shape
    length, half, total = 2 * rows, pieces[0].shape[1], pieces[0].shape[2]
    ff = total // 3
    tiles = [(s, min(CHUNK, ff - s)) for s in range(0, ff, CHUNK)]

    def kernel(*refs):
        piece_refs, quarter_refs, upstream_refs = refs[:10], refs[10:12], refs[12:14]
        wide_ref, hidden_spread, down_spread = refs[14:17]
        hidden_ref, grad_ref, low_ref, grad_low_down, grad_low_ref, near_ref, away_ref = refs[17:24]
        held, x_ref, up_ref, sems, x_sems = refs[24:]
        arriving = [
            copy_quarters(upstream_refs, up_ref, x_sems.at[0]),
            copy_quarters(quarter_refs, x_ref, x_sems.at[1]),
        ]
        groups = [(2 * ff, ff)]
        for s, w in tiles:
            groups += [(s, w), (ff + s, w)]
        groups = copy_pieces(piece_refs, held, sems, groups)
        wait_all(arriving[0])
        grad_low_down[...] = (ADAPTER_SCALING * product(up_ref[...], wide_ref[...])).astype(B16)
        wait_all(arriving[1])
        low_ref[...] = product(x_ref[...], wide_ref[...]).astype(B16)
        low_half = low_ref[...] * jnp.asarray(ADAPTER_SCALING, B16)
        wait_all(groups[0])
        for i, (s, w) in enumerate(tiles):
            columns = slice(s, s + w)
            up_columns = slice(ff + s, ff + s + w)
            down_columns = slice(2 * ff + s, 2 * ff + s + w)
            grad_hidden = product(
                up_ref[...], held[:, :, :, :, down_columns].reshape(model, w)
            ) + product(grad_low_down[...], down_spread[:, columns])
            wait_all(groups[2 * i + 1])
            gate = product(x_ref[...], held[:, :, :, :, columns].reshape(model, w)) + product(
                low_half, hidden_spread[:, columns]
            )
            wait_all(groups[2 * i + 2])
            upper = product(x_ref[...], held[:, :, :, :, up_columns].reshape(model, w)) + product(
                low_half, hidden_spread[:, up_columns]
            )
            sigmoid_gate = 1.0 / (1.0 + jnp.exp(-gate))
            swish = gate * sigmoid_gate
            hidden_ref[:, columns] = (swish * upper).astype(B16)
            grad_ref[:, columns] = (
                grad_hidden * upper * (sigmoid_gate + swish * (1.0 - sigmoid_gate))
            ).astype(B16)
            grad_ref[:, up_columns] = (grad_hidden * swish).astype(B16)
        grad_low_ref[...] = (
            ADAPTER_SCALING * dot_of(grad_ref[...], hidden_spread[...], RIGHT_TURNED)
        ).astype(B16)
        for start in range(0, model, CHUNK):
            blocks = slice(start // (4 * half), (start + CHUNK) // (4 * half))
            weights = held[blocks, :, :, :, 0 : 2 * ff].reshape(CHUNK, 2 * ff)
            values = dot_of(grad_ref[...], weights, RIGHT_TURNED) + dot_of(
                grad_low_ref[...], wide_ref[start : start + CHUNK, :], RIGHT_TURNED
            )
            near_ref[:, start : start + CHUNK] = values[:rows]
            away_ref[:, start : start + CHUNK] = values[rows:].astype(B16)

    return pl.pallas_call(
        kernel,
        out_shape=[
            shape(B16, length, ff),
            shape(B16, length, 2 * ff),
            shape(B16, length, LANES),
            shape(B16, length, LANES),
            shape(B16, length, LANES),
            shape(F32, rows, model),
            shape(B16, rows, model),
        ],
        in_specs=[ANY] * 14 + [VMEM] * 3,
        out_specs=[VMEM] * 7,
        scratch_shapes=[
            pltpu.VMEM((16, 2, 2, half, total), B16),
            pltpu.VMEM((length, model), B16),
            pltpu.VMEM((length, model), B16),
            pltpu.SemaphoreType.DMA((2 * len(tiles) + 1,)),
            pltpu.SemaphoreType.DMA((2,)),
        ],
        compiler_params=params(52),
        cost_estimate=cost(10 * length * model * ff, 3e7),
    )(*pieces, *quarters, *upstream, picked_wide, spread_hidden, spread_down)


def down_part(pieces, halves, quarters, upstream, picked_wide, spread_down):
    rows, model = quarters[0].shape
    half, total = pieces[0].shape[1], pieces[0].shape[2]
    ff = total // 3

    def kernel(*refs):
        piece_refs, half_refs = refs[:10], (refs[10:15], refs[15:20])
        quarter_refs, upstream_refs = refs[20:24], refs[24:28]
        wide_ref, down_spread = refs[28:30]
        near_ref, away_ref, narrow_ref, wide_out = refs[30:34]
        held, x_ref, up_ref, sems, down_sems = refs[34:]
        arriving = [
            copy_quarters(upstream_refs, up_ref, sems.at[0]),
            copy_quarters(quarter_refs, x_ref, sems.at[1]),
        ]
        groups = copy_pieces(piece_refs, held, down_sems, [(2 * ff, ff)], 2 * ff)
        lows = []
        for f in range(2):
            hidden_ref = half_refs[f][0]
            low = dot_of(hidden_ref[...], down_spread[...], RIGHT_TURNED).astype(B16)
            lows.append(low * jnp.asarray(ADAPTER_SCALING, B16))
        for x in range(2):
            right = sum(
                dot_of(low_ref[...], grad_ref[:, x * ff : (x + 1) * ff], LEFT_TURNED)
                for _, grad_ref, low_ref, _, _ in half_refs
            )
            narrow_ref[:, x * ff : (x + 1) * ff] = (
                ADAPTER_SCALING * right[(3 + x) * RANK : (4 + x) * RANK]
            ).astype(B16)
        left = sum(
            dot_of(grad_low_down[...], hidden_ref[...], LEFT_TURNED)
            for hidden_ref, _, _, grad_low_down, _ in half_refs
        )
        narrow_ref[:, 2 * ff : 3 * ff] = left[6 * RANK : 7 * RANK].astype(B16)
        wait_all(groups[0])
        for f in range(2):
            hidden_ref = half_refs[f][0]
            for start in range(0, model, CHUNK):
                blocks = slice(start // (4 * half), (start + CHUNK) // (4 * half))
                values = dot_of(
                    hidden_ref[...], held[blocks].reshape(CHUNK, ff), RIGHT_TURNED
                ) + dot_of(lows[f], wide_ref[start : start + CHUNK, :], RIGHT_TURNED)
                near_ref[f * rows : (f + 1) * rows, start : start + CHUNK] = values[:rows]
                away_ref[f * rows : (f + 1) * rows, start : start + CHUNK] = values[rows:].astype(
                    B16
                )
        wait_all(arriving[0])
        wait_all(arriving[1])
        wide = 0.0
        for f in range(2):
            part = slice(2 * f * rows, 2 * (f + 1) * rows)
            wide += dot_of(lows[f], up_ref[part, :], LEFT_TURNED)
            wide += dot_of(half_refs[f][4][...], x_ref[part, :], LEFT_TURNED)
        wide_out[...] = wide

    return pl.pallas_call(
        kernel,
        out_shape=[
            shape(F32, 2 * rows, model),
            shape(B16, 2 * rows, model),
            shape(B16, RANK, 3 * ff),
            shape(F32, LANES, model),
        ],
        in_specs=[ANY] * 10 + [VMEM] * 10 + [ANY] * 8 + [VMEM] * 2,
        out_specs=[VMEM] * 4,
        scratch_shapes=[
            pltpu.VMEM((16, 2, 2, half, ff), B16),
            pltpu.VMEM((4 * rows, model), B16),
            pltpu.VMEM((4 * rows, model), B16),
            pltpu.SemaphoreType.DMA((2,)),
            pltpu.SemaphoreType.DMA((1,)),
        ],
        compiler_params=params(48),
        cost_estimate=cost(10 * rows * model * ff, 3e7),
    )(*pieces, *halves[0], *halves[1], *quarters, *upstream, picked_wide, spread_down)


def attention_grads(
    own, lambda_all, weights, qkv, raw, lse, att, low_in, low_out, branch, quarters, picked_wide, spread_in, spread_out, wide_sum, heads
):
    rows, model = quarters[0].shape
    length, width = qkv.shape
    proj, half = width // 3, weights.shape[3]

    def kernel(own_ref, lambda_ref, *refs):
        weights_hbm, branch_refs, quarter_refs = refs[0], refs[1:5], refs[5:9]
        qkv_ref, raw_ref, lse_ref, att_ref, low_ref, low_out_ref = refs[9:15]
        wide_ref, in_ref, out_ref, wide_sum_ref = refs[15:19]
        grad_ref, grad_low_ref, narrow_ref, wide_grad_ref = refs[19:23]
        w_ref, branch_ref, x_ref, graw_ref, acc_ref, sems = refs[23:]
        weight_copy = pltpu.make_async_copy(
            weights_hbm.at[:, :, :, :, pl.ds(width, proj)], w_ref, sems.at[0]
        )
        weight_copy.start()
        arriving = copy_quarters(branch_refs, branch_ref, sems.at[1])
        arriving_x = copy_quarters(quarter_refs, x_ref, sems.at[2])
        wait_all(arriving)
        grad_low_out = (ADAPTER_SCALING * product(branch_ref[...], wide_ref[...])).astype(B16)
        weight_copy.wait()
        grad_in = product(branch_ref[...], w_ref[...].reshape(model, proj)) + product(
            grad_low_out, out_ref[...]
        )
        left = dot_of(grad_low_out, att_ref[...], LEFT_TURNED)
        narrow_ref[:, width : width + proj] = left[5 * RANK : 6 * RANK].astype(B16)
        for r in range(4):
            start = pl.multiple_of((own_ref[0] ^ r) * rows, rows)
            for head in range(heads):
                columns = slice(head * 2 * HEAD_DIM, (head + 1) * 2 * HEAD_DIM)
                values = raw_ref[pl.ds(start, rows), columns]
                factor = lax.rsqrt(jnp.mean(values * values, axis=-1, keepdims=True) + NORM_EPS)
                grad = norm_backward(
                    values, factor, OUT_GAIN, grad_in[r * rows : (r + 1) * rows, columns]
                )
                graw_ref[pl.ds(start, rows), columns] = grad.astype(B16)
        for head in range(heads):
            column = head * 2 * HEAD_DIM
            value_columns = slice(2 * proj + column, 2 * proj + column + 2 * HEAD_DIM)
            key_columns = slice(proj + column, proj + column + 2 * HEAD_DIM)
            for block in reversed(range(length // BLOCK)):
                queries = slice(block * BLOCK, (block + 1) * BLOCK)
                keys = slice(0, (block + 1) * BLOCK)
                graw = graw_ref[queries, column : column + 2 * HEAD_DIM]
                probs = []
                for c in range(2):
                    scores = scores_of(qkv_ref, proj, column + c * HEAD_DIM, queries, keys)
                    probs.append(
                        jnp.exp(scores - lse_ref[head * 2 + c : head * 2 + c + 1, queries])
                    )
                lambda_one = lambda_ref[head]
                combined = (probs[0] - lambda_one * probs[1]).astype(B16)
                grad_values = product(combined, graw)
                grad_combined = dot_of(qkv_ref[keys, value_columns], graw, RIGHT_TURNED)
                grad_keys = []
                for c in range(2):
                    first = column + c * HEAD_DIM
                    weighted = probs[c] * grad_combined
                    inner = jnp.sum(weighted, axis=0, keepdims=True)
                    scale = HEAD_DIM**-0.5 if c == 0 else -lambda_one * HEAD_DIM**-0.5
                    grad_scores = ((weighted - probs[c] * inner) * scale).astype(B16)
                    grad_keys.append(
                        product(grad_scores, qkv_ref[queries, first : first + HEAD_DIM])
                    )
                    acc_ref[queries, first : first + HEAD_DIM] = dot_of(
                        grad_scores,
                        qkv_ref[keys, proj + first : proj + first + HEAD_DIM],
                        LEFT_TURNED,
                    )
                grad_key = jnp.concatenate(grad_keys, axis=1)
                if block == length // BLOCK - 1:
                    acc_ref[keys, key_columns] = grad_key
                    acc_ref[keys, value_columns] = grad_values
                else:
                    acc_ref[keys, key_columns] += grad_key
                    acc_ref[keys, value_columns] += grad_values
        for r in range(4):
            start = pl.multiple_of((own_ref[0] ^ r) * rows, rows)
            grad_ref[r * rows : (r + 1) * rows, :] = acc_ref[pl.ds(start, rows), :].astype(B16)
        grad_low_ref[...] = (
            ADAPTER_SCALING * dot_of(grad_ref[...], in_ref[...], RIGHT_TURNED)
        ).astype(B16)
        for x in range(3):
            columns = slice(x * proj, (x + 1) * proj)
            right = dot_of(low_ref[...], grad_ref[:, columns], LEFT_TURNED)
            narrow_ref[:, columns] = (
                ADAPTER_SCALING * right[x * RANK : (x + 1) * RANK]
            ).astype(B16)
        wait_all(arriving_x)
        low_half = low_out_ref[...] * jnp.asarray(ADAPTER_SCALING, B16)
        wide = (
            wide_sum_ref[...]
            + dot_of(low_half, branch_ref[...], LEFT_TURNED)
            + dot_of(grad_low_ref[...], x_ref[...], LEFT_TURNED)
        )
        for start in range(0, model, LANES):
            wide_grad_ref[start : start + LANES, :] = wide[:, start : start + LANES].T.astype(B16)

    return pl.pallas_call(
        kernel,
        out_shape=[
            shape(B16, length, width),
            shape(B16, length, LANES),
            shape(B16, RANK, width + proj),
            shape(B16, model, LANES),
        ],
        in_specs=[SMEM, SMEM] + [ANY] * 9 + [VMEM] * 10,
        out_specs=[VMEM] * 4,
        scratch_shapes=[
            pltpu.VMEM((16, 2, 2, half, proj), B16),
            pltpu.VMEM((length, model), B16),
            pltpu.VMEM((length, model), B16),
            pltpu.VMEM((length, proj), B16),
            pltpu.VMEM((length, width), F32),
            pltpu.SemaphoreType.DMA((3,)),
        ],
        compiler_params=params(52),
        cost_estimate=cost(3 * length * model * proj, 2e7),
    )(
        own,
        lambda_all,
        weights,
        *branch,
        *quarters,
        qkv,
        raw,
        lse,
        att,
        low_in,
        low_out,
        picked_wide,
        spread_in,
        spread_out,
        wide_sum,
    )


def input_part(grad, grad_low, weights, picked_wide):
    length, width = grad.shape
    rows, half, model = length // 4, weights.shape[3], picked_wide.shape[0]

    def kernel(grad_ref, grad_low_ref, weights_hbm, wide_ref, away_ref, near_ref, w_ref, sem):
        copy = pltpu.make_async_copy(weights_hbm.at[:, :, :, :, pl.ds(0, width)], w_ref, sem)
        copy.start()
        copy.wait()
        for pick, target in ((away_rows, away_ref), (near_rows, near_ref)):
            values = pick(grad_ref, rows, ALL)
            low = pick(grad_low_ref, rows, ALL)
            for start in range(0, model, CHUNK):
                blocks = slice(start // (4 * half), (start + CHUNK) // (4 * half))
                target[:, start : start + CHUNK] = (
                    dot_of(values, w_ref[blocks].reshape(CHUNK, width), RIGHT_TURNED)
                    + dot_of(low, wide_ref[start : start + CHUNK, :], RIGHT_TURNED)
                ).astype(target.dtype)

    return pl.pallas_call(
        kernel,
        out_shape=[shape(B16, 2 * rows, model), shape(F32, 2 * rows, model)],
        in_specs=[VMEM, VMEM, ANY, VMEM],
        out_specs=[VMEM, VMEM],
        scratch_shapes=[
            pltpu.VMEM((16, 2, 2, half, width), B16),
            pltpu.SemaphoreType.DMA,
        ],
        compiler_params=params(40),
        cost_estimate=cost(2 * length * model * width, 2e7),
    )(grad, grad_low, weights, picked_wide)


def adam_step(parameter, gradient, moment, variance, factor):
    clipped = gradient * factor
    moment_new = BETA_FIRST * moment + (1.0 - BETA_FIRST) * clipped
    variance_new = BETA_SECOND * variance + (1.0 - BETA_SECOND) * clipped * clipped
    moment_hat = moment_new / (1.0 - BETA_FIRST**STEP)
    variance_hat = variance_new / (1.0 - BETA_SECOND**STEP)
    updated = parameter - LEARN_RATE * (
        moment_hat / (jnp.sqrt(variance_hat) + ADAM_EPS) + WEIGHT_DECAY * parameter
    )
    return (clipped, updated, moment_new, variance_new)


def flat_rows(stacked):
    moved = stacked.astype(B16).transpose(1, 0, 2)
    return moved.reshape(stacked.shape[1], -1)


def local(
    tokens,
    cotangent,
    adapter_ids,
    norm_gains,
    lambda_vectors,
    weight_inputs,
    weight_output,
    hidden_weight_matrix,
    weight_down,
    adapter_wide,
    adapter_attention,
    adapter_feedforward,
    moment_wide,
    variance_wide,
    moment_attention,
    variance_attention,
    moment_feedforward,
    variance_feedforward,
):
    place = Place()
    adapter = adapter_ids[0]
    own_quarter = place.tensor.astype(jnp.int32).reshape(1)
    local_tokens = tokens[0].astype(F32)
    upstream_b = cotangent[0]
    gain_values = norm_gains.astype(F32)
    lambda_all = (
        jnp.exp(jnp.sum(lambda_vectors[0] * lambda_vectors[1], axis=-1))
        - jnp.exp(jnp.sum(lambda_vectors[2] * lambda_vectors[3], axis=-1))
        + LAMBDA_INIT
    )
    heads_local = lambda_vectors.shape[1]
    proj = weight_inputs.shape[2]
    ff = hidden_weight_matrix.shape[2]
    model = tokens.shape[2]

    shard = jnp.concatenate(
        [
            weight_inputs[0],
            weight_inputs[1],
            weight_inputs[2],
            weight_output.T,
            hidden_weight_matrix[0],
            hidden_weight_matrix[1],
            weight_down.T,
        ],
        axis=1,
    )
    wide_rows = adapter_wide.astype(B16).transpose(0, 2, 1).reshape(7 * RANK, LANES)
    narrow_rows = jnp.concatenate(
        [
            flat_rows(adapter_attention).reshape(-1, LANES),
            flat_rows(adapter_feedforward).reshape(-1, LANES),
        ]
    )
    attention_rows, narrow_count = 4 * 4 * proj // LANES, narrow_rows.shape[0]
    adapter_rows = jnp.concatenate([wide_rows, narrow_rows])
    adapter_rows = jnp.pad(adapter_rows, ((0, -adapter_rows.shape[0] % 16), (0, 0)))
    normed_one, scale_one = norm_forward(local_tokens, gain_values[0])
    normed_one_b = normed_one.astype(B16)

    (other, core_normed), (shard, upstream_b) = exchange(
        [(shard, PAIR_X), (normed_one_b, CORES)], shard, upstream_b
    )
    blocks = first_blocks(shard, other, place)
    sends = ring_sends(*blocks)
    (*near, far_upstream), (normed_out,) = exchange(sends + [(upstream_b, FAR_X)], normed_one_b)
    (*far, core_upstream), (normed_out, adapter_rows) = exchange(
        relay_sends(sends, near) + [(upstream_b, CORES)], normed_out, adapter_rows
    )
    attention_width = 4 * proj
    planes_one = planes(*blocks, near, far, 0, attention_width)
    sends = plane_sends(*planes_one)
    all_adapters = lax.all_to_all(
        jnp.broadcast_to(adapter_rows, (32,) + adapter_rows.shape),
        "dp",
        split_axis=0,
        concat_axis=0,
        tiled=True,
    )
    (*near_one, far_normed), (all_adapters, far_upstream, *parts) = exchange(
        sends + [(normed_out, FAR_X)], all_adapters, far_upstream, *blocks, *near, *far
    )
    planes_two = planes(*parts[:2], parts[2:6], parts[6:], attention_width, 3 * ff)

    onehot_rows = (
        jnp.arange(LANES)[None, :, None]
        == (adapter * RANK + jnp.arange(LANES) - RANK * jnp.arange(7)[:, None])[:, None, :]
    ) & (jnp.arange(LANES)[None, None, :] // RANK == jnp.arange(7)[:, None, None])
    wide_mine = (
        all_adapters[:, : 7 * RANK]
        .reshape(32, 7, RANK, LANES)
        .transpose(0, 2, 1, 3)
        .reshape(512, 7 * LANES)
    )
    picked_t = product(wide_mine, onehot_rows.astype(B16).reshape(7 * LANES, LANES)).astype(B16)
    (*far_one, picked_far), (planes_two, far_normed, far_upstream) = exchange(
        relay_sends(sends, near_one) + [(picked_t, FAR_X)], planes_two, far_normed, far_upstream
    )
    picked_all = in_place(
        [picked_t, send(picked_t, CORES), picked_far, send(picked_far, CORES)], place
    ).reshape(4, 32, 16, LANES)
    picked_wide = picked_all.transpose(1, 0, 2, 3).reshape(model, LANES)
    mine = lax.dynamic_slice_in_dim(all_adapters, adapter * 4, 4, 0)
    mine = mine[:, 7 * RANK : 7 * RANK + narrow_count]
    picked_rows = jnp.concatenate(
        [
            mine[:, :attention_rows].reshape(RANK, 4 * proj),
            mine[:, attention_rows:].reshape(RANK, 3 * ff),
        ],
        axis=1,
    )
    slots = jnp.concatenate(
        [jnp.full((w,), x, jnp.int32) for x, w in zip((0, 1, 2, 5, 3, 4, 6), [proj] * 4 + [ff] * 3)]
    )
    spread = jnp.where(
        slots[None, :] == jnp.arange(LANES)[:, None] // RANK,
        jnp.concatenate([picked_rows] * 8, axis=0),
        0,
    ).astype(B16)
    spread_in, spread_out = spread[:, : 3 * proj], spread[:, 3 * proj : 4 * proj]
    spread_hidden = spread[:, 4 * proj : 4 * proj + 2 * ff]
    spread_down = spread[:, 4 * proj + 2 * ff :]

    seq_normed_one = [normed_one_b, core_normed, far_normed, send(far_normed, CORES)]
    seq_upstream = [upstream_b, core_upstream, far_upstream, send(far_upstream, CORES)]
    w_attention, attention_b, raw, lse, qkv, low_in, low_out, away, near_sum = attention_part(
        own_quarter,
        lambda_all,
        pieces_of(planes_one, near_one, far_one),
        seq_normed_one,
        picked_wide,
        spread_in,
        spread_out,
        heads_local,
    )
    sends = plane_sends(*planes_two)
    near_two, (away, near_sum) = exchange(sends, away, near_sum)
    far_two, _ = exchange(relay_sends(sends, near_two))
    pieces_two = pieces_of(planes_two, near_two, far_two)
    staying, leaving = core_sum(near_sum, away)
    residual_one = local_tokens + staying + send(leaving, FAR_X).astype(F32)

    second_normalized, scale_two = norm_forward(residual_one, gain_values[1])
    normed_two_b = second_normalized.astype(B16)
    core_two, far_two_tokens = send(normed_two_b, CORES), send(normed_two_b, FAR_X)
    near_half = hidden_part(
        pieces_two,
        [normed_two_b, core_two],
        seq_upstream[:2],
        picked_wide,
        spread_hidden,
        spread_down,
    )
    far_two_tokens, *near_half = together(far_two_tokens, *near_half)
    seq_normed_two = [normed_two_b, core_two, far_two_tokens, send(far_two_tokens, CORES)]
    far_half = hidden_part(
        pieces_two,
        seq_normed_two[2:],
        seq_upstream[2:],
        picked_wide,
        spread_hidden,
        spread_down,
    )
    leaving = (far_half[5] + send(far_half[6], CORES).astype(F32)).astype(B16)
    leaving, *half_values = together(leaving, *near_half[:5], *far_half[:5])
    near_down, away_down, narrow_two, wide_two = down_part(
        pieces_two,
        (half_values[:5], half_values[5:]),
        seq_normed_two,
        seq_upstream,
        picked_wide,
        spread_down,
    )
    arrived, near_down, away_down = together(send(leaving, FAR_X), near_down, away_down)
    grad_normed_two = (
        near_half[5] + send(near_half[6], CORES).astype(F32) + arrived.astype(F32)
    )
    grad_residual = upstream_b.astype(F32) + norm_backward(
        residual_one, scale_two, gain_values[1], grad_normed_two
    )
    grad_branch_b = grad_residual.astype(B16)
    down_staying, down_leaving = core_sum(near_down, away_down)
    far_branch, down_leaving = together(send(grad_branch_b, FAR_X), down_leaving)
    seq_grad_branch = [
        grad_branch_b,
        send(grad_branch_b, CORES),
        far_branch,
        send(far_branch, CORES),
    ]

    grad_projected, grad_low_in, narrow_one, wide_grads = attention_grads(
        own_quarter,
        lambda_all,
        w_attention,
        qkv,
        raw,
        lse,
        attention_b,
        low_in,
        low_out,
        seq_grad_branch,
        seq_normed_one,
        picked_wide,
        spread_in,
        spread_out,
        wide_two,
        heads_local,
    )
    down_arrived, narrow_one, wide_grads = together(
        send(down_leaving, FAR_X), narrow_one, wide_grads
    )
    result = residual_one + down_staying + down_arrived.astype(F32)
    away, near_sum = input_part(grad_projected, grad_low_in, w_attention, picked_wide)

    split_grads = jnp.concatenate([narrow_one, narrow_two], axis=1)
    columns = split_grads.shape[1]
    piece = -(-columns // 1024) * 128
    split_blocks = (
        jnp.pad(split_grads, ((0, 0), (0, 8 * piece - columns)))
        .reshape(4, 4, 2, 4, piece)
        .transpose(1, 2, 0, 3, 4)
        .reshape(128, piece // 128, 128)
    )
    blocks = jnp.concatenate(
        [
            wide_grads.reshape(128, 16, 128),
            split_blocks,
            jnp.broadcast_to(adapter.astype(B16), (128, 8 - piece // 128, 128)),
        ],
        axis=1,
    )
    arrived, away, near_sum = together(
        lax.all_to_all(blocks, AXES, split_axis=0, concat_axis=0, tiled=True), away, near_sum
    )
    staying, leaving = core_sum(near_sum, away)
    ids_all = arrived.reshape(32, 4, 24, 128)[:, 0, 23, 0].astype(jnp.int32)
    member = ids_all[None, :] == jnp.arange(ADAPTERS)[:, None]
    onehot = member.astype(B16)
    wide_sum = contract(
        "es,sn->en",
        onehot,
        arrived[:, :16].reshape(32, 4 * 16 * 128),
    ).reshape(8, 4, 16, 128).sum(1)
    split_sum = contract(
        "es,sn->en", onehot, arrived[:, 16:].reshape(32, 4 * 8 * 128)
    ).reshape(8, 4, 8, 128)[:, :, : piece // 128]
    squares = jnp.sum(wide_sum * wide_sum) + jnp.sum(split_sum * split_sum)
    grads_wide = (
        wide_sum[:, :, :112].reshape(8, 16, 7, 16).transpose(2, 0, 3, 1).reshape(7, 128, 16)
    )
    mine = place.dp % 4
    split_out = jnp.concatenate(
        [split_sum.reshape(32, 7, 128), jnp.zeros((32, 1, 128), F32)], axis=1
    ).reshape(8, 1, 4, 8, 128)
    quarter = jnp.arange(4)[None, :, None, None, None]
    spread = jnp.where(quarter == mine, split_out, 0.0).reshape(128, 8, 128)
    spread = jnp.where(jnp.arange(8)[None, :, None] == 7, squares, spread)
    leaving, spread = together(leaving, spread)
    input_arrived, placed = together(
        send(leaving, FAR_X),
        lax.all_to_all(spread, AXES, split_axis=0, concat_axis=0, tiled=True),
    )
    grad_normed_one = staying + input_arrived.astype(F32)
    grad_input = grad_residual + norm_backward(
        local_tokens, scale_one, gain_values[0], grad_normed_one
    )
    total_squares = jnp.sum(placed[:, 7, 0])
    from_mine = lax.dynamic_index_in_dim(
        placed.reshape(8, 4, 4, 8, 128), mine, 1, keepdims=False
    )
    split_rows = from_mine[:, :, :7].reshape(4, 8 * piece)[:, :columns]
    grads_attention = split_rows[:, : 4 * proj].reshape(4, 4, proj).transpose(1, 0, 2)
    grads_feedforward = split_rows[:, 4 * proj :].reshape(4, 3, ff).transpose(1, 0, 2)

    grad_norm = jnp.sqrt(total_squares)
    factor = CLIP_NORM / (grad_norm + 1e-06)
    wide_new = adam_step(adapter_wide, grads_wide, moment_wide, variance_wide, factor)
    attention_new = adam_step(
        adapter_attention, grads_attention, moment_attention, variance_attention, factor
    )
    feedforward_new = adam_step(
        adapter_feedforward, grads_feedforward, moment_feedforward, variance_feedforward, factor
    )
    return (
        result.astype(B16)[None],
        grad_input.astype(B16)[None],
        grad_norm,
        wide_new[0],
        attention_new[0],
        feedforward_new[0],
        wide_new[1],
        attention_new[1],
        feedforward_new[1],
        wide_new[2],
        attention_new[2],
        feedforward_new[2],
        wide_new[3],
        attention_new[3],
        feedforward_new[3],
    )


def solution(mesh):
    return jax.shard_map(
        local,
        mesh=mesh,
        in_specs=(
            P("dp", "tensor", None),
            P("dp", "tensor", None),
            P("dp"),
            P(),
            P(None, "tensor", None),
            P(None, "dp", "tensor"),
            P("tensor", "dp"),
            P(None, "dp", "tensor"),
            P("tensor", "dp"),
            P(None, None, ("dp", "tensor")),
            P(None, "dp", "tensor"),
            P(None, "dp", "tensor"),
            P(None, None, ("dp", "tensor")),
            P(None, None, ("dp", "tensor")),
            P(None, "dp", "tensor"),
            P(None, "dp", "tensor"),
            P(None, "dp", "tensor"),
            P(None, "dp", "tensor"),
        ),
        out_specs=(
            P("dp", "tensor", None),
            P("dp", "tensor", None),
            P(),
            P(None, None, ("dp", "tensor")),
            P(None, "dp", "tensor"),
            P(None, "dp", "tensor"),
            P(None, None, ("dp", "tensor")),
            P(None, "dp", "tensor"),
            P(None, "dp", "tensor"),
            P(None, None, ("dp", "tensor")),
            P(None, "dp", "tensor"),
            P(None, "dp", "tensor"),
            P(None, None, ("dp", "tensor")),
            P(None, "dp", "tensor"),
            P(None, "dp", "tensor"),
        ),
        check_vma=False,
    )
```

```python
import jax
import jax.numpy as jnp
from jax import lax
from jax.experimental import pallas as pl
from jax.experimental.pallas import tpu as pltpu
from jax.sharding import PartitionSpec as P

HEAD_DIM = 128
ADAPTERS = 8
RANK = 16
BLOCK = 256
STEP = 10


NORM_EPS = 1e-05
ADAPTER_SCALING = 0.5
LAMBDA_INIT = 0.2
OUT_GAIN = 0.8
CLIP_NORM = 1.0
LEARN_RATE = 0.05
BETA_FIRST = 0.9
BETA_SECOND = 0.999
ADAM_EPS = 1e-08
WEIGHT_DECAY = 0.01
NEG_LARGE = -1e30
AXES = ("dp", "tensor")
B16 = jnp.bfloat16
F32 = jnp.float32


def product(left, right):
    return jnp.dot(left, right, preferred_element_type=F32)


def contract(form, left, right):
    return jnp.einsum(form, left, right, preferred_element_type=F32)


def index_of(z, y, x, core):
    x, y, z, core = x % 4, y % 4, z % 4, core % 2
    return ((z * 4 + y) * 2 + x % 2) * 4 + (x // 2) * 2 + core


def routes(move):
    pairs = []
    for z in range(4):
        for y in range(4):
            for x in range(4):
                for core in range(2):
                    pairs.append((index_of(z, y, x, core), index_of(*move(z, y, x, core))))
    return pairs


UP_Z = routes(lambda z, y, x, c: (z + 1, y, x, c))
DOWN_Z = routes(lambda z, y, x, c: (z - 1, y, x, c))
FAR_Z = routes(lambda z, y, x, c: (z + 2, y, x, c))
UP_Y = routes(lambda z, y, x, c: (z, y + 1, x, c))
DOWN_Y = routes(lambda z, y, x, c: (z, y - 1, x, c))
FAR_Y = routes(lambda z, y, x, c: (z, y + 2, x, c))
PAIR_X = routes(lambda z, y, x, c: (z, y, x ^ 1, c))
FAR_X = routes(lambda z, y, x, c: (z, y, x + 2, c))
CORES = routes(lambda z, y, x, c: (z, y, x, 1 - c))


def send(values, pairs):
    return lax.ppermute(values, AXES, pairs)


class Place:
    def __init__(self):
        tensor = lax.axis_index("tensor")
        self.far, self.core, self.tensor = tensor // 2, tensor % 2, tensor
        self.dp = lax.axis_index("dp")


def together(*values):
    return lax.optimization_barrier(values)


OFFSETS = (0, 3, 1, 2)
LANES = 128
CHUNK = 512


def copy_pieces(pieces, held, sems, groups):
    sources = (pieces[:5], pieces[5:10])
    dp = lax.axis_index("dp")
    at = (dp // 8, (dp // 2) & 3)
    started = []
    for i, (start, width) in enumerate(groups):
        columns = pl.ds(start, width)
        copies = []
        for order in range(2):
            for outer in range(4):
                for block in range(4):
                    places = [0, 0]
                    places[order] = (at[order] + OFFSETS[outer]) & 3
                    places[1 - order] = (at[1 - order] + OFFSETS[block]) & 3
                    if outer < 3:
                        source = sources[order][outer].at[pl.ds(2 * block, 2), :, columns]
                    else:
                        part = sources[order][3 + block // 2]
                        source = part.at[pl.ds(2 * (block % 2), 2), :, columns]
                    copy = pltpu.make_async_copy(
                        source, held.at[places[0] * 4 + places[1], :, order, :, columns], sems.at[i]
                    )
                    copy.start()
                    copies.append(copy)
        started.append(copies)
    return started


def copy_quarters(quarters, held, sem):
    rows = quarters[0].shape[0]
    copies = [
        pltpu.make_async_copy(quarter, held.at[pl.ds(i * rows, rows), :], sem)
        for i, quarter in enumerate(quarters)
    ]
    for copy in copies:
        copy.start()
    return copies


def wait_all(copies):
    for copy in copies:
        copy.wait()


def first_blocks(shard, other, place):
    half = shard.shape[0] // 2
    swap = place.dp % 2 == 1
    low, high = jnp.where(swap, other, shard), jnp.where(swap, shard, other)
    return (jnp.stack([low[:half], high[:half]]), jnp.stack([low[half:], high[half:]]))


def ring_sends(part_a, part_b):
    return [(part_a, UP_Y), (part_a, DOWN_Y), (part_b, UP_Z), (part_b, DOWN_Z)]


def plane_sends(part_a, part_b):
    return [(part_a, UP_Z), (part_a, DOWN_Z), (part_b, UP_Y), (part_b, DOWN_Y)]


def relay_sends(sends, arrived):
    out = []
    for i, (_, pairs) in enumerate(sends):
        middle = arrived[i].shape[0] // 2
        out.append((arrived[i][:middle] if i % 2 == 0 else arrived[i][middle:], pairs))
    return out


def planes(part_a, part_b, near, far, start, width):
    cut = lambda v: v[..., start : start + width]
    return (
        jnp.concatenate([cut(v) for v in (part_a, near[0], near[1], far[0], far[1])], axis=0),
        jnp.concatenate([cut(v) for v in (part_b, near[2], near[3], far[2], far[3])], axis=0),
    )


def pieces_of(plane_pair, near, far):
    return (
        plane_pair[0],
        near[0],
        near[1],
        far[0],
        far[1],
        plane_pair[1],
        near[2],
        near[3],
        far[2],
        far[3],
    )


def exchange(sends, *others):
    results = [send(values, pairs) for values, pairs in sends]
    out = together(*results, *others)
    return list(out[: len(sends)]), list(out[len(sends) :])


def in_place(values, place):
    own, core, far, far_core = values
    swap_core, swap_far = place.core == 1, place.far == 1
    near = jnp.stack([jnp.where(swap_core, core, own), jnp.where(swap_core, own, core)])
    away = jnp.stack([jnp.where(swap_core, far_core, far), jnp.where(swap_core, far, far_core)])
    return jnp.concatenate(
        [jnp.where(swap_far, away, near), jnp.where(swap_far, near, away)], axis=0
    )


def core_sum(near, away):
    rows = near.shape[0] // 2
    arrived = send(away, CORES)
    staying = near[:rows] + arrived[:rows].astype(F32)
    return staying, (near[rows:] + arrived[rows:].astype(F32)).astype(B16)


def norm_forward(values, gain_value):
    factor = lax.rsqrt(jnp.mean(values * values, axis=-1, keepdims=True) + NORM_EPS)
    return (values * factor * gain_value, factor)


def norm_backward(values, factor, gain_value, gradient):
    scaled = gradient * gain_value
    return factor * (
        scaled - values * factor * factor * jnp.mean(scaled * values, axis=-1, keepdims=True)
    )


RIGHT_TURNED = (((1,), (1,)), ((), ()))
LEFT_TURNED = (((0,), (0,)), ((), ()))


def dot_of(left, right, dims):
    return lax.dot_general(left, right, dims, preferred_element_type=F32)


def away_rows(ref, rows, columns):
    return jnp.concatenate([ref[rows : 2 * rows, columns], ref[3 * rows : 4 * rows, columns]])


def near_rows(ref, rows, columns):
    return jnp.concatenate([ref[0:rows, columns], ref[2 * rows : 3 * rows, columns]])


ALL = slice(None)
VMEM = pl.BlockSpec(memory_space=pltpu.VMEM)
SMEM = pl.BlockSpec(memory_space=pltpu.SMEM)
ANY = pl.BlockSpec(memory_space=pl.ANY)


def shape(dtype, *dims):
    return jax.ShapeDtypeStruct(dims, dtype)


def params(mib):
    return pltpu.CompilerParams(vmem_limit_bytes=mib * 2**20)


def cost(flops, size):
    return pl.CostEstimate(flops=int(flops), bytes_accessed=int(size), transcendentals=0)


def scores_of(qkv_ref, proj, first, queries, keys):
    return (
        dot_of(
            qkv_ref[keys, proj + first : proj + first + HEAD_DIM],
            qkv_ref[queries, first : first + HEAD_DIM],
            RIGHT_TURNED,
        )
        * HEAD_DIM**-0.5
    )


def projection_part(own, pieces, quarters, picked_wide, spread_in):
    rows, model = quarters[0].shape
    length, half, total = 4 * rows, pieces[0].shape[1], pieces[0].shape[2]
    width = spread_in.shape[1]
    proj = width // 3

    def kernel(own_ref, *refs):
        piece_refs, quarter_refs = refs[:10], refs[10:14]
        wide_ref, in_ref, w_out, qkv_ref, low_ref = refs[14:19]
        held, x_ref, sems, x_sem, out_sem = refs[19:]
        arriving = copy_quarters(quarter_refs, x_ref, x_sem)
        groups = copy_pieces(piece_refs, held, sems, [(0, width), (width, total - width)])
        wait_all(arriving)
        low_ref[...] = product(x_ref[...], wide_ref[...]).astype(B16)
        low_half = low_ref[...] * jnp.asarray(ADAPTER_SCALING, B16)
        wait_all(groups[0])
        for i in range(3):
            columns = slice(i * proj, (i + 1) * proj)
            weights = held[:, :, :, :, columns].reshape(model, proj)
            for f in range(2):
                part = slice(2 * f * rows, 2 * (f + 1) * rows)
                values = product(x_ref[part, :], weights) + product(
                    low_half[part], in_ref[:, columns]
                )
                for k in range(2):
                    start = pl.multiple_of((own_ref[0] ^ (2 * f + k)) * rows, rows)
                    qkv_ref[pl.ds(start, rows), columns] = values[
                        k * rows : (k + 1) * rows
                    ].astype(B16)
            if i == 0:
                wait_all(groups[1])
                leaving = pltpu.make_async_copy(held, w_out, out_sem)
                leaving.start()
        leaving.wait()

    return pl.pallas_call(
        kernel,
        out_shape=[
            shape(B16, 16, 2, 2, half, total),
            shape(B16, length, width),
            shape(B16, length, LANES),
        ],
        in_specs=[SMEM] + [ANY] * 14 + [VMEM] * 2,
        out_specs=[ANY] + [VMEM] * 2,
        scratch_shapes=[
            pltpu.VMEM((16, 2, 2, half, total), B16),
            pltpu.VMEM((length, model), B16),
            pltpu.SemaphoreType.DMA((2,)),
            pltpu.SemaphoreType.DMA,
            pltpu.SemaphoreType.DMA,
        ],
        compiler_params=params(32),
        cost_estimate=cost(2 * length * model * total, 2.4e7),
    )(own, *pieces, *quarters, picked_wide, spread_in)


def attention_part(own, lambda_all, weights, qkv, picked_wide, spread_out, heads):
    length, width = qkv.shape
    proj, half, model = width // 3, weights.shape[3], picked_wide.shape[0]
    rows = length // 4

    def kernel(own_ref, lambda_ref, weights_hbm, qkv_ref, wide_ref, out_ref, *refs):
        att_ref, raw_out, lse_ref, low_out_ref, away_out, near_out = refs[:6]
        held, raw_ref, away_ref, near_ref, w_sem, raw_sem, sems = refs[6:]
        weight_copy = pltpu.make_async_copy(
            weights_hbm.at[:, :, :, :, pl.ds(width, proj)], held, w_sem
        )
        weight_copy.start()
        for head in range(heads):
            column = head * 2 * HEAD_DIM
            value_columns = slice(2 * proj + column, 2 * proj + column + 2 * HEAD_DIM)
            for block in range(length // BLOCK):
                queries = slice(block * BLOCK, (block + 1) * BLOCK)
                keys = slice(0, (block + 1) * BLOCK)
                parts = []
                for c in range(2):
                    scores = scores_of(qkv_ref, proj, column + c * HEAD_DIM, queries, keys)
                    top = jnp.max(scores, axis=0, keepdims=True)
                    shifted = jnp.exp(scores - top)
                    total_sum = jnp.sum(shifted, axis=0, keepdims=True)
                    lse_ref[head * 2 + c : head * 2 + c + 1, queries] = top + jnp.log(total_sum)
                    parts.append(shifted * (1.0 / total_sum))
                combined = (parts[0] - lambda_ref[head] * parts[1]).astype(B16)
                raw = dot_of(combined, qkv_ref[keys, value_columns], LEFT_TURNED)
                raw_ref[queries, column : column + 2 * HEAD_DIM] = raw
        raw_copy = pltpu.make_async_copy(raw_ref, raw_out, raw_sem)
        raw_copy.start()
        for t in range(4):
            start = pl.multiple_of((own_ref[0] ^ t) * rows, rows)
            for head in range(heads):
                columns = slice(head * 2 * HEAD_DIM, (head + 1) * 2 * HEAD_DIM)
                raw = raw_ref[t * rows : (t + 1) * rows, columns]
                factor = lax.rsqrt(jnp.mean(raw * raw, axis=-1, keepdims=True) + NORM_EPS)
                att_ref[pl.ds(start, rows), columns] = (raw * factor * OUT_GAIN).astype(B16)
        low_out_ref[...] = dot_of(att_ref[...], out_ref[...], RIGHT_TURNED).astype(B16)
        weight_copy.wait()
        leaving = [raw_copy]
        for i, (pick, target, out) in enumerate(
            ((away_rows, away_ref, away_out), (near_rows, near_ref, near_out))
        ):
            values = pick(att_ref, rows, ALL)
            low = pick(low_out_ref, rows, ALL) * jnp.asarray(ADAPTER_SCALING, B16)
            for start in range(0, model, CHUNK):
                blocks = slice(start // (4 * half), (start + CHUNK) // (4 * half))
                target[:, start : start + CHUNK] = (
                    dot_of(values, held[blocks].reshape(CHUNK, proj), RIGHT_TURNED)
                    + dot_of(low, wide_ref[start : start + CHUNK, :], RIGHT_TURNED)
                ).astype(target.dtype)
            copy = pltpu.make_async_copy(target, out, sems.at[i])
            copy.start()
            leaving.append(copy)
        wait_all(leaving)

    return pl.pallas_call(
        kernel,
        out_shape=[
            shape(B16, length, proj),
            shape(F32, length, proj),
            shape(F32, 2 * heads, length),
            shape(B16, length, LANES),
            shape(B16, 2 * rows, model),
            shape(F32, 2 * rows, model),
        ],
        in_specs=[SMEM, SMEM, ANY] + [VMEM] * 3,
        out_specs=[VMEM, ANY, VMEM, VMEM, ANY, ANY],
        scratch_shapes=[
            pltpu.VMEM((16, 2, 2, half, proj), B16),
            pltpu.VMEM((length, proj), F32),
            pltpu.VMEM((2 * rows, model), B16),
            pltpu.VMEM((2 * rows, model), F32),
            pltpu.SemaphoreType.DMA,
            pltpu.SemaphoreType.DMA,
            pltpu.SemaphoreType.DMA((2,)),
        ],
        compiler_params=params(32),
        cost_estimate=cost(2 * length * model * proj + 4 * length * length * proj, 2e7),
    )(own, lambda_all, weights, qkv, picked_wide, spread_out)


def hidden_grad(w_down, upstream, picked_wide, spread_down):
    rows, model = upstream[0].shape
    length, ff = 4 * rows, spread_down.shape[1]

    def kernel(*refs):
        down_hbm, upstream_refs = refs[0], refs[1:5]
        wide_ref, down_spread, grad_low_ref, grad_ref, down_ref, up_ref, sems = refs[5:]
        down_copy = pltpu.make_async_copy(down_hbm.at[:, pl.ds(0, ff)], down_ref, sems.at[1])
        arriving = copy_quarters(upstream_refs, up_ref, sems.at[0])
        down_copy.start()
        wait_all(arriving)
        grad_low_ref[...] = (ADAPTER_SCALING * product(up_ref[...], wide_ref[...])).astype(B16)
        down_copy.wait()
        for start in range(0, ff, CHUNK):
            columns = slice(start, min(start + CHUNK, ff))
            grad_ref[:, columns] = (
                product(up_ref[...], down_ref[:, columns])
                + product(grad_low_ref[...], down_spread[:, columns])
            ).astype(B16)

    return pl.pallas_call(
        kernel,
        out_shape=[shape(B16, length, LANES), shape(B16, length, ff)],
        in_specs=[ANY] * 5 + [VMEM] * 2,
        out_specs=[VMEM] * 2,
        scratch_shapes=[
            pltpu.VMEM((model, ff), B16),
            pltpu.VMEM((length, model), B16),
            pltpu.SemaphoreType.DMA((2,)),
        ],
        compiler_params=params(32),
        cost_estimate=cost(2 * length * model * ff, 1.5e7),
    )(w_down, *upstream, picked_wide, spread_down)


def hidden_part(pieces, grad_hidden, quarters, picked_wide, spread_hidden):
    rows, model = quarters[0].shape
    length, half, total = 4 * rows, pieces[0].shape[1], pieces[0].shape[2]
    ff = total // 2
    tiles = [(s, min(CHUNK, ff - s)) for s in range(0, ff, CHUNK)]

    def kernel(*refs):
        piece_refs, quarter_refs = refs[:10], refs[10:14]
        grad_hidden_ref, wide_ref, hidden_spread = refs[14:17]
        hidden_out, grad_out, low_ref, grad_low_ref, away_out, near_out = refs[17:23]
        hidden_ref, grad_ref, away_ref, near_ref, held, x_ref, sems, x_sem, out_sems = refs[23:]
        arriving = copy_quarters(quarter_refs, x_ref, x_sem)
        groups = copy_pieces(piece_refs, held, sems, [(0, ff), (ff, ff)])
        wait_all(arriving)
        low_ref[...] = product(x_ref[...], wide_ref[...]).astype(B16)
        low_half = low_ref[...] * jnp.asarray(ADAPTER_SCALING, B16)
        for i, (s, w) in enumerate(tiles):
            columns = slice(s, s + w)
            up_columns = slice(ff + s, ff + s + w)
            grad_hidden = grad_hidden_ref[:, columns].astype(F32)
            if i == 0:
                wait_all(groups[0])
            gate = product(
                x_ref[...], held[:, :, :, :, columns].reshape(model, w)
            ) + product(low_half, hidden_spread[:, columns])
            if i == 0:
                wait_all(groups[1])
            upper = product(
                x_ref[...], held[:, :, :, :, up_columns].reshape(model, w)
            ) + product(low_half, hidden_spread[:, up_columns])
            sigmoid_gate = 1.0 / (1.0 + jnp.exp(-gate))
            swish = gate * sigmoid_gate
            hidden_ref[:, columns] = (swish * upper).astype(B16)
            grad_ref[:, columns] = (
                grad_hidden * upper * (sigmoid_gate + swish * (1.0 - sigmoid_gate))
            ).astype(B16)
            grad_ref[:, up_columns] = (grad_hidden * swish).astype(B16)
        leaving = [
            pltpu.make_async_copy(hidden_ref, hidden_out, out_sems.at[0]),
            pltpu.make_async_copy(grad_ref, grad_out, out_sems.at[1]),
        ]
        for copy in leaving:
            copy.start()
        grad_low_ref[...] = (
            ADAPTER_SCALING * dot_of(grad_ref[...], hidden_spread[...], RIGHT_TURNED)
        ).astype(B16)
        for i, (pick, target, out) in enumerate(
            ((away_rows, away_ref, away_out), (near_rows, near_ref, near_out))
        ):
            values = pick(grad_ref, rows, ALL)
            low = pick(grad_low_ref, rows, ALL)
            for start in range(0, model, CHUNK):
                blocks = slice(start // (4 * half), (start + CHUNK) // (4 * half))
                weights = held[blocks].reshape(CHUNK, total)
                target[:, start : start + CHUNK] = (
                    dot_of(values, weights, RIGHT_TURNED)
                    + dot_of(low, wide_ref[start : start + CHUNK, :], RIGHT_TURNED)
                ).astype(target.dtype)
            copy = pltpu.make_async_copy(target, out, out_sems.at[2 + i])
            copy.start()
            leaving.append(copy)
        wait_all(leaving)

    return pl.pallas_call(
        kernel,
        out_shape=[
            shape(B16, length, ff),
            shape(B16, length, total),
            shape(B16, length, LANES),
            shape(B16, length, LANES),
            shape(B16, 2 * rows, model),
            shape(F32, 2 * rows, model),
        ],
        in_specs=[ANY] * 14 + [VMEM] * 3,
        out_specs=[ANY, ANY, VMEM, VMEM, ANY, ANY],
        scratch_shapes=[
            pltpu.VMEM((length, ff), B16),
            pltpu.VMEM((length, total), B16),
            pltpu.VMEM((2 * rows, model), B16),
            pltpu.VMEM((2 * rows, model), F32),
            pltpu.VMEM((16, 2, 2, half, total), B16),
            pltpu.VMEM((length, model), B16),
            pltpu.SemaphoreType.DMA((2,)),
            pltpu.SemaphoreType.DMA,
            pltpu.SemaphoreType.DMA((4,)),
        ],
        compiler_params=params(56),
        cost_estimate=cost(8 * length * model * ff, 3e7),
    )(*pieces, *quarters, grad_hidden, picked_wide, spread_hidden)


def down_part(hidden, grad, low, grad_low_down, grad_low, w_down, quarters, upstream, picked_wide, spread_down):
    rows, model = quarters[0].shape
    length, ff = hidden.shape

    def kernel(*refs):
        hidden_ref, grad_ref, low_ref, grad_low_down, grad_low_ref, down_hbm = refs[:6]
        quarter_refs, upstream_refs = refs[6:10], refs[10:14]
        wide_ref, down_spread = refs[14:16]
        away_ref, near_ref, narrow_ref, wide_out = refs[16:20]
        down_ref, x_ref, up_ref, sems = refs[20:]
        down_copy = pltpu.make_async_copy(down_hbm.at[:, pl.ds(0, ff)], down_ref, sems.at[2])
        down_copy.start()
        arriving = [
            copy_quarters(upstream_refs, up_ref, sems.at[0]),
            copy_quarters(quarter_refs, x_ref, sems.at[1]),
        ]
        low_down = dot_of(hidden_ref[...], down_spread[...], RIGHT_TURNED).astype(B16)
        low_half = low_down * jnp.asarray(ADAPTER_SCALING, B16)
        down_copy.wait()
        for first, target in ((1, away_ref), (0, near_ref)):
            pick = away_rows if first else near_rows
            values = pick(hidden_ref, rows, ALL)
            scaled = jnp.concatenate(
                [
                    low_half[first * rows : (first + 1) * rows],
                    low_half[(first + 2) * rows : (first + 3) * rows],
                ]
            )
            for start in range(0, model, CHUNK):
                target[:, start : start + CHUNK] = (
                    dot_of(values, down_ref[start : start + CHUNK, :], RIGHT_TURNED)
                    + dot_of(scaled, wide_ref[start : start + CHUNK, :], RIGHT_TURNED)
                ).astype(target.dtype)
        for x in range(2):
            right = dot_of(low_ref[...], grad_ref[:, x * ff : (x + 1) * ff], LEFT_TURNED)
            narrow_ref[:, x * ff : (x + 1) * ff] = (
                ADAPTER_SCALING * right[(3 + x) * RANK : (4 + x) * RANK]
            ).astype(B16)
        left = dot_of(grad_low_down[...], hidden_ref[...], LEFT_TURNED)
        narrow_ref[:, 2 * ff : 3 * ff] = left[6 * RANK : 7 * RANK].astype(B16)
        wait_all(arriving[0])
        wait_all(arriving[1])
        wide_out[...] = dot_of(low_half, up_ref[...], LEFT_TURNED) + dot_of(
            grad_low_ref[...], x_ref[...], LEFT_TURNED
        )

    return pl.pallas_call(
        kernel,
        out_shape=[
            shape(B16, 2 * rows, model),
            shape(F32, 2 * rows, model),
            shape(B16, RANK, 3 * ff),
            shape(F32, LANES, model),
        ],
        in_specs=[VMEM] * 5 + [ANY] * 9 + [VMEM] * 2,
        out_specs=[VMEM] * 4,
        scratch_shapes=[
            pltpu.VMEM((model, ff), B16),
            pltpu.VMEM((length, model), B16),
            pltpu.VMEM((length, model), B16),
            pltpu.SemaphoreType.DMA((3,)),
        ],
        compiler_params=params(48),
        cost_estimate=cost(2.6 * length * model * ff, 3e7),
    )(hidden, grad, low, grad_low_down, grad_low, w_down, *quarters, *upstream, picked_wide, spread_down)


def attention_grads(
    own, lambda_all, weights, qkv, raw, lse, att, low_in, low_out, branch, quarters, picked_wide, spread_in, spread_out, wide_sum, heads
):
    rows, model = quarters[0].shape
    length, width = qkv.shape
    proj, half = width // 3, weights.shape[3]

    def kernel(own_ref, lambda_ref, *refs):
        weights_hbm, branch_refs, quarter_refs = refs[0], refs[1:5], refs[5:9]
        qkv_ref, raw_ref, lse_ref, att_ref, low_ref, low_out_ref = refs[9:15]
        wide_ref, in_ref, out_ref, wide_sum_ref = refs[15:19]
        grad_ref, grad_low_ref, narrow_ref, wide_grad_ref = refs[19:23]
        w_ref, branch_ref, x_ref, graw_ref, acc_ref, sems = refs[23:]
        weight_copy = pltpu.make_async_copy(
            weights_hbm.at[:, :, :, :, pl.ds(width, proj)], w_ref, sems.at[0]
        )
        weight_copy.start()
        arriving = copy_quarters(branch_refs, branch_ref, sems.at[1])
        arriving_x = copy_quarters(quarter_refs, x_ref, sems.at[2])
        wait_all(arriving)
        grad_low_out = (ADAPTER_SCALING * product(branch_ref[...], wide_ref[...])).astype(B16)
        weight_copy.wait()
        grad_in = product(branch_ref[...], w_ref[...].reshape(model, proj)) + product(
            grad_low_out, out_ref[...]
        )
        left = dot_of(grad_low_out, att_ref[...], LEFT_TURNED)
        narrow_ref[:, width : width + proj] = left[5 * RANK : 6 * RANK].astype(B16)
        for r in range(4):
            start = pl.multiple_of((own_ref[0] ^ r) * rows, rows)
            for head in range(heads):
                columns = slice(head * 2 * HEAD_DIM, (head + 1) * 2 * HEAD_DIM)
                values = raw_ref[pl.ds(start, rows), columns]
                factor = lax.rsqrt(jnp.mean(values * values, axis=-1, keepdims=True) + NORM_EPS)
                grad = norm_backward(
                    values, factor, OUT_GAIN, grad_in[r * rows : (r + 1) * rows, columns]
                )
                graw_ref[pl.ds(start, rows), columns] = grad.astype(B16)
        for head in range(heads):
            column = head * 2 * HEAD_DIM
            value_columns = slice(2 * proj + column, 2 * proj + column + 2 * HEAD_DIM)
            key_columns = slice(proj + column, proj + column + 2 * HEAD_DIM)
            for block in reversed(range(length // BLOCK)):
                queries = slice(block * BLOCK, (block + 1) * BLOCK)
                keys = slice(0, (block + 1) * BLOCK)
                graw = graw_ref[queries, column : column + 2 * HEAD_DIM]
                probs = []
                for c in range(2):
                    scores = scores_of(qkv_ref, proj, column + c * HEAD_DIM, queries, keys)
                    probs.append(
                        jnp.exp(scores - lse_ref[head * 2 + c : head * 2 + c + 1, queries])
                    )
                lambda_one = lambda_ref[head]
                combined = (probs[0] - lambda_one * probs[1]).astype(B16)
                grad_values = product(combined, graw)
                grad_combined = dot_of(qkv_ref[keys, value_columns], graw, RIGHT_TURNED)
                grad_keys = []
                for c in range(2):
                    first = column + c * HEAD_DIM
                    weighted = probs[c] * grad_combined
                    inner = jnp.sum(weighted, axis=0, keepdims=True)
                    scale = HEAD_DIM**-0.5 if c == 0 else -lambda_one * HEAD_DIM**-0.5
                    grad_scores = ((weighted - probs[c] * inner) * scale).astype(B16)
                    grad_keys.append(
                        product(grad_scores, qkv_ref[queries, first : first + HEAD_DIM])
                    )
                    acc_ref[queries, first : first + HEAD_DIM] = dot_of(
                        grad_scores,
                        qkv_ref[keys, proj + first : proj + first + HEAD_DIM],
                        LEFT_TURNED,
                    )
                grad_key = jnp.concatenate(grad_keys, axis=1)
                if block == length // BLOCK - 1:
                    acc_ref[keys, key_columns] = grad_key
                    acc_ref[keys, value_columns] = grad_values
                else:
                    acc_ref[keys, key_columns] += grad_key
                    acc_ref[keys, value_columns] += grad_values
        for r in range(4):
            start = pl.multiple_of((own_ref[0] ^ r) * rows, rows)
            grad_ref[r * rows : (r + 1) * rows, :] = acc_ref[pl.ds(start, rows), :].astype(B16)
        grad_low_ref[...] = (
            ADAPTER_SCALING * dot_of(grad_ref[...], in_ref[...], RIGHT_TURNED)
        ).astype(B16)
        for x in range(3):
            columns = slice(x * proj, (x + 1) * proj)
            right = dot_of(low_ref[...], grad_ref[:, columns], LEFT_TURNED)
            narrow_ref[:, columns] = (
                ADAPTER_SCALING * right[x * RANK : (x + 1) * RANK]
            ).astype(B16)
        wait_all(arriving_x)
        low_half = low_out_ref[...] * jnp.asarray(ADAPTER_SCALING, B16)
        wide = (
            wide_sum_ref[...]
            + dot_of(low_half, branch_ref[...], LEFT_TURNED)
            + dot_of(grad_low_ref[...], x_ref[...], LEFT_TURNED)
        )
        for start in range(0, model, LANES):
            wide_grad_ref[start : start + LANES, :] = wide[:, start : start + LANES].T.astype(B16)

    return pl.pallas_call(
        kernel,
        out_shape=[
            shape(B16, length, width),
            shape(B16, length, LANES),
            shape(B16, RANK, width + proj),
            shape(B16, model, LANES),
        ],
        in_specs=[SMEM, SMEM] + [ANY] * 9 + [VMEM] * 10,
        out_specs=[VMEM] * 4,
        scratch_shapes=[
            pltpu.VMEM((16, 2, 2, half, proj), B16),
            pltpu.VMEM((length, model), B16),
            pltpu.VMEM((length, model), B16),
            pltpu.VMEM((length, proj), B16),
            pltpu.VMEM((length, width), F32),
            pltpu.SemaphoreType.DMA((3,)),
        ],
        compiler_params=params(52),
        cost_estimate=cost(3 * length * model * proj, 2e7),
    )(
        own,
        lambda_all,
        weights,
        *branch,
        *quarters,
        qkv,
        raw,
        lse,
        att,
        low_in,
        low_out,
        picked_wide,
        spread_in,
        spread_out,
        wide_sum,
    )


def input_part(grad, grad_low, weights, picked_wide):
    length, width = grad.shape
    rows, half, model = length // 4, weights.shape[3], picked_wide.shape[0]

    def kernel(grad_ref, grad_low_ref, weights_hbm, wide_ref, away_ref, near_ref, w_ref, sem):
        copy = pltpu.make_async_copy(weights_hbm.at[:, :, :, :, pl.ds(0, width)], w_ref, sem)
        copy.start()
        copy.wait()
        for pick, target in ((away_rows, away_ref), (near_rows, near_ref)):
            values = pick(grad_ref, rows, ALL)
            low = pick(grad_low_ref, rows, ALL)
            for start in range(0, model, CHUNK):
                blocks = slice(start // (4 * half), (start + CHUNK) // (4 * half))
                target[:, start : start + CHUNK] = (
                    dot_of(values, w_ref[blocks].reshape(CHUNK, width), RIGHT_TURNED)
                    + dot_of(low, wide_ref[start : start + CHUNK, :], RIGHT_TURNED)
                ).astype(target.dtype)

    return pl.pallas_call(
        kernel,
        out_shape=[shape(B16, 2 * rows, model), shape(F32, 2 * rows, model)],
        in_specs=[VMEM, VMEM, ANY, VMEM],
        out_specs=[VMEM, VMEM],
        scratch_shapes=[
            pltpu.VMEM((16, 2, 2, half, width), B16),
            pltpu.SemaphoreType.DMA,
        ],
        compiler_params=params(40),
        cost_estimate=cost(2 * length * model * width, 2e7),
    )(grad, grad_low, weights, picked_wide)


def sum_sequences(quarter_place, keys, arrived, split_count):
    def kernel(place_ref, keys_ref, arrived_ref, spread_ref, wide_ref):
        values = arrived_ref[...]

        def summed(key, count):
            target = lax.broadcasted_iota(jnp.int32, (count, 1), 0)
            return product((target == key).astype(F32).astype(B16), values)

        split = summed(keys_ref[0:1, :], 256)
        wide = summed(keys_ref[1:2, :], 128)
        squares = jnp.sum(split * split) + jnp.sum(wide * wide)
        spread_ref[...] = jnp.zeros_like(spread_ref)
        is_last = lax.broadcasted_iota(jnp.int32, (8, LANES), 0) == 7
        for device in range(128):
            spread_ref[device] = jnp.where(is_last, squares, 0.0)
        for adapter in range(ADAPTERS):
            for t in range(4):
                block = split[(adapter * 4 + t) * 8 : (adapter * 4 + t + 1) * 8]
                spread_ref[adapter * 16 + place_ref[0] * 4 + t] = jnp.where(
                    is_last, squares, block
                )
            rows = wide[adapter * RANK : (adapter + 1) * RANK]
            for x in range(7):
                wide_ref[x, :, adapter * RANK : (adapter + 1) * RANK] = rows[
                    :, x * RANK : (x + 1) * RANK
                ]

    return pl.pallas_call(
        kernel,
        out_shape=[shape(F32, 128, 8, LANES), shape(F32, 7, RANK, LANES)],
        in_specs=[SMEM, VMEM, VMEM],
        out_specs=[VMEM, VMEM],
        compiler_params=params(24),
        cost_estimate=cost(1e9, 2e6),
    )(quarter_place, keys, arrived)


def update_adapters(quarter_place, placed, split_count, wide, attention, feedforward):
    count, attention_chunks = attention[0].shape[0], attention[0].shape[2] // LANES
    hidden_chunks = feedforward[0].shape[2] // LANES

    def kernel(place_ref, placed_ref, *refs):
        wide_refs, attention_refs, hidden_refs = refs[:4], refs[4:7], refs[7:10]
        norm_ref, outs = refs[10], refs[11:23]
        attention_grad, hidden_grads = refs[23:]
        total = placed_ref[0, 7:8, :]
        for device in range(1, 128):
            total += placed_ref[device, 7:8, :]
        norm = jnp.sqrt(total)
        norm_ref[...] = norm
        factor = CLIP_NORM / (norm + 1e-06)
        for r in range(4):
            for chunk in range(count * attention_chunks + feedforward[0].shape[0] * hidden_chunks):
                eighth, row = chunk // split_count, chunk % split_count
                device = (2 * r + eighth // 4) * 16 + place_ref[0] * 4 + eighth % 4
                values = placed_ref[device, row : row + 1, :]
                if chunk < count * attention_chunks:
                    x, column = chunk // attention_chunks, chunk % attention_chunks * LANES
                    attention_grad[x, r : r + 1, column : column + LANES] = values
                else:
                    rest = chunk - count * attention_chunks
                    x, column = rest // hidden_chunks, rest % hidden_chunks * LANES
                    hidden_grads[x, r : r + 1, column : column + LANES] = values
        groups = (
            (wide_refs[1], wide_refs[0], wide_refs[2], wide_refs[3]),
            (attention_refs[0], attention_grad, attention_refs[1], attention_refs[2]),
            (hidden_refs[0], hidden_grads, hidden_refs[1], hidden_refs[2]),
        )
        for i, group in enumerate(groups):
            for x in range(group[0].shape[0]):
                values = [v[x] for v in group]
                whole = jnp.concatenate([factor] * (values[0].shape[1] // LANES), axis=1)
                for out, result in zip(outs[4 * i : 4 * i + 4], adam_step(*values, whole)):
                    out[x] = result

    like = lambda v: [shape(F32, *v.shape)] * 4
    return pl.pallas_call(
        kernel,
        out_shape=[shape(F32, 1, LANES)] + like(wide[0]) + like(attention[0]) + like(feedforward[0]),
        in_specs=[SMEM] + [VMEM] * 11,
        out_specs=[VMEM] * 13,
        scratch_shapes=[
            pltpu.VMEM(attention[0].shape, F32),
            pltpu.VMEM(feedforward[0].shape, F32),
        ],
        compiler_params=params(24),
        cost_estimate=cost(1e7, 3e6),
    )(quarter_place, placed, *wide, *attention, *feedforward)


def adam_step(parameter, gradient, moment, variance, factor):
    clipped = gradient * factor
    moment_new = BETA_FIRST * moment + (1.0 - BETA_FIRST) * clipped
    variance_new = BETA_SECOND * variance + (1.0 - BETA_SECOND) * clipped * clipped
    moment_hat = moment_new / (1.0 - BETA_FIRST**STEP)
    variance_hat = variance_new / (1.0 - BETA_SECOND**STEP)
    updated = parameter - LEARN_RATE * (
        moment_hat / (jnp.sqrt(variance_hat) + ADAM_EPS) + WEIGHT_DECAY * parameter
    )
    return (clipped, updated, moment_new, variance_new)


def flat_rows(stacked):
    moved = stacked.astype(B16).transpose(1, 0, 2)
    return moved.reshape(stacked.shape[1], -1)


def local(
    tokens,
    cotangent,
    adapter_ids,
    norm_gains,
    lambda_vectors,
    weight_inputs,
    weight_output,
    hidden_weight_matrix,
    weight_down,
    adapter_wide,
    adapter_attention,
    adapter_feedforward,
    moment_wide,
    variance_wide,
    moment_attention,
    variance_attention,
    moment_feedforward,
    variance_feedforward,
):
    place = Place()
    adapter = adapter_ids[0]
    own_quarter = place.tensor.astype(jnp.int32).reshape(1)
    local_tokens = tokens[0].astype(F32)
    upstream_b = cotangent[0]
    gain_values = norm_gains.astype(F32)
    lambda_all = (
        jnp.exp(jnp.sum(lambda_vectors[0] * lambda_vectors[1], axis=-1))
        - jnp.exp(jnp.sum(lambda_vectors[2] * lambda_vectors[3], axis=-1))
        + LAMBDA_INIT
    )
    heads_local = lambda_vectors.shape[1]
    proj = weight_inputs.shape[2]
    ff = hidden_weight_matrix.shape[2]
    model = tokens.shape[2]

    shard_one = jnp.concatenate(
        [weight_inputs[0], weight_inputs[1], weight_inputs[2], weight_output.T], axis=1
    )
    shard_two = jnp.concatenate([hidden_weight_matrix[0], hidden_weight_matrix[1]], axis=1)
    wide_rows = adapter_wide.astype(B16).transpose(0, 2, 1).reshape(7 * RANK, LANES)
    attention_rows = flat_rows(adapter_attention).reshape(-1, LANES)
    attention_count, id_row = attention_rows.shape[0], 7 * RANK + attention_rows.shape[0]
    to_tiles = lambda v: jnp.pad(v, ((0, -v.shape[0] % 16), (0, 0)))
    first_rows = to_tiles(
        jnp.concatenate(
            [wide_rows, attention_rows, jnp.broadcast_to(adapter.astype(B16), (1, LANES))]
        )
    )
    hidden_rows = to_tiles(flat_rows(adapter_feedforward).reshape(-1, LANES))
    hidden_shape = hidden_rows.shape
    rest = jnp.concatenate(
        [weight_down.T, hidden_rows.reshape(weight_down.shape[1], -1)], axis=1
    )
    normed_one, scale_one = norm_forward(local_tokens, gain_values[0])
    normed_one_b = normed_one.astype(B16)

    own_pair = jnp.concatenate([normed_one_b, upstream_b], axis=0)
    (other_one, other_first, core_pair), (shard_one, shard_two, normed_out) = exchange(
        [(shard_one, PAIR_X), (first_rows, PAIR_X), (own_pair, CORES)],
        shard_one,
        shard_two,
        normed_one_b,
    )

    def pair_of(mine, theirs):
        swap = place.dp % 2 == 1
        return jnp.stack([jnp.where(swap, theirs, mine), jnp.where(swap, mine, theirs)])

    def gather_rest(pair):
        groups = [list(range(0, 32, 2)), list(range(1, 32, 2))]
        gathered = lax.all_gather(pair, "dp", axis=0, tiled=False, axis_index_groups=groups)
        return gathered.reshape((32,) + pair.shape[1:])

    first_adapters = gather_rest(pair_of(first_rows, other_first))
    blocks_one = first_blocks(shard_one, other_one, place)
    sends = ring_sends(*blocks_one)
    other_two = send(shard_two, PAIR_X)
    near, (normed_out, rest) = exchange(sends, normed_out, rest)
    (*far, other_rest), (normed_out, other_two) = exchange(
        relay_sends(sends, near) + [(rest, PAIR_X)], normed_out, other_two
    )
    gathered = gather_rest(pair_of(rest, other_rest)).reshape(model, -1)
    planes_one = planes(*blocks_one, near, far, 0, 4 * proj)
    sends = plane_sends(*planes_one)
    (*near_one, far_normed), (first_adapters, upstream_out) = exchange(
        sends + [(normed_out, FAR_X)], first_adapters, upstream_b
    )
    blocks_two = first_blocks(shard_two, other_two, place)

    onehot_rows = (
        jnp.arange(LANES)[None, :, None]
        == (adapter * RANK + jnp.arange(LANES) - RANK * jnp.arange(7)[:, None])[:, None, :]
    ) & (jnp.arange(LANES)[None, None, :] // RANK == jnp.arange(7)[:, None, None])
    wide_mine = (
        first_adapters[:, : 7 * RANK]
        .reshape(32, 7, RANK, LANES)
        .transpose(0, 2, 1, 3)
        .reshape(512, 7 * LANES)
    )
    picked_t = product(wide_mine, onehot_rows.astype(B16).reshape(7 * LANES, LANES)).astype(B16)
    (*far_one, picked_far), (far_normed, upstream_out, *blocks_two) = exchange(
        relay_sends(sends, near_one) + [(picked_t, FAR_X)], far_normed, upstream_out, *blocks_two
    )
    picked_all = in_place(
        [picked_t, send(picked_t, CORES), picked_far, send(picked_far, CORES)], place
    ).reshape(4, 32, 16, LANES)
    picked_wide = picked_all.transpose(1, 0, 2, 3).reshape(model, LANES)
    def picked_rows(gathered, first, count, width):
        mine = lax.dynamic_slice_in_dim(gathered, adapter * 4, 4, 0)
        return mine[:, first : first + count].reshape(RANK, width)

    def spread_rows(rows, slots, width):
        slot = jnp.concatenate([jnp.full((width,), x, jnp.int32) for x in slots])
        return jnp.where(
            slot[None, :] == jnp.arange(LANES)[:, None] // RANK,
            jnp.concatenate([rows] * 8, axis=0),
            0,
        ).astype(B16)

    spread = spread_rows(
        picked_rows(first_adapters, 7 * RANK, attention_count, 4 * proj), (0, 1, 2, 5), proj
    )
    spread_in, spread_out = spread[:, : 3 * proj], spread[:, 3 * proj :]
    ids_all = first_adapters[:, id_row, 0].astype(jnp.int32)

    token_rows = normed_one_b.shape[0]
    seq_normed_one = [
        normed_one_b,
        core_pair[:token_rows],
        far_normed,
        send(far_normed, CORES),
    ]
    w_attention, qkv, low_in = projection_part(
        own_quarter,
        pieces_of(planes_one, near_one, far_one),
        seq_normed_one,
        picked_wide,
        spread_in,
    )
    attention_b, raw, lse, low_out, away, near_sum = attention_part(
        own_quarter, lambda_all, w_attention, qkv, picked_wide, spread_out, heads_local
    )
    sends = ring_sends(*blocks_two)
    far_upstream = send(upstream_out, FAR_X)
    near, (away, near_sum) = exchange(sends, away, near_sum)
    far, (away, near_sum, far_upstream) = exchange(
        relay_sends(sends, near), away, near_sum, far_upstream
    )
    seq_upstream = [
        upstream_b,
        core_pair[token_rows:],
        far_upstream,
        send(far_upstream, CORES),
    ]
    staying, leaving = core_sum(near_sum, away)
    planes_two = planes(*blocks_two, near, far, 0, 2 * ff)
    sends = plane_sends(*planes_two)
    (*near_two, arrived), (gathered, *seq_upstream) = exchange(
        sends + [(leaving, FAR_X)], gathered, *seq_upstream
    )
    hidden_picked = lax.dynamic_slice_in_dim(gathered, adapter * 256, 256, 0)[:, ff:]
    hidden_picked = hidden_picked.reshape((4,) + hidden_shape)[:, : 3 * ff * 4 // LANES]
    spread = spread_rows(hidden_picked.reshape(RANK, 3 * ff), (3, 4, 6), ff)
    spread_hidden, spread_down = spread[:, : 2 * ff], spread[:, 2 * ff :]
    w_down = gathered
    grad_low_down, grad_hidden = hidden_grad(w_down, seq_upstream, picked_wide, spread_down)
    residual_one = local_tokens + staying + arrived.astype(F32)
    second_normalized, scale_two = norm_forward(residual_one, gain_values[1])
    normed_two_b = second_normalized.astype(B16)
    (*far_two, far_tokens), (grad_low_down, grad_hidden) = exchange(
        relay_sends(sends, near_two) + [(normed_two_b, FAR_X)], grad_low_down, grad_hidden
    )
    seq_normed_two = [
        normed_two_b,
        send(normed_two_b, CORES),
        far_tokens,
        send(far_tokens, CORES),
    ]

    hidden_b, grad_gate_up, low_hidden, grad_low_hidden, away, near_sum = hidden_part(
        pieces_of(planes_two, near_two, far_two),
        grad_hidden,
        seq_normed_two,
        picked_wide,
        spread_hidden,
    )
    grad_staying, leaving = core_sum(near_sum, away)
    leaving, hidden_b, grad_gate_up = together(leaving, hidden_b, grad_gate_up)
    away_down, near_down, narrow_two, wide_two = down_part(
        hidden_b,
        grad_gate_up,
        low_hidden,
        grad_low_down,
        grad_low_hidden,
        w_down,
        seq_normed_two,
        seq_upstream,
        picked_wide,
        spread_down,
    )
    arrived, near_down, away_down = together(send(leaving, FAR_X), near_down, away_down)
    grad_normed_two = grad_staying + arrived.astype(F32)
    grad_residual = upstream_b.astype(F32) + norm_backward(
        residual_one, scale_two, gain_values[1], grad_normed_two
    )
    grad_branch_b = grad_residual.astype(B16)
    down_staying, down_leaving = core_sum(near_down, away_down)
    far_branch, down_leaving = together(send(grad_branch_b, FAR_X), down_leaving)
    seq_grad_branch = [
        grad_branch_b,
        send(grad_branch_b, CORES),
        far_branch,
        send(far_branch, CORES),
    ]

    grad_projected, grad_low_in, narrow_one, wide_grads = attention_grads(
        own_quarter,
        lambda_all,
        w_attention,
        qkv,
        raw,
        lse,
        attention_b,
        low_in,
        low_out,
        seq_grad_branch,
        seq_normed_one,
        picked_wide,
        spread_in,
        spread_out,
        wide_two,
        heads_local,
    )
    down_arrived, narrow_one, wide_grads = together(
        send(down_leaving, FAR_X), narrow_one, wide_grads
    )
    result = residual_one + down_staying + down_arrived.astype(F32)
    away, near_sum = input_part(grad_projected, grad_low_in, w_attention, picked_wide)

    split_grads = jnp.concatenate([narrow_one, narrow_two], axis=1)
    columns = split_grads.shape[1]
    row_count = RANK + 8
    piece = -(-columns // 1024) * 128
    split_count = piece // LANES
    split_blocks = (
        jnp.pad(split_grads, ((0, 0), (0, 8 * piece - columns)))
        .reshape(4, 4, 2, 4, piece)
        .transpose(1, 2, 0, 3, 4)
        .reshape(128, split_count, LANES)
    )
    blocks = jnp.concatenate(
        [
            wide_grads.reshape(128, RANK, LANES),
            split_blocks,
            jnp.zeros((128, 8 - split_count, LANES), B16),
        ],
        axis=1,
    )
    source = jnp.arange(128 * row_count, dtype=jnp.int32)
    source_row, source_t = source % row_count, source // row_count % 4
    source_id = jnp.repeat(ids_all, 4 * row_count)
    split_row = source_row - RANK
    split_key = jnp.where(
        (split_row >= 0) & (split_row < split_count), source_id * 32 + source_t * 8 + split_row, -1
    )
    wide_key = jnp.where(source_row < RANK, source_id * RANK + source_row, -1)
    keys = jnp.stack([split_key, wide_key])
    quarter_place = (place.dp % 4).astype(jnp.int32).reshape(1)
    arrived, away, near_sum, keys = together(
        lax.all_to_all(blocks, AXES, split_axis=0, concat_axis=0, tiled=True),
        away,
        near_sum,
        keys,
    )
    spread, grads_wide = sum_sequences(
        quarter_place, keys, arrived.reshape(128 * row_count, LANES), split_count
    )
    staying, leaving = core_sum(near_sum, away)
    input_arrived, placed = together(
        send(leaving, FAR_X),
        lax.all_to_all(spread, AXES, split_axis=0, concat_axis=0, tiled=True),
    )
    grad_normed_one = staying + input_arrived.astype(F32)
    grad_input = grad_residual + norm_backward(
        local_tokens, scale_one, gain_values[0], grad_normed_one
    )
    turned = lambda v: v.transpose(0, 2, 1)
    grad_norm, *updates = update_adapters(
        quarter_place,
        placed,
        split_count,
        (grads_wide, turned(adapter_wide), turned(moment_wide), turned(variance_wide)),
        (adapter_attention, moment_attention, variance_attention),
        (adapter_feedforward, moment_feedforward, variance_feedforward),
    )
    wide_new = [turned(v) for v in updates[:4]]
    attention_new, feedforward_new = updates[4:8], updates[8:]
    return (
        result.astype(B16)[None],
        grad_input.astype(B16)[None],
        grad_norm[0, 0],
        wide_new[0],
        attention_new[0],
        feedforward_new[0],
        wide_new[1],
        attention_new[1],
        feedforward_new[1],
        wide_new[2],
        attention_new[2],
        feedforward_new[2],
        wide_new[3],
        attention_new[3],
        feedforward_new[3],
    )


def solution(mesh):
    return jax.shard_map(
        local,
        mesh=mesh,
        in_specs=(
            P("dp", "tensor", None),
            P("dp", "tensor", None),
            P("dp"),
            P(),
            P(None, "tensor", None),
            P(None, "dp", "tensor"),
            P("tensor", "dp"),
            P(None, "dp", "tensor"),
            P("tensor", "dp"),
            P(None, None, ("dp", "tensor")),
            P(None, "dp", "tensor"),
            P(None, "dp", "tensor"),
            P(None, None, ("dp", "tensor")),
            P(None, None, ("dp", "tensor")),
            P(None, "dp", "tensor"),
            P(None, "dp", "tensor"),
            P(None, "dp", "tensor"),
            P(None, "dp", "tensor"),
        ),
        out_specs=(
            P("dp", "tensor", None),
            P("dp", "tensor", None),
            P(),
            P(None, None, ("dp", "tensor")),
            P(None, "dp", "tensor"),
            P(None, "dp", "tensor"),
            P(None, None, ("dp", "tensor")),
            P(None, "dp", "tensor"),
            P(None, "dp", "tensor"),
            P(None, None, ("dp", "tensor")),
            P(None, "dp", "tensor"),
            P(None, "dp", "tensor"),
            P(None, None, ("dp", "tensor")),
            P(None, "dp", "tensor"),
            P(None, "dp", "tensor"),
        ),
        check_vma=False,
    )
```

```python
import jax
import jax.numpy as jnp
from jax import lax
from jax.experimental import pallas as pl
from jax.experimental.pallas import tpu as pltpu
from jax.sharding import PartitionSpec as P

HEAD_DIM = 128
ADAPTERS = 8
RANK = 16
BLOCK = 256
STEP = 10


NORM_EPS = 1e-05
ADAPTER_SCALING = 0.5
LAMBDA_INIT = 0.2
OUT_GAIN = 0.8
CLIP_NORM = 1.0
LEARN_RATE = 0.05
BETA_FIRST = 0.9
BETA_SECOND = 0.999
ADAM_EPS = 1e-08
WEIGHT_DECAY = 0.01
NEG_LARGE = -1e30
AXES = ("dp", "tensor")
B16 = jnp.bfloat16
F32 = jnp.float32


def product(left, right):
    return jnp.dot(left, right, preferred_element_type=F32)


def contract(form, left, right):
    return jnp.einsum(form, left, right, preferred_element_type=F32)


def index_of(z, y, x, core):
    x, y, z, core = x % 4, y % 4, z % 4, core % 2
    return ((z * 4 + y) * 2 + x % 2) * 4 + (x // 2) * 2 + core


def routes(move):
    pairs = []
    for z in range(4):
        for y in range(4):
            for x in range(4):
                for core in range(2):
                    pairs.append((index_of(z, y, x, core), index_of(*move(z, y, x, core))))
    return pairs


UP_Z = routes(lambda z, y, x, c: (z + 1, y, x, c))
DOWN_Z = routes(lambda z, y, x, c: (z - 1, y, x, c))
FAR_Z = routes(lambda z, y, x, c: (z + 2, y, x, c))
UP_Y = routes(lambda z, y, x, c: (z, y + 1, x, c))
DOWN_Y = routes(lambda z, y, x, c: (z, y - 1, x, c))
FAR_Y = routes(lambda z, y, x, c: (z, y + 2, x, c))
PAIR_X = routes(lambda z, y, x, c: (z, y, x ^ 1, c))
FAR_X = routes(lambda z, y, x, c: (z, y, x + 2, c))
CORES = routes(lambda z, y, x, c: (z, y, x, 1 - c))


def send(values, pairs):
    return lax.ppermute(values, AXES, pairs)


class Place:
    def __init__(self):
        tensor = lax.axis_index("tensor")
        self.far, self.core, self.tensor = tensor // 2, tensor % 2, tensor
        self.dp = lax.axis_index("dp")


def together(*values):
    return lax.optimization_barrier(values)


OFFSETS = (0, 3, 1, 2)
LANES = 128
CHUNK = 512


def copy_pieces(pieces, held, sems, groups):
    sources = (pieces[:5], pieces[5:10])
    dp = lax.axis_index("dp")
    at = (dp // 8, (dp // 2) & 3)
    started = []
    for i, (start, width) in enumerate(groups):
        columns = pl.ds(start, width)
        copies = []
        for order in range(2):
            for outer in range(4):
                for block in range(4):
                    places = [0, 0]
                    places[order] = (at[order] + OFFSETS[outer]) & 3
                    places[1 - order] = (at[1 - order] + OFFSETS[block]) & 3
                    if outer < 3:
                        source = sources[order][outer].at[pl.ds(2 * block, 2), :, columns]
                    else:
                        part = sources[order][3 + block // 2]
                        source = part.at[pl.ds(2 * (block % 2), 2), :, columns]
                    copy = pltpu.make_async_copy(
                        source, held.at[places[0] * 4 + places[1], :, order, :, columns], sems.at[i]
                    )
                    copy.start()
                    copies.append(copy)
        started.append(copies)
    return started


def copy_quarters(quarters, held, sem):
    rows = quarters[0].shape[0]
    copies = [
        pltpu.make_async_copy(
            quarter, held.at[pl.ds(i * rows, rows), pl.ds(0, quarter.shape[1])], sem
        )
        for i, quarter in enumerate(quarters)
    ]
    for copy in copies:
        copy.start()
    return copies


def copy_factors(wide, spread, held, sems):
    copies = [
        pltpu.make_async_copy(
            wide, held.at[pl.ds(0, 16), :, :, :, pl.ds(held.shape[4] - LANES, LANES)], sems.at[0]
        )
    ]
    if spread is not None:
        copies.append(
            pltpu.make_async_copy(
                spread, held.at[16, :, :, :, pl.ds(0, spread.shape[3])], sems.at[1]
            )
        )
    for copy in copies:
        copy.start()
    return copies


def as_blocks(factor, half):
    return factor.reshape(-1, 2, 2, half, factor.shape[1])


def wait_all(copies):
    for copy in copies:
        copy.wait()


def first_blocks(shard, other, place):
    half = shard.shape[0] // 2
    swap = place.dp % 2 == 1
    low, high = jnp.where(swap, other, shard), jnp.where(swap, shard, other)
    return (jnp.stack([low[:half], high[:half]]), jnp.stack([low[half:], high[half:]]))


def ring_sends(part_a, part_b):
    return [(part_a, UP_Y), (part_a, DOWN_Y), (part_b, UP_Z), (part_b, DOWN_Z)]


def plane_sends(part_a, part_b):
    return [(part_a, UP_Z), (part_a, DOWN_Z), (part_b, UP_Y), (part_b, DOWN_Y)]


def relay_sends(sends, arrived):
    out = []
    for i, (_, pairs) in enumerate(sends):
        middle = arrived[i].shape[0] // 2
        out.append((arrived[i][:middle] if i % 2 == 0 else arrived[i][middle:], pairs))
    return out


def planes(part_a, part_b, near, far, start, width):
    cut = lambda v: v[..., start : start + width]
    return (
        jnp.concatenate([cut(v) for v in (part_a, near[0], near[1], far[0], far[1])], axis=0),
        jnp.concatenate([cut(v) for v in (part_b, near[2], near[3], far[2], far[3])], axis=0),
    )


def pieces_of(plane_pair, near, far):
    return (
        plane_pair[0],
        near[0],
        near[1],
        far[0],
        far[1],
        plane_pair[1],
        near[2],
        near[3],
        far[2],
        far[3],
    )


def exchange(sends, *others):
    results = [send(values, pairs) for values, pairs in sends]
    out = together(*results, *others)
    return list(out[: len(sends)]), list(out[len(sends) :])


def in_place(values, place):
    own, core, far, far_core = values
    swap_core, swap_far = place.core == 1, place.far == 1
    near = jnp.stack([jnp.where(swap_core, core, own), jnp.where(swap_core, own, core)])
    away = jnp.stack([jnp.where(swap_core, far_core, far), jnp.where(swap_core, far, far_core)])
    return jnp.concatenate(
        [jnp.where(swap_far, away, near), jnp.where(swap_far, near, away)], axis=0
    )


def core_sum(near, away):
    rows = near.shape[0] // 2
    arrived = send(away, CORES)
    staying = near[:rows] + arrived[:rows].astype(F32)
    return staying, (near[rows:] + arrived[rows:].astype(F32)).astype(B16)


def norm_forward(values, gain_value):
    factor = lax.rsqrt(jnp.mean(values * values, axis=-1, keepdims=True) + NORM_EPS)
    return (values * factor * gain_value, factor)


def norm_backward(values, factor, gain_value, gradient):
    scaled = gradient * gain_value
    return factor * (
        scaled - values * factor * factor * jnp.mean(scaled * values, axis=-1, keepdims=True)
    )


RIGHT_TURNED = (((1,), (1,)), ((), ()))
LEFT_TURNED = (((0,), (0,)), ((), ()))


def dot_of(left, right, dims):
    return lax.dot_general(left, right, dims, preferred_element_type=F32)


def away_rows(ref, rows, columns):
    return jnp.concatenate([ref[rows : 2 * rows, columns], ref[3 * rows : 4 * rows, columns]])


def near_rows(ref, rows, columns):
    return jnp.concatenate([ref[0:rows, columns], ref[2 * rows : 3 * rows, columns]])


ALL = slice(None)
VMEM = pl.BlockSpec(memory_space=pltpu.VMEM)
SMEM = pl.BlockSpec(memory_space=pltpu.SMEM)
ANY = pl.BlockSpec(memory_space=pl.ANY)


def shape(dtype, *dims):
    return jax.ShapeDtypeStruct(dims, dtype)


def params(mib):
    return pltpu.CompilerParams(vmem_limit_bytes=mib * 2**20)


def cost(flops, size):
    return pl.CostEstimate(flops=int(flops), bytes_accessed=int(size), transcendentals=0)


def scores_of(qkv_ref, proj, first, queries, keys):
    return (
        dot_of(
            qkv_ref[keys, proj + first : proj + first + HEAD_DIM],
            qkv_ref[queries, first : first + HEAD_DIM],
            RIGHT_TURNED,
        )
        * HEAD_DIM**-0.5
    )


def projection_part(own, pieces, quarters, picked_wide, spread_in):
    rows, model = quarters[0].shape
    length, half, total = 4 * rows, pieces[0].shape[1], pieces[0].shape[2]
    width = spread_in.shape[1]
    proj = width // 3

    def kernel(own_ref, *refs):
        piece_refs, quarter_refs = refs[:10], refs[10:14]
        wide_ref, in_ref, w_out, qkv_ref, low_ref = refs[14:19]
        held, x_ref, sems, x_sem, factor_sems, out_sem = refs[19:]
        arriving = copy_quarters(quarter_refs, x_ref, x_sem)
        factors = copy_factors(wide_ref, in_ref, held, factor_sems)
        groups = copy_pieces(piece_refs, held, sems, [(0, width), (width, total - width)])
        wait_all(arriving)
        wait_all(factors)
        wide = held[0:16, :, :, :, total:].reshape(model, LANES)
        low_ref[...] = product(x_ref[:, :model], wide).astype(B16)
        x_ref[:, model:] = low_ref[...] * jnp.asarray(ADAPTER_SCALING, B16)
        wait_all(groups[0])
        for f in range(2):
            part = slice(2 * f * rows, 2 * (f + 1) * rows)
            weights = held[:, :, :, :, 0:width].reshape(model + LANES, width)
            values = product(x_ref[part, :], weights)
            for k in range(2):
                start = pl.multiple_of((own_ref[0] ^ (2 * f + k)) * rows, rows)
                qkv_ref[pl.ds(start, rows), :] = values[k * rows : (k + 1) * rows].astype(B16)
            if f == 0:
                wait_all(groups[1])
                leaving = pltpu.make_async_copy(
                    held.at[pl.ds(0, 16), :, :, :, pl.ds(0, total)], w_out, out_sem
                )
                leaving.start()
        leaving.wait()

    return pl.pallas_call(
        kernel,
        out_shape=[
            shape(B16, 16, 2, 2, half, total),
            shape(B16, length, width),
            shape(B16, length, LANES),
        ],
        in_specs=[SMEM] + [ANY] * 16,
        out_specs=[ANY] + [VMEM] * 2,
        scratch_shapes=[
            pltpu.VMEM((17, 2, 2, half, total + LANES), B16),
            pltpu.VMEM((length, model + LANES), B16),
            pltpu.SemaphoreType.DMA((2,)),
            pltpu.SemaphoreType.DMA,
            pltpu.SemaphoreType.DMA((2,)),
            pltpu.SemaphoreType.DMA,
        ],
        compiler_params=params(32),
        cost_estimate=cost(2 * length * model * total, 2.4e7),
    )(
        own,
        *pieces,
        *quarters,
        as_blocks(picked_wide, half),
        spread_in.reshape(2, 2, half, width),
    )


def attention_part(own, lambda_all, weights, qkv, picked_wide, spread_out, heads):
    length, width = qkv.shape
    proj, half, model = width // 3, weights.shape[3], picked_wide.shape[0]
    rows = length // 4

    def kernel(own_ref, lambda_ref, weights_hbm, qkv_ref, wide_ref, out_ref, *refs):
        att_ref, raw_out, lse_ref, low_out_ref, away_out, near_out = refs[:6]
        held, raw_ref, away_ref, near_ref, w_sem, raw_sem, sems = refs[6:]
        weight_copy = pltpu.make_async_copy(
            weights_hbm.at[:, :, :, :, pl.ds(width, proj)], held, w_sem
        )
        weight_copy.start()
        for head in range(heads):
            column = head * 2 * HEAD_DIM
            value_columns = slice(2 * proj + column, 2 * proj + column + 2 * HEAD_DIM)
            for block in range(length // BLOCK):
                queries = slice(block * BLOCK, (block + 1) * BLOCK)
                keys = slice(0, (block + 1) * BLOCK)
                parts = []
                for c in range(2):
                    scores = scores_of(qkv_ref, proj, column + c * HEAD_DIM, queries, keys)
                    top = jnp.max(scores, axis=0, keepdims=True)
                    shifted = jnp.exp(scores - top)
                    total_sum = jnp.sum(shifted, axis=0, keepdims=True)
                    lse_ref[head * 2 + c : head * 2 + c + 1, queries] = top + jnp.log(total_sum)
                    parts.append(shifted * (1.0 / total_sum))
                combined = (parts[0] - lambda_ref[head] * parts[1]).astype(B16)
                raw = dot_of(combined, qkv_ref[keys, value_columns], LEFT_TURNED)
                raw_ref[queries, column : column + 2 * HEAD_DIM] = raw
        raw_copy = pltpu.make_async_copy(raw_ref, raw_out, raw_sem)
        raw_copy.start()
        for t in range(4):
            start = pl.multiple_of((own_ref[0] ^ t) * rows, rows)
            for head in range(heads):
                columns = slice(head * 2 * HEAD_DIM, (head + 1) * 2 * HEAD_DIM)
                raw = raw_ref[t * rows : (t + 1) * rows, columns]
                factor = lax.rsqrt(jnp.mean(raw * raw, axis=-1, keepdims=True) + NORM_EPS)
                att_ref[pl.ds(start, rows), columns] = (raw * factor * OUT_GAIN).astype(B16)
        low_out_ref[...] = dot_of(att_ref[...], out_ref[...], RIGHT_TURNED).astype(B16)
        weight_copy.wait()
        leaving = [raw_copy]
        for i, (pick, target, out) in enumerate(
            ((away_rows, away_ref, away_out), (near_rows, near_ref, near_out))
        ):
            values = pick(att_ref, rows, ALL)
            low = pick(low_out_ref, rows, ALL) * jnp.asarray(ADAPTER_SCALING, B16)
            for start in range(0, model, CHUNK):
                blocks = slice(start // (4 * half), (start + CHUNK) // (4 * half))
                target[:, start : start + CHUNK] = (
                    dot_of(values, held[blocks].reshape(CHUNK, proj), RIGHT_TURNED)
                    + dot_of(low, wide_ref[start : start + CHUNK, :], RIGHT_TURNED)
                ).astype(target.dtype)
            copy = pltpu.make_async_copy(target, out, sems.at[i])
            copy.start()
            leaving.append(copy)
        wait_all(leaving)

    return pl.pallas_call(
        kernel,
        out_shape=[
            shape(B16, length, proj),
            shape(F32, length, proj),
            shape(F32, 2 * heads, length),
            shape(B16, length, LANES),
            shape(B16, 2 * rows, model),
            shape(F32, 2 * rows, model),
        ],
        in_specs=[SMEM, SMEM, ANY] + [VMEM] * 3,
        out_specs=[VMEM, ANY, VMEM, VMEM, ANY, ANY],
        scratch_shapes=[
            pltpu.VMEM((16, 2, 2, half, proj), B16),
            pltpu.VMEM((length, proj), F32),
            pltpu.VMEM((2 * rows, model), B16),
            pltpu.VMEM((2 * rows, model), F32),
            pltpu.SemaphoreType.DMA,
            pltpu.SemaphoreType.DMA,
            pltpu.SemaphoreType.DMA((2,)),
        ],
        compiler_params=params(32),
        cost_estimate=cost(2 * length * model * proj + 4 * length * length * proj, 2e7),
    )(own, lambda_all, weights, qkv, picked_wide, spread_out)


def hidden_grad(w_down, upstream, picked_wide, spread_down):
    rows, model = upstream[0].shape
    length, ff = 4 * rows, spread_down.shape[1]

    def kernel(*refs):
        down_hbm, upstream_refs = refs[0], refs[1:5]
        wide_ref, down_spread, grad_low_ref, grad_ref, down_ref, up_ref, sems = refs[5:]
        down_copy = pltpu.make_async_copy(down_hbm.at[:, pl.ds(0, ff)], down_ref.at[pl.ds(0, model), :], sems.at[1])
        arriving = copy_quarters(upstream_refs, up_ref, sems.at[0])
        down_copy.start()
        wait_all(arriving)
        grad_low_ref[...] = (
            ADAPTER_SCALING * product(up_ref[:, :model], wide_ref[...])
        ).astype(B16)
        up_ref[:, model:] = grad_low_ref[...]
        down_ref[model:, :] = down_spread[...]
        down_copy.wait()
        for f in range(2):
            part = slice(2 * f * rows, 2 * (f + 1) * rows)
            grad_ref[part, :] = product(up_ref[part, :], down_ref[...]).astype(B16)

    return pl.pallas_call(
        kernel,
        out_shape=[shape(B16, length, LANES), shape(B16, length, ff)],
        in_specs=[ANY] * 5 + [VMEM] * 2,
        out_specs=[VMEM] * 2,
        scratch_shapes=[
            pltpu.VMEM((model + LANES, ff), B16),
            pltpu.VMEM((length, model + LANES), B16),
            pltpu.SemaphoreType.DMA((2,)),
        ],
        compiler_params=params(32),
        cost_estimate=cost(2 * length * model * ff, 1.5e7),
    )(w_down, *upstream, picked_wide, spread_down)


def hidden_part(pieces, grad_hidden, quarters, picked_wide, spread_hidden):
    rows, model = quarters[0].shape
    length, half, total = 4 * rows, pieces[0].shape[1], pieces[0].shape[2]
    ff = total // 2

    def kernel(*refs):
        piece_refs, quarter_refs = refs[:10], refs[10:14]
        grad_hidden_ref, wide_ref, hidden_spread = refs[14:17]
        hidden_out, grad_out, low_ref, grad_low_ref, away_out, near_out = refs[17:23]
        hidden_ref, grad_ref, gate_ref, away_ref, near_ref, held, x_ref = refs[23:30]
        sems, x_sem, factor_sems, out_sems = refs[30:]
        arriving = copy_quarters(quarter_refs, x_ref, x_sem)
        factors = copy_factors(wide_ref, hidden_spread, held, factor_sems)
        gate_copies = copy_pieces(piece_refs, held, sems, [(0, ff)])
        wait_all(arriving)
        wait_all(factors)
        wide = held[0:16, :, :, :, total:].reshape(model, LANES)
        low_ref[...] = product(x_ref[:, :model], wide).astype(B16)
        x_ref[:, model:] = low_ref[...] * jnp.asarray(ADAPTER_SCALING, B16)
        up_copies = copy_pieces(piece_refs, held, sems.at[pl.ds(1, 1)], [(ff, ff)])
        wait_all(gate_copies[0])
        gate_ref[...] = product(
            x_ref[...], held[:, :, :, :, 0:ff].reshape(model + LANES, ff)
        )
        wait_all(up_copies[0])
        for f in range(2):
            part = slice(2 * f * rows, 2 * (f + 1) * rows)
            upper = product(
                x_ref[part, :], held[:, :, :, :, ff:total].reshape(model + LANES, ff)
            )
            gate = gate_ref[part, :]
            sigmoid_gate = 1.0 / (1.0 + jnp.exp(-gate))
            swish = gate * sigmoid_gate
            hidden_ref[part, :] = (swish * upper).astype(B16)
            grad_hidden = grad_hidden_ref[part, :].astype(F32)
            grad_ref[part, 0:ff] = (
                grad_hidden * upper * (sigmoid_gate + swish * (1.0 - sigmoid_gate))
            ).astype(B16)
            grad_ref[part, ff:total] = (grad_hidden * swish).astype(B16)
        leaving = [
            pltpu.make_async_copy(hidden_ref, hidden_out, out_sems.at[0]),
            pltpu.make_async_copy(grad_ref.at[:, pl.ds(0, total)], grad_out, out_sems.at[1]),
        ]
        for copy in leaving:
            copy.start()
        spread = held[16, :, :, :, 0:total].reshape(LANES, total)
        grad_low_ref[...] = (
            ADAPTER_SCALING * dot_of(grad_ref[:, :total], spread, RIGHT_TURNED)
        ).astype(B16)
        grad_ref[:, total:] = grad_low_ref[...]
        weights = held[0:16].reshape(model, total + LANES)
        for i, (pick, target, out) in enumerate(
            ((away_rows, away_ref, away_out), (near_rows, near_ref, near_out))
        ):
            target[...] = dot_of(pick(grad_ref, rows, ALL), weights, RIGHT_TURNED).astype(
                target.dtype
            )
            copy = pltpu.make_async_copy(target, out, out_sems.at[2 + i])
            copy.start()
            leaving.append(copy)
        wait_all(leaving)

    return pl.pallas_call(
        kernel,
        out_shape=[
            shape(B16, length, ff),
            shape(B16, length, total),
            shape(B16, length, LANES),
            shape(B16, length, LANES),
            shape(B16, 2 * rows, model),
            shape(F32, 2 * rows, model),
        ],
        in_specs=[ANY] * 14 + [VMEM] + [ANY] * 2,
        out_specs=[ANY, ANY, VMEM, VMEM, ANY, ANY],
        scratch_shapes=[
            pltpu.VMEM((length, ff), B16),
            pltpu.VMEM((length, total + LANES), B16),
            pltpu.VMEM((length, ff), F32),
            pltpu.VMEM((2 * rows, model), B16),
            pltpu.VMEM((2 * rows, model), F32),
            pltpu.VMEM((17, 2, 2, half, total + LANES), B16),
            pltpu.VMEM((length, model + LANES), B16),
            pltpu.SemaphoreType.DMA((2,)),
            pltpu.SemaphoreType.DMA,
            pltpu.SemaphoreType.DMA((2,)),
            pltpu.SemaphoreType.DMA((4,)),
        ],
        compiler_params=params(60),
        cost_estimate=cost(8 * length * model * ff, 3e7),
    )(
        *pieces,
        *quarters,
        grad_hidden,
        as_blocks(picked_wide, half),
        spread_hidden.reshape(2, 2, half, total),
    )


def down_part(hidden, grad, low, grad_low_down, grad_low, w_down, quarters, upstream, picked_wide, spread_down):
    rows, model = quarters[0].shape
    length, ff = hidden.shape

    def kernel(*refs):
        hidden_ref, grad_ref, low_ref, grad_low_down, grad_low_ref, down_hbm = refs[:6]
        quarter_refs, upstream_refs = refs[6:10], refs[10:14]
        wide_ref, down_spread = refs[14:16]
        away_ref, near_ref, narrow_ref, wide_out = refs[16:20]
        down_ref, x_ref, up_ref, sems = refs[20:]
        down_copy = pltpu.make_async_copy(down_hbm.at[:, pl.ds(0, ff)], down_ref, sems.at[2])
        down_copy.start()
        arriving = [
            copy_quarters(upstream_refs, up_ref, sems.at[0]),
            copy_quarters(quarter_refs, x_ref, sems.at[1]),
        ]
        low_down = dot_of(hidden_ref[...], down_spread[...], RIGHT_TURNED).astype(B16)
        low_half = low_down * jnp.asarray(ADAPTER_SCALING, B16)
        down_copy.wait()
        weights = jnp.concatenate([down_ref[...], wide_ref[...]], axis=1)
        for first, target in ((1, away_ref), (0, near_ref)):
            blocks = [slice(k * rows, (k + 1) * rows) for k in (first, first + 2)]
            values = jnp.concatenate(
                [
                    jnp.concatenate([hidden_ref[block, :], low_half[block]], axis=1)
                    for block in blocks
                ]
            )
            target[...] = dot_of(values, weights, RIGHT_TURNED).astype(target.dtype)
        for x in range(2):
            right = dot_of(low_ref[...], grad_ref[:, x * ff : (x + 1) * ff], LEFT_TURNED)
            narrow_ref[:, x * ff : (x + 1) * ff] = (
                ADAPTER_SCALING * right[(3 + x) * RANK : (4 + x) * RANK]
            ).astype(B16)
        left = dot_of(grad_low_down[...], hidden_ref[...], LEFT_TURNED)
        narrow_ref[:, 2 * ff : 3 * ff] = left[6 * RANK : 7 * RANK].astype(B16)
        wait_all(arriving[0])
        wait_all(arriving[1])
        wide_out[...] = dot_of(low_half, up_ref[...], LEFT_TURNED) + dot_of(
            grad_low_ref[...], x_ref[...], LEFT_TURNED
        )

    return pl.pallas_call(
        kernel,
        out_shape=[
            shape(B16, 2 * rows, model),
            shape(F32, 2 * rows, model),
            shape(B16, RANK, 3 * ff),
            shape(F32, LANES, model),
        ],
        in_specs=[VMEM] * 5 + [ANY] * 9 + [VMEM] * 2,
        out_specs=[VMEM] * 4,
        scratch_shapes=[
            pltpu.VMEM((model, ff), B16),
            pltpu.VMEM((length, model), B16),
            pltpu.VMEM((length, model), B16),
            pltpu.SemaphoreType.DMA((3,)),
        ],
        compiler_params=params(48),
        cost_estimate=cost(2.6 * length * model * ff, 3e7),
    )(hidden, grad, low, grad_low_down, grad_low, w_down, *quarters, *upstream, picked_wide, spread_down)


def attention_grads(
    own, lambda_all, weights, qkv, raw, lse, att, low_in, low_out, branch, quarters, picked_wide, spread_in, spread_out, wide_sum, heads
):
    rows, model = quarters[0].shape
    length, width = qkv.shape
    proj, half = width // 3, weights.shape[3]

    def kernel(own_ref, lambda_ref, *refs):
        weights_hbm, branch_refs, quarter_refs = refs[0], refs[1:5], refs[5:9]
        qkv_ref, raw_ref, lse_ref, att_ref, low_ref, low_out_ref = refs[9:15]
        wide_ref, in_ref, out_ref, wide_sum_ref = refs[15:19]
        grad_ref, grad_low_ref, narrow_ref, wide_grad_ref = refs[19:23]
        w_ref, branch_ref, x_ref, graw_ref, acc_ref, sems = refs[23:]
        weight_copy = pltpu.make_async_copy(
            weights_hbm.at[:, :, :, :, pl.ds(width, proj)],
            w_ref.at[pl.ds(0, 16), :, :, :, :],
            sems.at[0],
        )
        weight_copy.start()
        arriving = copy_quarters(branch_refs, branch_ref, sems.at[1])
        arriving_x = copy_quarters(quarter_refs, x_ref, sems.at[2])
        wait_all(arriving)
        grad_low_out = (
            ADAPTER_SCALING * product(branch_ref[:, :model], wide_ref[...])
        ).astype(B16)
        branch_ref[:, model:] = grad_low_out
        w_ref[16] = out_ref[...].reshape(2, 2, half, proj)
        weight_copy.wait()
        grad_in = product(branch_ref[...], w_ref[...].reshape(model + LANES, proj))
        left = dot_of(grad_low_out, att_ref[...], LEFT_TURNED)
        narrow_ref[:, width : width + proj] = left[5 * RANK : 6 * RANK].astype(B16)
        for r in range(4):
            start = pl.multiple_of((own_ref[0] ^ r) * rows, rows)
            for head in range(heads):
                columns = slice(head * 2 * HEAD_DIM, (head + 1) * 2 * HEAD_DIM)
                values = raw_ref[pl.ds(start, rows), columns]
                factor = lax.rsqrt(jnp.mean(values * values, axis=-1, keepdims=True) + NORM_EPS)
                grad = norm_backward(
                    values, factor, OUT_GAIN, grad_in[r * rows : (r + 1) * rows, columns]
                )
                graw_ref[pl.ds(start, rows), columns] = grad.astype(B16)
        for head in range(heads):
            column = head * 2 * HEAD_DIM
            value_columns = slice(2 * proj + column, 2 * proj + column + 2 * HEAD_DIM)
            key_columns = slice(proj + column, proj + column + 2 * HEAD_DIM)
            for block in reversed(range(length // BLOCK)):
                queries = slice(block * BLOCK, (block + 1) * BLOCK)
                keys = slice(0, (block + 1) * BLOCK)
                graw = graw_ref[queries, column : column + 2 * HEAD_DIM]
                probs = []
                for c in range(2):
                    scores = scores_of(qkv_ref, proj, column + c * HEAD_DIM, queries, keys)
                    probs.append(
                        jnp.exp(scores - lse_ref[head * 2 + c : head * 2 + c + 1, queries])
                    )
                lambda_one = lambda_ref[head]
                combined = (probs[0] - lambda_one * probs[1]).astype(B16)
                grad_values = product(combined, graw)
                grad_combined = dot_of(qkv_ref[keys, value_columns], graw, RIGHT_TURNED)
                grad_keys = []
                for c in range(2):
                    first = column + c * HEAD_DIM
                    weighted = probs[c] * grad_combined
                    inner = jnp.sum(weighted, axis=0, keepdims=True)
                    scale = HEAD_DIM**-0.5 if c == 0 else -lambda_one * HEAD_DIM**-0.5
                    grad_scores = ((weighted - probs[c] * inner) * scale).astype(B16)
                    grad_keys.append(
                        product(grad_scores, qkv_ref[queries, first : first + HEAD_DIM])
                    )
                    acc_ref[queries, first : first + HEAD_DIM] = dot_of(
                        grad_scores,
                        qkv_ref[keys, proj + first : proj + first + HEAD_DIM],
                        LEFT_TURNED,
                    )
                grad_key = jnp.concatenate(grad_keys, axis=1)
                if block == length // BLOCK - 1:
                    acc_ref[keys, key_columns] = grad_key
                    acc_ref[keys, value_columns] = grad_values
                else:
                    acc_ref[keys, key_columns] += grad_key
                    acc_ref[keys, value_columns] += grad_values
        for r in range(4):
            start = pl.multiple_of((own_ref[0] ^ r) * rows, rows)
            grad_ref[r * rows : (r + 1) * rows, :] = acc_ref[pl.ds(start, rows), :].astype(B16)
        grad_low_ref[...] = (
            ADAPTER_SCALING * dot_of(grad_ref[...], in_ref[...], RIGHT_TURNED)
        ).astype(B16)
        for x in range(3):
            columns = slice(x * proj, (x + 1) * proj)
            right = dot_of(low_ref[...], grad_ref[:, columns], LEFT_TURNED)
            narrow_ref[:, columns] = (
                ADAPTER_SCALING * right[x * RANK : (x + 1) * RANK]
            ).astype(B16)
        wait_all(arriving_x)
        low_half = low_out_ref[...] * jnp.asarray(ADAPTER_SCALING, B16)
        wide = (
            wide_sum_ref[...]
            + dot_of(low_half, branch_ref[:, :model], LEFT_TURNED)
            + dot_of(grad_low_ref[...], x_ref[...], LEFT_TURNED)
        )
        for start in range(0, model, LANES):
            wide_grad_ref[start : start + LANES, :] = wide[:, start : start + LANES].T.astype(B16)

    return pl.pallas_call(
        kernel,
        out_shape=[
            shape(B16, length, width),
            shape(B16, length, LANES),
            shape(B16, RANK, width + proj),
            shape(B16, model, LANES),
        ],
        in_specs=[SMEM, SMEM] + [ANY] * 9 + [VMEM] * 10,
        out_specs=[VMEM] * 4,
        scratch_shapes=[
            pltpu.VMEM((17, 2, 2, half, proj), B16),
            pltpu.VMEM((length, model + LANES), B16),
            pltpu.VMEM((length, model), B16),
            pltpu.VMEM((length, proj), B16),
            pltpu.VMEM((length, width), F32),
            pltpu.SemaphoreType.DMA((3,)),
        ],
        compiler_params=params(52),
        cost_estimate=cost(3 * length * model * proj, 2e7),
    )(
        own,
        lambda_all,
        weights,
        *branch,
        *quarters,
        qkv,
        raw,
        lse,
        att,
        low_in,
        low_out,
        picked_wide,
        spread_in,
        spread_out,
        wide_sum,
    )


def input_part(grad, grad_low, weights, picked_wide):
    length, width = grad.shape
    rows, half, model = length // 4, weights.shape[3], picked_wide.shape[0]

    def kernel(grad_ref, grad_low_ref, weights_hbm, wide_ref, away_ref, near_ref, w_ref, sem, factor_sems):
        copy = pltpu.make_async_copy(
            weights_hbm.at[:, :, :, :, pl.ds(0, width)],
            w_ref.at[:, :, :, :, pl.ds(0, width)],
            sem,
        )
        copy.start()
        wait_all(copy_factors(wide_ref, None, w_ref, factor_sems))
        copy.wait()
        weights = w_ref[...].reshape(model, width + LANES)
        for pick, target in ((away_rows, away_ref), (near_rows, near_ref)):
            values = jnp.concatenate(
                [pick(grad_ref, rows, ALL), pick(grad_low_ref, rows, ALL)], axis=1
            )
            target[...] = dot_of(values, weights, RIGHT_TURNED).astype(target.dtype)

    return pl.pallas_call(
        kernel,
        out_shape=[shape(B16, 2 * rows, model), shape(F32, 2 * rows, model)],
        in_specs=[VMEM, VMEM, ANY, ANY],
        out_specs=[VMEM, VMEM],
        scratch_shapes=[
            pltpu.VMEM((16, 2, 2, half, width + LANES), B16),
            pltpu.SemaphoreType.DMA,
            pltpu.SemaphoreType.DMA((1,)),
        ],
        compiler_params=params(40),
        cost_estimate=cost(2 * length * model * width, 2e7),
    )(grad, grad_low, weights, as_blocks(picked_wide, half))


def sum_sequences(quarter_place, keys, arrived, split_count):
    def kernel(place_ref, keys_ref, arrived_ref, spread_ref, wide_ref):
        values = arrived_ref[...]

        def summed(key, count):
            target = lax.broadcasted_iota(jnp.int32, (count, 1), 0)
            return product((target == key).astype(F32).astype(B16), values)

        split = summed(keys_ref[0:1, :], 256)
        wide = summed(keys_ref[1:2, :], 128)
        squares = jnp.sum(split * split) + jnp.sum(wide * wide)
        spread_ref[...] = jnp.zeros_like(spread_ref)
        is_last = lax.broadcasted_iota(jnp.int32, (8, LANES), 0) == 7
        for device in range(128):
            spread_ref[device] = jnp.where(is_last, squares, 0.0)
        for adapter in range(ADAPTERS):
            for t in range(4):
                block = split[(adapter * 4 + t) * 8 : (adapter * 4 + t + 1) * 8]
                spread_ref[adapter * 16 + place_ref[0] * 4 + t] = jnp.where(
                    is_last, squares, block
                )
            rows = wide[adapter * RANK : (adapter + 1) * RANK]
            for x in range(7):
                wide_ref[x, :, adapter * RANK : (adapter + 1) * RANK] = rows[
                    :, x * RANK : (x + 1) * RANK
                ]

    return pl.pallas_call(
        kernel,
        out_shape=[shape(F32, 128, 8, LANES), shape(F32, 7, RANK, LANES)],
        in_specs=[SMEM, VMEM, VMEM],
        out_specs=[VMEM, VMEM],
        compiler_params=params(24),
        cost_estimate=cost(1e9, 2e6),
    )(quarter_place, keys, arrived)


def update_adapters(quarter_place, placed, split_count, wide, attention, feedforward):
    count, attention_chunks = attention[0].shape[0], attention[0].shape[2] // LANES
    hidden_chunks = feedforward[0].shape[2] // LANES

    def kernel(place_ref, placed_ref, *refs):
        wide_refs, attention_refs, hidden_refs = refs[:4], refs[4:7], refs[7:10]
        norm_ref, outs = refs[10], refs[11:23]
        attention_grad, hidden_grads = refs[23:]
        total = placed_ref[0, 7:8, :]
        for device in range(1, 128):
            total += placed_ref[device, 7:8, :]
        norm = jnp.sqrt(total)
        norm_ref[...] = norm
        factor = CLIP_NORM / (norm + 1e-06)
        for r in range(4):
            for chunk in range(count * attention_chunks + feedforward[0].shape[0] * hidden_chunks):
                eighth, row = chunk // split_count, chunk % split_count
                device = (2 * r + eighth // 4) * 16 + place_ref[0] * 4 + eighth % 4
                values = placed_ref[device, row : row + 1, :]
                if chunk < count * attention_chunks:
                    x, column = chunk // attention_chunks, chunk % attention_chunks * LANES
                    attention_grad[x, r : r + 1, column : column + LANES] = values
                else:
                    rest = chunk - count * attention_chunks
                    x, column = rest // hidden_chunks, rest % hidden_chunks * LANES
                    hidden_grads[x, r : r + 1, column : column + LANES] = values
        groups = (
            (wide_refs[1], wide_refs[0], wide_refs[2], wide_refs[3]),
            (attention_refs[0], attention_grad, attention_refs[1], attention_refs[2]),
            (hidden_refs[0], hidden_grads, hidden_refs[1], hidden_refs[2]),
        )
        for i, group in enumerate(groups):
            for x in range(group[0].shape[0]):
                values = [v[x] for v in group]
                whole = jnp.concatenate([factor] * (values[0].shape[1] // LANES), axis=1)
                for out, result in zip(outs[4 * i : 4 * i + 4], adam_step(*values, whole)):
                    out[x] = result

    like = lambda v: [shape(F32, *v.shape)] * 4
    return pl.pallas_call(
        kernel,
        out_shape=[shape(F32, 1, LANES)] + like(wide[0]) + like(attention[0]) + like(feedforward[0]),
        in_specs=[SMEM] + [VMEM] * 11,
        out_specs=[VMEM] * 13,
        scratch_shapes=[
            pltpu.VMEM(attention[0].shape, F32),
            pltpu.VMEM(feedforward[0].shape, F32),
        ],
        compiler_params=params(24),
        cost_estimate=cost(1e7, 3e6),
    )(quarter_place, placed, *wide, *attention, *feedforward)


def adam_step(parameter, gradient, moment, variance, factor):
    clipped = gradient * factor
    moment_new = BETA_FIRST * moment + (1.0 - BETA_FIRST) * clipped
    variance_new = BETA_SECOND * variance + (1.0 - BETA_SECOND) * clipped * clipped
    moment_hat = moment_new / (1.0 - BETA_FIRST**STEP)
    variance_hat = variance_new / (1.0 - BETA_SECOND**STEP)
    updated = parameter - LEARN_RATE * (
        moment_hat / (jnp.sqrt(variance_hat) + ADAM_EPS) + WEIGHT_DECAY * parameter
    )
    return (clipped, updated, moment_new, variance_new)


def flat_rows(stacked):
    moved = stacked.astype(B16).transpose(1, 0, 2)
    return moved.reshape(stacked.shape[1], -1)


def local(
    tokens,
    cotangent,
    adapter_ids,
    norm_gains,
    lambda_vectors,
    weight_inputs,
    weight_output,
    hidden_weight_matrix,
    weight_down,
    adapter_wide,
    adapter_attention,
    adapter_feedforward,
    moment_wide,
    variance_wide,
    moment_attention,
    variance_attention,
    moment_feedforward,
    variance_feedforward,
):
    place = Place()
    adapter = adapter_ids[0]
    own_quarter = place.tensor.astype(jnp.int32).reshape(1)
    local_tokens = tokens[0].astype(F32)
    upstream_b = cotangent[0]
    gain_values = norm_gains.astype(F32)
    lambda_all = (
        jnp.exp(jnp.sum(lambda_vectors[0] * lambda_vectors[1], axis=-1))
        - jnp.exp(jnp.sum(lambda_vectors[2] * lambda_vectors[3], axis=-1))
        + LAMBDA_INIT
    )
    heads_local = lambda_vectors.shape[1]
    proj = weight_inputs.shape[2]
    ff = hidden_weight_matrix.shape[2]
    model = tokens.shape[2]

    shard_one = jnp.concatenate(
        [weight_inputs[0], weight_inputs[1], weight_inputs[2], weight_output.T], axis=1
    )
    shard_two = jnp.concatenate([hidden_weight_matrix[0], hidden_weight_matrix[1]], axis=1)
    wide_rows = adapter_wide.astype(B16).transpose(0, 2, 1).reshape(7 * RANK, LANES)
    attention_rows = flat_rows(adapter_attention).reshape(-1, LANES)
    attention_count, id_row = attention_rows.shape[0], 7 * RANK + attention_rows.shape[0]
    to_tiles = lambda v: jnp.pad(v, ((0, -v.shape[0] % 16), (0, 0)))
    first_rows = to_tiles(
        jnp.concatenate(
            [wide_rows, attention_rows, jnp.broadcast_to(adapter.astype(B16), (1, LANES))]
        )
    )
    hidden_rows = to_tiles(flat_rows(adapter_feedforward).reshape(-1, LANES))
    hidden_shape = hidden_rows.shape
    rest = jnp.concatenate(
        [weight_down.T, hidden_rows.reshape(weight_down.shape[1], -1)], axis=1
    )
    normed_one, scale_one = norm_forward(local_tokens, gain_values[0])
    normed_one_b = normed_one.astype(B16)

    own_pair = jnp.concatenate([normed_one_b, upstream_b], axis=0)
    (other_one, other_first, core_pair), (shard_one, shard_two, normed_out) = exchange(
        [(shard_one, PAIR_X), (first_rows, PAIR_X), (own_pair, CORES)],
        shard_one,
        shard_two,
        normed_one_b,
    )

    def pair_of(mine, theirs):
        swap = place.dp % 2 == 1
        return jnp.stack([jnp.where(swap, theirs, mine), jnp.where(swap, mine, theirs)])

    def gather_rest(pair):
        groups = [list(range(0, 32, 2)), list(range(1, 32, 2))]
        gathered = lax.all_gather(pair, "dp", axis=0, tiled=False, axis_index_groups=groups)
        return gathered.reshape((32,) + pair.shape[1:])

    first_adapters = gather_rest(pair_of(first_rows, other_first))
    blocks_one = first_blocks(shard_one, other_one, place)
    sends = ring_sends(*blocks_one)
    other_two = send(shard_two, PAIR_X)
    near, (normed_out, rest) = exchange(sends, normed_out, rest)
    (*far, other_rest), (normed_out, other_two) = exchange(
        relay_sends(sends, near) + [(rest, PAIR_X)], normed_out, other_two
    )
    gathered = gather_rest(pair_of(rest, other_rest)).reshape(model, -1)
    planes_one = planes(*blocks_one, near, far, 0, 4 * proj)
    sends = plane_sends(*planes_one)
    (*near_one, far_normed), (first_adapters, upstream_out) = exchange(
        sends + [(normed_out, FAR_X)], first_adapters, upstream_b
    )
    blocks_two = first_blocks(shard_two, other_two, place)

    onehot_rows = (
        jnp.arange(LANES)[None, :, None]
        == (adapter * RANK + jnp.arange(LANES) - RANK * jnp.arange(7)[:, None])[:, None, :]
    ) & (jnp.arange(LANES)[None, None, :] // RANK == jnp.arange(7)[:, None, None])
    wide_mine = (
        first_adapters[:, : 7 * RANK]
        .reshape(32, 7, RANK, LANES)
        .transpose(0, 2, 1, 3)
        .reshape(512, 7 * LANES)
    )
    picked_t = product(wide_mine, onehot_rows.astype(B16).reshape(7 * LANES, LANES)).astype(B16)
    (*far_one, picked_far), (far_normed, upstream_out, *blocks_two) = exchange(
        relay_sends(sends, near_one) + [(picked_t, FAR_X)], far_normed, upstream_out, *blocks_two
    )
    picked_all = in_place(
        [picked_t, send(picked_t, CORES), picked_far, send(picked_far, CORES)], place
    ).reshape(4, 32, 16, LANES)
    picked_wide = picked_all.transpose(1, 0, 2, 3).reshape(model, LANES)
    def picked_rows(gathered, first, count, width):
        mine = lax.dynamic_slice_in_dim(gathered, adapter * 4, 4, 0)
        return mine[:, first : first + count].reshape(RANK, width)

    def spread_rows(rows, slots, width):
        slot = jnp.concatenate([jnp.full((width,), x, jnp.int32) for x in slots])
        return jnp.where(
            slot[None, :] == jnp.arange(LANES)[:, None] // RANK,
            jnp.concatenate([rows] * 8, axis=0),
            0,
        ).astype(B16)

    spread = spread_rows(
        picked_rows(first_adapters, 7 * RANK, attention_count, 4 * proj), (0, 1, 2, 5), proj
    )
    spread_in, spread_out = spread[:, : 3 * proj], spread[:, 3 * proj :]
    ids_all = first_adapters[:, id_row, 0].astype(jnp.int32)

    token_rows = normed_one_b.shape[0]
    seq_normed_one = [
        normed_one_b,
        core_pair[:token_rows],
        far_normed,
        send(far_normed, CORES),
    ]
    w_attention, qkv, low_in = projection_part(
        own_quarter,
        pieces_of(planes_one, near_one, far_one),
        seq_normed_one,
        picked_wide,
        spread_in,
    )
    attention_b, raw, lse, low_out, away, near_sum = attention_part(
        own_quarter, lambda_all, w_attention, qkv, picked_wide, spread_out, heads_local
    )
    sends = ring_sends(*blocks_two)
    far_upstream = send(upstream_out, FAR_X)
    near, (away, near_sum) = exchange(sends, away, near_sum)
    far, (away, near_sum, far_upstream) = exchange(
        relay_sends(sends, near), away, near_sum, far_upstream
    )
    seq_upstream = [
        upstream_b,
        core_pair[token_rows:],
        far_upstream,
        send(far_upstream, CORES),
    ]
    staying, leaving = core_sum(near_sum, away)
    planes_two = planes(*blocks_two, near, far, 0, 2 * ff)
    sends = plane_sends(*planes_two)
    (*near_two, arrived), (residual_part, gathered, *seq_upstream) = exchange(
        sends + [(leaving, FAR_X)], local_tokens + staying, gathered, *seq_upstream
    )
    hidden_picked = lax.dynamic_slice_in_dim(gathered, adapter * 256, 256, 0)[:, ff:]
    hidden_picked = hidden_picked.reshape((4,) + hidden_shape)[:, : 3 * ff * 4 // LANES]
    spread = spread_rows(hidden_picked.reshape(RANK, 3 * ff), (3, 4, 6), ff)
    spread_hidden, spread_down = spread[:, : 2 * ff], spread[:, 2 * ff :]
    w_down = gathered
    grad_low_down, grad_hidden = hidden_grad(w_down, seq_upstream, picked_wide, spread_down)
    residual_one = residual_part + arrived.astype(F32)
    second_normalized, scale_two = norm_forward(residual_one, gain_values[1])
    normed_two_b = second_normalized.astype(B16)
    normed_two_b, *near_two = together(normed_two_b, *near_two)
    (*far_two, far_tokens), (grad_low_down, grad_hidden) = exchange(
        relay_sends(sends, near_two) + [(normed_two_b, FAR_X)], grad_low_down, grad_hidden
    )
    seq_normed_two = [
        normed_two_b,
        send(normed_two_b, CORES),
        far_tokens,
        send(far_tokens, CORES),
    ]

    hidden_b, grad_gate_up, low_hidden, grad_low_hidden, away, near_sum = hidden_part(
        pieces_of(planes_two, near_two, far_two),
        grad_hidden,
        seq_normed_two,
        picked_wide,
        spread_hidden,
    )
    grad_staying, leaving = core_sum(near_sum, away)
    leaving, hidden_b, grad_gate_up = together(leaving, hidden_b, grad_gate_up)
    away_down, near_down, narrow_two, wide_two = down_part(
        hidden_b,
        grad_gate_up,
        low_hidden,
        grad_low_down,
        grad_low_hidden,
        w_down,
        seq_normed_two,
        seq_upstream,
        picked_wide,
        spread_down,
    )
    arrived, grad_staying, near_down, away_down = together(
        send(leaving, FAR_X), grad_staying, near_down, away_down
    )
    grad_normed_two = grad_staying + arrived.astype(F32)
    grad_residual = upstream_b.astype(F32) + norm_backward(
        residual_one, scale_two, gain_values[1], grad_normed_two
    )
    grad_branch_b = grad_residual.astype(B16)
    down_staying, down_leaving = core_sum(near_down, away_down)
    far_branch, down_leaving = together(send(grad_branch_b, FAR_X), down_leaving)
    seq_grad_branch = [
        grad_branch_b,
        send(grad_branch_b, CORES),
        far_branch,
        send(far_branch, CORES),
    ]

    grad_projected, grad_low_in, narrow_one, wide_grads = attention_grads(
        own_quarter,
        lambda_all,
        w_attention,
        qkv,
        raw,
        lse,
        attention_b,
        low_in,
        low_out,
        seq_grad_branch,
        seq_normed_one,
        picked_wide,
        spread_in,
        spread_out,
        wide_two,
        heads_local,
    )
    down_arrived, narrow_one, wide_grads = together(
        send(down_leaving, FAR_X), narrow_one, wide_grads
    )
    result = residual_one + down_staying + down_arrived.astype(F32)
    away, near_sum = input_part(grad_projected, grad_low_in, w_attention, picked_wide)

    split_grads = jnp.concatenate([narrow_one, narrow_two], axis=1)
    columns = split_grads.shape[1]
    row_count = RANK + 8
    piece = -(-columns // 1024) * 128
    split_count = piece // LANES
    split_blocks = (
        jnp.pad(split_grads, ((0, 0), (0, 8 * piece - columns)))
        .reshape(4, 4, 2, 4, piece)
        .transpose(1, 2, 0, 3, 4)
        .reshape(128, split_count, LANES)
    )
    blocks = jnp.concatenate(
        [
            wide_grads.reshape(128, RANK, LANES),
            split_blocks,
            jnp.zeros((128, 8 - split_count, LANES), B16),
        ],
        axis=1,
    )
    source = jnp.arange(128 * row_count, dtype=jnp.int32)
    source_row, source_t = source % row_count, source // row_count % 4
    source_id = jnp.repeat(ids_all, 4 * row_count)
    split_row = source_row - RANK
    split_key = jnp.where(
        (split_row >= 0) & (split_row < split_count), source_id * 32 + source_t * 8 + split_row, -1
    )
    wide_key = jnp.where(source_row < RANK, source_id * RANK + source_row, -1)
    keys = jnp.stack([split_key, wide_key])
    quarter_place = (place.dp % 4).astype(jnp.int32).reshape(1)
    arrived, away, near_sum, keys = together(
        lax.all_to_all(blocks, AXES, split_axis=0, concat_axis=0, tiled=True),
        away,
        near_sum,
        keys,
    )
    from_core = send(away, CORES)
    spread, grads_wide = sum_sequences(
        quarter_place, keys, arrived.reshape(128 * row_count, LANES), split_count
    )
    rows = near_sum.shape[0] // 2
    leaving = (near_sum[rows:] + from_core[rows:].astype(F32)).astype(B16)
    staying = near_sum[:rows] + from_core[:rows].astype(F32)
    grad_normed_one = staying + send(leaving, FAR_X).astype(F32)
    grad_input = grad_residual + norm_backward(
        local_tokens, scale_one, gain_values[0], grad_normed_one
    )
    placed, grad_input = together(
        lax.all_to_all(spread, AXES, split_axis=0, concat_axis=0, tiled=True),
        grad_input.astype(B16),
    )
    turned = lambda v: v.transpose(0, 2, 1)
    grad_norm, *updates = update_adapters(
        quarter_place,
        placed,
        split_count,
        (grads_wide, turned(adapter_wide), turned(moment_wide), turned(variance_wide)),
        (adapter_attention, moment_attention, variance_attention),
        (adapter_feedforward, moment_feedforward, variance_feedforward),
    )
    wide_new = [turned(v) for v in updates[:4]]
    attention_new, feedforward_new = updates[4:8], updates[8:]
    return (
        result.astype(B16)[None],
        grad_input.astype(B16)[None],
        grad_norm[0, 0],
        wide_new[0],
        attention_new[0],
        feedforward_new[0],
        wide_new[1],
        attention_new[1],
        feedforward_new[1],
        wide_new[2],
        attention_new[2],
        feedforward_new[2],
        wide_new[3],
        attention_new[3],
        feedforward_new[3],
    )


def solution(mesh):
    return jax.shard_map(
        local,
        mesh=mesh,
        in_specs=(
            P("dp", "tensor", None),
            P("dp", "tensor", None),
            P("dp"),
            P(),
            P(None, "tensor", None),
            P(None, "dp", "tensor"),
            P("tensor", "dp"),
            P(None, "dp", "tensor"),
            P("tensor", "dp"),
            P(None, None, ("dp", "tensor")),
            P(None, "dp", "tensor"),
            P(None, "dp", "tensor"),
            P(None, None, ("dp", "tensor")),
            P(None, None, ("dp", "tensor")),
            P(None, "dp", "tensor"),
            P(None, "dp", "tensor"),
            P(None, "dp", "tensor"),
            P(None, "dp", "tensor"),
        ),
        out_specs=(
            P("dp", "tensor", None),
            P("dp", "tensor", None),
            P(),
            P(None, None, ("dp", "tensor")),
            P(None, "dp", "tensor"),
            P(None, "dp", "tensor"),
            P(None, None, ("dp", "tensor")),
            P(None, "dp", "tensor"),
            P(None, "dp", "tensor"),
            P(None, None, ("dp", "tensor")),
            P(None, "dp", "tensor"),
            P(None, "dp", "tensor"),
            P(None, None, ("dp", "tensor")),
            P(None, "dp", "tensor"),
            P(None, "dp", "tensor"),
        ),
        check_vma=False,
    )
```
